32 devices in a mesh: dp: 8 (over z, y), mp: 4 (over x, core).
Axes of the slice: x: 2, y: 2, z: 4, core: 2. Of those that a mesh axis runs over, the one named last changes fastest.
Arguments:
- media: bfloat16 [16, 1280, 1024], P('dp'), may hold values from -6 to 6
- latents: bfloat16 [16, 64, 1024], P('dp'), may hold values from -6 to 6
- cotangent: bfloat16 [16, 64, 1024], P('dp'), may hold values from -6 to 6
- image_counts: int32 [16], P('dp'), may hold values from 1 to 5
- query_matrix: bfloat16 [1024, 512], P('dp', 'mp'), may hold values from -0.1875 to 0.1875
- k_weight: bfloat16 [1024, 512], P('dp', 'mp'), may hold values from -0.1875 to 0.1875
- v_weight: bfloat16 [1024, 512], P('dp', 'mp'), may hold values from -0.1875 to 0.1875
- output_projection_weight: bfloat16 [512, 1024], P('mp', 'dp'), may hold values from -6 to 6
- up_projection_weight: bfloat16 [1024, 4096], P('dp', 'mp'), may hold values from -0.1875 to 0.1875
- down_projection_weight: bfloat16 [4096, 1024], P('mp', 'dp'), may hold values from -0.09375 to 0.09375
- media_gain: bfloat16 [1024], P('dp'), may hold values from 0.5 to 1.5
- media_bias: bfloat16 [1024], P('dp'), may hold values from -3 to 3
- latent_gain: bfloat16 [1024], P('dp'), may hold values from 0.5 to 1.5
- latent_bias: bfloat16 [1024], P('dp'), may hold values from -3 to 3
- ff_gain: bfloat16 [1024], P('dp'), may hold values from 0.5 to 1.5
- ff_bias: bfloat16 [1024], P('dp'), may hold values from -3 to 3
Outputs:
- latents_out: bfloat16 [16, 64, 1024], P('dp')
- media_grad: bfloat16 [16, 1280, 1024], P('dp')
- latent_grad: bfloat16 [16, 64, 1024], P('dp')
- query_weight_grad: float32 [1024, 512], P('dp', 'mp')
- k_grad: float32 [1024, 512], P('dp', 'mp')
- v_grad: float32 [1024, 512], P('dp', 'mp')
- output_projection_grad: float32 [512, 1024], P('mp', 'dp')
- up_projection_grad: float32 [1024, 4096], P('dp', 'mp')
- down_projection_grad: float32 [4096, 1024], P('mp', 'dp')
- media_gain_grad: float32 [1024], P('dp')
- media_bias_grad: float32 [1024], P('dp')
- latent_gain_grad: float32 [1024], P('dp')
- latent_bias_grad: float32 [1024], P('dp')
- ff_gain_grad: float32 [1024], P('dp')
- ff_bias_grad: float32 [1024], P('dp')
The draws below stay inside these ranges and needn't reach their ends.
Inputs may be any that keep to these rules, and one draw needn't show every extreme that they name: image_counts[b] is the number of images of sample b; they fill its first image slots.
All inputs are finite; a program needn't handle non-finite values.
Results may differ from the reference program's by a relative error of at most 0.017.
Values may be sent and summed in bfloat16 or wider, within the bound.
A program may use at most 128 MiB of HBM per device.

```python
import jax
import jax.numpy as jnp
from jax import lax

D = 1024
HEADS = 8
HEAD = 64
FF = 4096
LAT = 64
PATCH = 256
SLOTS = 5
SAMPLES = 16


def touch_ends(drawn, stream_key, smallest, top_value):
    shape = drawn.shape
    place = [jax.random.randint(jax.random.fold_in(stream_key, axis), (), 0, shape[axis]) for axis in range(len(shape))]
    drawn = drawn.at[tuple(place)].set(smallest)
    longest = shape.index(max(shape))
    place[longest] = (place[longest] + 1) % shape[longest]
    return drawn.at[tuple(place)].set(top_value)


def block_scale(rng, shape, shards, low, top_value):
    level, own = 1.0, jax.random.fold_in(rng, 6)
    for axis_at, parts in shards:
        heights = jnp.exp(jax.random.uniform(jax.random.fold_in(own, axis_at), (parts,), jnp.float32, low / len(shards), top_value / len(shards)))
        level = level * jnp.repeat(heights, shape[axis_at] // parts).reshape([-1 if axis == axis_at else 1 for axis in range(len(shape))])
    return level


def gaussian(rng, extent, width, reach, shards=(), dtype=jnp.bfloat16):
    values = jax.random.normal(rng, extent, jnp.float32) * width
    if len(shards) > 0:
        values = block_scale(rng, extent, shards, -0.22, 0.18) * values
    return jnp.clip(values, min=-reach, max=reach).astype(dtype)


def setup_inputs(seed: int = 0) -> dict:
    arg_keys = jax.random.split(jax.random.key(seed), 17)
    return {
        "media": gaussian(arg_keys[0], (SAMPLES, SLOTS * PATCH, D), 1.0, 6.0, ((0, 8),)),
        "latents": gaussian(arg_keys[1], (SAMPLES, LAT, D), 1.0, 6.0, ((0, 8),)),
        "cotangent": gaussian(arg_keys[2], (SAMPLES, LAT, D), 1.0, 6.0, ((0, 8),)),
        "image_counts": touch_ends(jax.random.randint(arg_keys[3], (SAMPLES,), 1, SLOTS + 1), jax.random.fold_in(arg_keys[3], 1), 1, SLOTS).astype(jnp.int32),
        "query_matrix": gaussian(arg_keys[4], (D, HEADS * HEAD), D ** -0.5, 0.1875, ((0, 8), (1, 4))),
        "k_weight": gaussian(arg_keys[5], (D, HEADS * HEAD), D ** -0.5, 0.1875, ((0, 8), (1, 4))),
        "v_weight": gaussian(arg_keys[6], (D, HEADS * HEAD), D ** -0.5, 0.1875, ((0, 8), (1, 4))),
        "output_projection_weight": gaussian(arg_keys[7], (HEADS * HEAD, D), (max(1, HEADS * HEAD * PATCH // 131072)) ** -0.5, 6.0, ((0, 4), (1, 8))),
        "up_projection_weight": gaussian(arg_keys[8], (D, FF), D ** -0.5, 0.1875, ((0, 8), (1, 4))),
        "down_projection_weight": gaussian(arg_keys[9], (FF, D), FF ** -0.5, 0.09375, ((0, 4), (1, 8))),
        "media_gain": jnp.clip(1.0 + 0.1 * jax.random.normal(arg_keys[10], (D,), jnp.float32), 0.5, 1.5).astype(jnp.bfloat16),
        "media_bias": gaussian(arg_keys[11], (D,), 0.5, 3.0, ((0, 8),)),
        "latent_gain": jnp.clip(1.0 + 0.1 * jax.random.normal(arg_keys[12], (D,), jnp.float32), 0.5, 1.5).astype(jnp.bfloat16),
        "latent_bias": gaussian(arg_keys[13], (D,), 0.5, 3.0, ((0, 8),)),
        "ff_gain": jnp.clip(1.0 + 0.1 * jax.random.normal(arg_keys[14], (D,), jnp.float32), 0.5, 1.5).astype(jnp.bfloat16),
        "ff_bias": gaussian(arg_keys[15], (D,), 0.5, 3.0, ((0, 8),)),
    }


@jax.custom_vjp
def low(v):
    return lax.optimization_barrier(v.astype(jnp.bfloat16)).astype(jnp.float32)

@jax.custom_vjp
def low_back(v):
    return v

def low_keep(v):
    return (low(v), None)

def low_pass(kept, grad):
    return (grad,)

def back_keep(v):
    return (v, None)

def back_low(kept, grad):
    return (low(grad),)
low.defvjp(low_keep, low_pass)
low_back.defvjp(back_keep, back_low)
highest = lax.Precision.HIGHEST

def layer_norm(inputs, gain, bias):
    center = inputs - lax.optimization_barrier(jnp.mean(inputs, axis=-1, keepdims=True))
    spread = lax.optimization_barrier(jnp.mean(center * center, axis=-1, keepdims=True))
    return center * lax.rsqrt(spread + 1e-05) * gain + bias

def forward(params, media, latents, count):
    query_matrix, k_weight, v_weight, output_projection_weight, up_projection_weight, down_projection_weight, media_gain, media_bias, latent_gain, latent_bias, ff_gain, ff_bias = params
    media_norm = low(layer_norm(media, media_gain, media_bias))
    latent_normed_rows = low(layer_norm(latents, latent_gain, latent_bias))
    key_input = jnp.concatenate([media_norm, latent_normed_rows], axis=0)
    query_rows = low(low_back(jnp.dot(latent_normed_rows, query_matrix, precision=highest))).reshape(LAT, HEADS, HEAD)
    keys = low(low_back(jnp.dot(key_input, k_weight, precision=highest))).reshape(SLOTS * PATCH + LAT, HEADS, HEAD)
    values = low(low_back(jnp.dot(key_input, v_weight, precision=highest))).reshape(SLOTS * PATCH + LAT, HEADS, HEAD)
    places = jnp.arange(SLOTS * PATCH + LAT)
    valid = jnp.logical_or(places // PATCH < count, places >= SLOTS * PATCH)
    scores = jnp.einsum('ihe,jhe->hij', query_rows, keys, precision=highest) * 0.125
    scores = low_back(jnp.where(valid[None, None, :], scores, -1e+30))
    row_max = lax.optimization_barrier(jnp.max(scores, axis=-1, keepdims=True))
    raised = jnp.exp(scores - row_max)
    attend = raised / lax.optimization_barrier(jnp.sum(raised, axis=-1, keepdims=True))
    mixed_rows = jnp.einsum('hij,jhe->ihe', low(attend), values, precision=highest).reshape(LAT, HEADS * HEAD)
    mixed_rows = low(low_back(mixed_rows))
    middle = latents + low_back(jnp.dot(mixed_rows, output_projection_weight, precision=highest))
    hidden_rows = low(layer_norm(middle, ff_gain, ff_bias))
    inner_rows = low_back(jnp.dot(hidden_rows, up_projection_weight, precision=highest))
    active_units = low(jax.nn.gelu(inner_rows, approximate=False))
    return middle + jnp.dot(active_units, down_projection_weight, precision=highest)

def reference(media, latents, cotangent, image_counts, query_matrix, k_weight, v_weight, output_projection_weight, up_projection_weight, down_projection_weight, media_gain, media_bias, latent_gain, latent_bias, ff_gain, ff_bias):
    params = tuple((member.astype(jnp.float32) for member in (query_matrix, k_weight, v_weight, output_projection_weight, up_projection_weight, down_projection_weight, media_gain, media_bias, latent_gain, latent_bias, ff_gain, ff_bias)))

    def one_sample(totals, sample):
        media_one, latent_one, tangent_one, count_one = sample

        def single(weights, media_in, latent_in):
            return forward(weights, media_in, latent_in, count_one)
        result, pullback = jax.vjp(single, params, media_one.astype(jnp.float32), latent_one.astype(jnp.float32))
        weight_grads, media_back, latent_back = pullback(tangent_one.astype(jnp.float32))
        totals = tuple((first + second for first, second in zip(totals, weight_grads)))
        return (totals, (result.astype(jnp.bfloat16), media_back.astype(jnp.bfloat16), latent_back.astype(jnp.bfloat16)))
    initial = tuple((jnp.zeros_like(member) for member in params))
    totals, outputs = lax.scan(one_sample, initial, (media, latents, cotangent, image_counts))
    return (outputs[0], outputs[1], outputs[2], totals[0], totals[1], totals[2], totals[3], totals[4], totals[5], totals[6], totals[7], totals[8], totals[9], totals[10], totals[11])
```

```python
import functools

import jax
import jax.numpy as jnp
from jax import lax
from jax.experimental import pallas as pl
from jax.experimental.pallas import tpu as pltpu
from jax.sharding import PartitionSpec as P

HEAD = 64
PATCH = 256
EPS = 1e-05
F32 = jnp.float32
BF16 = jnp.bfloat16
MESH = pl.DeviceIdType.MESH
NN = (((1,), (0,)), ((), ()))
NT = (((1,), (1,)), ((), ()))
TN = (((0,), (0,)), ((), ()))
SEMS = 160


def dot(a, b, dims):
    return lax.dot_general(a, b, dims, preferred_element_type=F32)


def at(start, size):
    return pl.ds(pl.multiple_of(start, size), size)


class Wire:
    def __init__(self, send_sem, recv_sem):
        self.send_sem, self.recv_sem = send_sem, recv_sem
        self.used, self.sent = 0, []

    def take(self, count=1):
        first = self.used
        self.used += count
        assert self.used <= SEMS
        return first

    def make(self, slot, src, dst, dev):
        return pltpu.make_async_remote_copy(
            src_ref=src,
            dst_ref=dst,
            send_sem=self.send_sem.at[slot],
            recv_sem=self.recv_sem.at[slot],
            device_id=dev,
            device_id_type=MESH,
        )

    def send(self, src, dst, dev):
        copy = self.make(self.take(), src, dst, dev)
        copy.start()
        self.sent.append(copy)
        return copy

    def drain(self):
        for copy in self.sent:
            copy.wait_send()


def norm_back(z, mean, rstd, gain, dy):
    zhat = (z - mean) * rstd
    t = dy * gain
    mt = jnp.mean(t, axis=-1, keepdims=True)
    mz = jnp.mean(t * zhat, axis=-1, keepdims=True)
    return rstd * (t - mt - zhat * mz), zhat


def layer_kernel(
    counts,
    media,
    latents,
    cot,
    wq,
    wk,
    wv,
    wo,
    up,
    down,
    mg,
    mb,
    lg,
    lb,
    fg,
    fb,
    lat_out,
    media_out,
    lgrad_out,
    gq,
    gk,
    gv,
    go,
    gup,
    gdown,
    vec0,
    vec1,
    vec2,
    vec3,
    vec4,
    vec5,
    send_sem,
    recv_sem,
    local_sem,
    prm_own,
    prm,
    vec,
    xin,
    lat,
    kin,
    mu,
    rs,
    w3,
    wob,
    upb,
    dnb,
    kb,
    vb,
    qb,
    att,
    attl,
    mix,
    mid,
    hid,
    cota,
    act,
    ig,
    hgs,
    hgr,
    hgx,
    fos,
    fors,
    fox,
    gus,
    gur,
    guo,
    gu,
    gua,
    gds,
    gdr,
    gdo,
    gd,
    gda,
    midg,
    lowb,
    mgr,
    kvg,
    qg,
    cgs,
    cgr,
    gown,
    g1,
    yr,
    g2,
    zr,
    dxs,
    accg,
    accb,
    mgo,
    outl,
    outg,
    vgs,
    vgc,
    vgt,
    vga,
):
    i = lax.axis_index("dp")
    j = lax.axis_index("mp")
    x, c = j // 2, j % 2
    yy, z = i % 2, i // 2
    zlo, zhi = z % 2, z // 2
    r = i % 4

    def peer(k):
        a = 1 - yy if k & 1 else yy
        b = 1 - zlo if k & 2 else zlo
        d = 1 - zhi if k & 4 else zhi
        return d * 4 + b * 2 + a

    jx = j + 2 - 4 * x
    jc = j + 1 - 2 * c
    ox = 1 - x
    oc = 1 - c
    xpart = (i, jx)
    cpart = (i, jc)
    ypart = (peer(1), j)
    wire = Wire(send_sem, recv_sem)

    def w3b(ii, xx, cc):
        return w3.at[xx, ii, :, at(cc * 384, 128 * 3)]

    local = []

    def bring(src, dst):
        copy = pltpu.make_async_copy(src, dst, local_sem.at[len(local)])
        copy.start()
        local.append(copy)
        return copy

    bring(wk, w3.at[x, i, :, at(c * 384, 128)])
    bring(wv, w3.at[x, i, :, at(c * 384 + 128, 128)])
    bring(wq, w3.at[x, i, :, at(c * 384 + 256, 128)])
    bring(wo, wob.at[j, :, at(i * 128, 128)])
    in_lat = bring(latents.at[c], lat)
    in_media = bring(media.at[c], xin)
    in_cot = bring(cot.at[c], cota.at[r])
    in_up = bring(up.at[:, at(r * 256, 256)], upb.at[i, :, at(c * 256, 256)])
    in_dn = bring(down.at[at(r * 256, 256), :], dnb.at[c, :, at(i * 128, 128)])
    for row, ref in enumerate((mg, mb, lg, lb, fg, fb)):
        prm_own[row : row + 1, :] = ref[...].astype(F32)
    prm_own[6:8, :] = jnp.zeros((2, 128), F32)
    prm[i] = prm_own[...]

    barrier = pltpu.get_barrier_semaphore()
    partners = [(peer(k), j) for k in range(1, 8)] + [xpart, cpart]
    partners += [(peer(k), jx) for k in range(1, 4)]
    for dev in partners:
        pl.semaphore_signal(barrier, inc=1, device_id=dev, device_id_type=MESH)
    pl.semaphore_wait(barrier, len(partners))

    got_prm = [wire.send(prm_own, prm.at[i], (peer(k), j)) for k in range(1, 8)]
    for copy in local[:4]:
        copy.wait()

    def wo_at(ii, jj):
        return wob.at[jj, :, at(ii * 128, 128)]

    def same(view, dev):
        return wire.send(view, view, dev)

    z3 = [same(w3b(i, x, c), (peer(2 * k), j)) for k in (1, 2, 3)]
    y3 = [same(w3b(i, x, c), ypart)]
    x3 = [same(w3b(i, x, c), xpart)]
    zo = [same(wo_at(i, j), (peer(2 * k), j)) for k in (1, 2, 3)]
    yo = [same(wo_at(i, j), ypart)]
    xo = [same(wo_at(i, j), xpart)]

    for copy in got_prm:
        copy.wait_recv()
    for ii in range(8):
        vec[:, ii * 128 : (ii + 1) * 128] = prm[ii]

    in_lat.wait()
    lat32 = lat[...].astype(F32)
    lmean = jnp.mean(lat32, axis=-1, keepdims=True)
    lcen = lat32 - lmean
    lrs = lax.rsqrt(jnp.mean(lcen * lcen, axis=-1, keepdims=True) + EPS)
    kin[1280:1344, :] = (lcen * lrs * vec[2:3, :] + vec[3:4, :]).astype(BF16)
    mu[1280:1344, :] = lmean
    rs[1280:1344, :] = lrs
    in_media.wait()

    def media_norm(lo, hi):
        def strip(t, carry):
            rows = at(t * 16, 16)
            v = xin[rows, :].astype(F32)
            m = jnp.mean(v, axis=-1, keepdims=True)
            cen = v - m
            rr = lax.rsqrt(jnp.mean(cen * cen, axis=-1, keepdims=True) + EPS)
            kin[rows, :] = (cen * rr * vec[0:1, :] + vec[1:2, :]).astype(BF16)
            mu[rows, :] = m
            rs[rows, :] = rr
            return carry

        lax.fori_loop(lo, hi, strip, 0)

    media_norm(0, 40)
    for k in (1, 2, 3):
        z3[k - 1].wait_recv()
        y3.append(same(w3b(peer(2 * k), x, c), ypart))
        x3.append(same(w3b(peer(2 * k), x, c), xpart))
    in_cot.wait()
    cots = [wire.send(cota.at[r], cota.at[r], (peer(k), j)) for k in (1, 2, 3)]
    ups, dns = [], []
    for k in range(1, 8):
        rk = peer(k) % 4
        ups.append(
            wire.send(
                up.at[:, at(rk * 256, 256)], upb.at[i, :, at(c * 256, 256)], (peer(k), j)
            )
        )
    for k in range(1, 8):
        rk = peer(k) % 4
        dns.append(
            wire.send(
                down.at[at(rk * 256, 256), :], dnb.at[c, :, at(i * 128, 128)], (peer(k), j)
            )
        )
    media_norm(40, 60)
    for k in (0, 1, 2, 3):
        y3[k].wait_recv()
        x3.append(same(w3b(peer(2 * k + 1), x, c), xpart))
    own3 = w3.at[x, :, :, at(c * 384, 128 * 3)]
    c3 = same(own3, cpart)
    for k in (1, 2, 3):
        zo[k - 1].wait_recv()
        yo.append(same(wo_at(peer(2 * k), j), ypart))
        xo.append(same(wo_at(peer(2 * k), j), xpart))
    media_norm(60, 80)
    for k in (0, 1, 2, 3):
        yo[k].wait_recv()
        xo.append(same(wo_at(peer(2 * k + 1), j), xpart))
    co = same(wob.at[j], cpart)
    c3.wait_recv()

    count = counts[c]
    head_of_lane = lax.broadcasted_iota(jnp.int32, (256, 256), 1) // HEAD
    head_of_row = lax.broadcasted_iota(jnp.int32, (256, 256), 0) // HEAD
    own_head = head_of_lane == head_of_row
    lane64 = lax.broadcasted_iota(jnp.int32, (64, 256), 1) // HEAD

    def spread(v):
        v = v.astype(F32)
        return jnp.where(own_head, jnp.concatenate([v, v, v, v], axis=0), 0.0).astype(BF16)

    def gather_heads(v):
        out = jnp.zeros((64, 256), F32)
        for h in range(4):
            out = jnp.where(lane64 == h, v[h * 64 : (h + 1) * 64, :], out)
        return out

    def w_kv(g, cc):
        return w3[g, :, :, cc * 384 : cc * 384 + 256].reshape(1024, 256)

    def w_q(g, cc):
        return w3[g, :, :, cc * 384 + 256 : cc * 384 + 384].reshape(1024, 128)

    def attention(g):
        def project(t, carry):
            rows = at(t * 448, 448)
            a = kin[rows, :]
            for cc in (0, 1):
                o = dot(a, w_kv(g, cc), NN)
                kb[g, rows, cc * 128 : (cc + 1) * 128] = o[:, :128].astype(BF16)
                vb[g, rows, cc * 128 : (cc + 1) * 128] = o[:, 128:].astype(BF16)
            return carry

        lax.fori_loop(0, 3, project, 0)
        for cc in (0, 1):
            qb[g, :, cc * 128 : (cc + 1) * 128] = dot(
                kin[1280:1344, :], w_q(g, cc), NN
            ).astype(BF16)
        q4 = spread(qb[g])

        def score(t, top):
            rows = at(t * 192, 192)
            s = dot(kb[g, rows, :], q4, NT) * 0.125
            key = lax.broadcasted_iota(jnp.int32, (192, 256), 0) + t * 192
            ok = jnp.logical_or(key < count * PATCH, key >= 1280)
            s = jnp.where(ok, s, -1e30)
            att[g, rows, :] = s
            return jnp.maximum(top, jnp.max(s, axis=0, keepdims=True))

        top = lax.fori_loop(0, 7, score, jnp.full((1, 256), -1e30, F32))

        def raise_(t, total):
            rows = at(t * 64, 64)
            e = jnp.exp(att[g, rows, :] - top)
            att[g, rows, :] = e
            return total + jnp.sum(e, axis=0, keepdims=True)

        total = lax.fori_loop(0, 21, raise_, jnp.zeros((1, 256), F32))
        scale = 1.0 / total

        def level(t, carry):
            rows = at(t * 64, 64)
            p = att[g, rows, :] * scale
            att[g, rows, :] = p
            attl[g, rows, :] = p.astype(BF16)
            return carry

        lax.fori_loop(0, 21, level, 0)
        mixed = dot(attl[g], vb[g], TN)
        mix[:, at(g * 256, 256)] = gather_heads(mixed).astype(BF16)

    attention(x)
    for copy in x3:
        copy.wait_recv()
    oth3 = w3.at[ox, :, :, at(c * 384, 128 * 3)]
    c3b = same(oth3, cpart)
    for copy in xo:
        copy.wait_recv()
    cob = same(wob.at[jx], cpart)
    c3b.wait_recv()
    attention(ox)
    co.wait_recv()
    cob.wait_recv()

    wo_all = wob[...].reshape(512, 1024)
    middle = lat[...].astype(F32) + dot(mix[...], wo_all, NN)
    mid[...] = middle
    fmean = jnp.mean(middle, axis=-1, keepdims=True)
    fcen = middle - fmean
    frs = lax.rsqrt(jnp.mean(fcen * fcen, axis=-1, keepdims=True) + EPS)
    hid[r] = (fcen * frs * vec[4:5, :] + vec[5:6, :]).astype(BF16)
    hids = [wire.send(hid.at[r], hid.at[r], (peer(k), j)) for k in (3, 2, 1)]

    in_up.wait()
    in_dn.wait()
    for copy in ups:
        copy.wait_recv()
    cup = same(upb.at[:, :, at(c * 256, 256)], cpart)
    for copy in dns:
        copy.wait_recv()
    cdn = same(dnb.at[c], cpart)
    for copy in hids:
        copy.wait_recv()
    for copy in cots:
        copy.wait_recv()
    cup.wait_recv()
    cdn.wait_recv()

    hid_all = hid[...].reshape(256, 1024)
    cot_all = cota[...].reshape(256, 1024)
    up_all = upb[...].reshape(1024, 512)
    dn_all = dnb[...].reshape(512, 1024)
    inner = dot(hid_all, up_all, NN)
    phi = 0.5 * (1.0 + lax.erf(inner * (0.5**0.5)))
    act[...] = (inner * phi).astype(BF16)
    agrad = dot(cot_all, dn_all, NT)
    dens = jnp.exp(inner * inner * -0.5) * 0.3989422804014327
    ig[...] = (agrad * (phi + inner * dens)).astype(BF16)
    hgs[...] = dot(ig[...], up_all, NT).astype(BF16).reshape(4, 64, 1024)

    def reduce_sends(src, dst):
        out = []
        slot = x * 4 + r
        for k in (7, 6, 5, 3, 2, 1, 4):
            kx, kr = k // 4, k % 4
            tx = ox if kx else x
            tr = peer(kr) % 4
            dev = (peer(kr), jx if kx else j)
            out.append(wire.send(src.at[tr, at(tx * 32, 32), :], dst.at[slot], dev))
        keep = pltpu.make_async_copy(
            src.at[r, at(x * 32, 32), :], dst.at[slot], local_sem.at[len(local)]
        )
        keep.start()
        local.append(keep)
        return out, keep

    hg_in, hg_keep = reduce_sends(hgs, hgr)

    gus[...] = dot(hid_all, ig[:, at(oc * 256, 256)], TN).astype(BF16).reshape(8, 128, 256)
    gu_in = wire.send(gus, gur, cpart)
    gds[...] = dot(act[:, at(oc * 256, 256)], cot_all, TN).astype(BF16)
    gd_in = wire.send(gds, gdr, cpart)
    guo[...] = dot(hid_all, ig[:, at(c * 256, 256)], TN).reshape(8, 128, 256)
    gdo[...] = dot(act[:, at(c * 256, 256)], cot_all, TN)

    hg_keep.wait()
    for copy in hg_in:
        copy.wait_recv()

    def sum_of(ref, n):
        total = ref[0].astype(F32)
        for s in range(1, n):
            total = total + ref[s].astype(F32)
        return total

    hgx[x] = sum_of(hgr, 8).astype(BF16)
    hgx_in = same(hgx.at[x], xpart)

    fos[...] = dot(act[...], dn_all, NN).astype(BF16).reshape(4, 64, 1024)
    gu_in.wait_recv()
    gu[...] = (guo[...] + gur[...].astype(F32)).astype(BF16)
    gua[i] = gu[i]
    gu_out = [wire.send(gu.at[peer(k)], gua.at[i], (peer(k), j)) for k in (4, 5, 6, 7, 1, 2, 3)]
    gd_in.wait_recv()
    gd[...] = (gdo[...] + gdr[...].astype(F32)).astype(BF16)
    gda[i] = gd[:, at(i * 128, 128)]
    gd_out = [
        wire.send(gd.at[:, at(peer(k) * 128, 128)], gda.at[i], (peer(k), j))
        for k in (4, 5, 6, 7, 1, 2, 3)
    ]

    hgx_in.wait_recv()
    fo_in, fo_keep = reduce_sends(fos, fors)
    dy = hgx[...].reshape(64, 1024).astype(F32)
    middle = mid[...]
    fmean = jnp.mean(middle, axis=-1, keepdims=True)
    fcen = middle - fmean
    frs = lax.rsqrt(jnp.mean(fcen * fcen, axis=-1, keepdims=True) + EPS)
    dz, zhat = norm_back(middle, fmean, frs, vec[4:5, :], dy)

    def put_vec(k, v):
        for ii in range(8):
            vgs[ii, k : k + 1, :] = v[:, ii * 128 : (ii + 1) * 128]

    put_vec(4, jnp.sum(dy * zhat, axis=0, keepdims=True))
    put_vec(5, jnp.sum(dy, axis=0, keepdims=True))
    middle_grad = cota[r].astype(F32) + dz
    midg[...] = middle_grad
    low = middle_grad.astype(BF16)
    wo_all = wob[...].reshape(512, 1024)
    mgr_all = dot(low, wo_all, NT).astype(BF16)
    for g in (0, 1):
        mgr[g] = mgr_all[:, g * 256 : (g + 1) * 256]
    lowb[...] = low

    def back(g):
        m4 = spread(mgr[g])
        q4 = spread(qb[g])

        def first(t, delta):
            rows = at(t * 192, 192)
            vg = dot(attl[g, rows, :], m4, NN).astype(BF16)
            kvg[rows, at(g * 512 + 128, 128)] = vg[:, :128]
            kvg[rows, at(g * 512 + 384, 128)] = vg[:, 128:]
            ag = dot(vb[g, rows, :], m4, NT)
            pa = att[g, rows, :] * ag
            dxs[rows, 0:256] = pa
            return delta + jnp.sum(pa, axis=0, keepdims=True)

        delta = lax.fori_loop(0, 7, first, jnp.zeros((1, 256), F32))

        def second(t, total):
            rows = at(t * 192, 192)
            sg = (dxs[rows, 0:256] - att[g, rows, :] * delta).astype(BF16)
            kg = (dot(sg, q4, NN) * 0.125).astype(BF16)
            kvg[rows, at(g * 512, 128)] = kg[:, :128]
            kvg[rows, at(g * 512 + 256, 128)] = kg[:, 128:]
            return total + dot(sg, kb[g, rows, :], TN)

        total = lax.fori_loop(0, 7, second, jnp.zeros((256, 256), F32))
        qg[g] = (gather_heads(total) * 0.125).astype(BF16)

    back(x)
    def weight_tile(t, carry):
        cols = at(t * 256, 256)
        two = pl.ds(t * 2, 2)
        o = dot(kin[:, cols], kvg[:, at(x * 512 + oc * 256, 256)], TN)
        cgs[two, :, 0:256] = o.astype(BF16).reshape(2, 128, 256)
        gown[cols, 0:256] = dot(kin[:, cols], kvg[:, at(x * 512 + c * 256, 256)], TN)
        return carry

    lax.fori_loop(0, 4, weight_tile, 0)

    def small_tile(t, carry):
        cols = at(t * 256, 256)
        dxs[cols, 0:256] = dot(kin[1280:1344, cols], qg[x], TN)
        dxs[cols, 256:512] = dot(lowb[:, cols], mix[:, at(x * 256, 256)], TN)
        return carry

    lax.fori_loop(0, 4, small_tile, 0)
    gown[:, 256:384] = dxs[0:1024, at(c * 128, 128)]
    gown[:, 384:512] = dxs[0:1024, at(256 + c * 128, 128)]
    cgs[:, :, 256:384] = dxs[0:1024, at(oc * 128, 128)].astype(BF16).reshape(8, 128, 128)
    cgs[:, :, 384:512] = dxs[0:1024, at(256 + oc * 128, 128)].astype(BF16).reshape(8, 128, 128)
    cg_in = wire.send(cgs, cgr, cpart)

    back(ox)

    cg_in.wait_recv()
    g1[...] = (
        (gown[...].reshape(8, 128, 512) + cgr[...].astype(F32)).astype(BF16).reshape(4, 2, 128, 512)
    )
    y_in = wire.send(g1.at[:, 1 - yy], yr, ypart)

    def dx_tile(rows):
        w_all = jnp.concatenate([w_kv(0, 0), w_kv(0, 1), w_kv(1, 0), w_kv(1, 1)], axis=1)
        return dot(kvg[rows, :], w_all, NT)

    accg[...] = jnp.zeros((8, 1024), F32)
    accb[...] = jnp.zeros((8, 1024), F32)
    out_base = wire.take(5)

    def out_copy(t, slot):
        rows = at(t * 256, 256)
        return wire.make(slot, mgo.at[rows, :], media_out.at[c, rows, :], cpart)

    def keep_copy(t):
        rows = at(t * 256, 256)
        return pltpu.make_async_copy(
            mgo.at[rows, :], media_out.at[c, rows, :], local_sem.at[20 + t]
        )

    def media_back(t, carry):
        dxs[0:256, :] = dx_tile(at(t * 256, 256))

        def strip(u, carry):
            here = at(u * 16, 16)
            rows = at(t * 256 + u * 16, 16)
            v = xin[rows, :].astype(F32)
            dy = dxs[here, :]
            dz, zhat = norm_back(v, mu[rows, :], rs[rows, :], vec[0:1, :], dy)
            mgo[rows, :] = dz.astype(BF16)
            pz = dy * zhat
            accg[...] += pz[0:8, :] + pz[8:16, :]
            accb[...] += dy[0:8, :] + dy[8:16, :]
            return carry

        lax.fori_loop(0, 16, strip, 0)
        out_copy(t, out_base + t).start()
        keep_copy(t).start()
        return carry

    lax.fori_loop(0, 5, media_back, 0)
    put_vec(0, jnp.sum(accg[...], axis=0, keepdims=True))
    put_vec(1, jnp.sum(accb[...], axis=0, keepdims=True))
    dxs[0:64, :] = dx_tile(pl.ds(1280, 64))
    q_all = jnp.concatenate([qg[0], qg[1]], axis=1)
    wq_all = jnp.concatenate([w_q(0, 0), w_q(0, 1), w_q(1, 0), w_q(1, 1)], axis=1)
    lsum = dxs[0:64, :] + dot(q_all, wq_all, NT)
    lat32 = lat[...].astype(F32)
    dz, zhat = norm_back(lat32, mu[1280:1344, :], rs[1280:1344, :], vec[2:3, :], lsum)
    outg[...] = (midg[...] + dz).astype(BF16)
    lg_in = wire.send(outg, lgrad_out.at[c], cpart)
    lg_keep = pltpu.make_async_copy(outg, lgrad_out.at[c], local_sem.at[25])
    lg_keep.start()
    put_vec(2, jnp.sum(lsum * zhat, axis=0, keepdims=True))
    put_vec(3, jnp.sum(lsum, axis=0, keepdims=True))
    for ii in range(8):
        vgs[ii, 6:8, :] = jnp.zeros((2, 128), F32)
    vg_in = wire.send(vgs, vgc, cpart)

    y_in.wait_recv()
    total = g1[:, yy].astype(F32) + yr[...].astype(F32)
    g2[...] = total.astype(BF16)
    z_in = [wire.send(g2.at[peer(2 * k) // 2], zr.at[z], (peer(2 * k), j)) for k in (1, 2, 3)]
    zr[z] = g2[z]

    vg_in.wait_recv()
    vgt[...] = vgs[...] + vgc[...]
    vga[i] = vgt[i]
    v_in = [wire.send(vgt.at[peer(k)], vga.at[i], (peer(k), j)) for k in range(1, 8)]

    fo_keep.wait()
    for copy in fo_in:
        copy.wait_recv()
    fox[x] = sum_of(fors, 8).astype(BF16)
    fox_in = same(fox.at[x], xpart)

    for copy in gu_out:
        copy.wait_recv()
    for q in range(4):
        gup[:, q * 256 : (q + 1) * 256] = gua[q].astype(F32) + gua[4 + q].astype(F32)
    for copy in gd_out:
        copy.wait_recv()
    for q in range(4):
        gdown[q * 256 : (q + 1) * 256, :] = gda[q].astype(F32) + gda[4 + q].astype(F32)

    fox_in.wait_recv()
    outl[...] = (mid[...] + fox[...].reshape(64, 1024).astype(F32)).astype(BF16)
    lo_in = wire.send(outl, lat_out.at[c], cpart)
    lo_keep = pltpu.make_async_copy(outl, lat_out.at[c], local_sem.at[26])
    lo_keep.start()

    for copy in z_in:
        copy.wait_recv()
    last = sum_of(zr, 4)
    gk[...] = last[:, 0:128]
    gv[...] = last[:, 128:256]
    gq[...] = last[:, 256:384]
    go[...] = last[:, 384:512].T
    for copy in v_in:
        copy.wait_recv()
    sums = sum_of(vga, 8)
    for k, ref in enumerate((vec0, vec1, vec2, vec3, vec4, vec5)):
        ref[...] = sums[k : k + 1, :]

    for t in range(5):
        keep_copy(t).wait()
        out = out_copy(t, out_base + t)
        out.wait_send()
        out.wait_recv()
    lg_keep.wait()
    lo_keep.wait()
    lg_in.wait_recv()
    lo_in.wait_recv()
    wire.drain()


SCRATCH = (
    ("prm_own", (8, 128), F32),
    ("prm", (8, 8, 128), F32),
    ("vec", (8, 1024), F32),
    ("xin", (1280, 1024), BF16),
    ("lat", (64, 1024), BF16),
    ("kin", (1344, 1024), BF16),
    ("mu", (1344, 1), F32),
    ("rs", (1344, 1), F32),
    ("w3", (2, 8, 128, 768), BF16),
    ("wob", (4, 128, 1024), BF16),
    ("upb", (8, 128, 512), BF16),
    ("dnb", (2, 256, 1024), BF16),
    ("kb", (2, 1344, 256), BF16),
    ("vb", (2, 1344, 256), BF16),
    ("qb", (2, 64, 256), BF16),
    ("att", (2, 1344, 256), F32),
    ("attl", (2, 1344, 256), BF16),
    ("mix", (64, 512), BF16),
    ("mid", (64, 1024), F32),
    ("hid", (4, 64, 1024), BF16),
    ("cota", (4, 64, 1024), BF16),
    ("act", (256, 512), BF16),
    ("ig", (256, 512), BF16),
    ("hgs", (4, 64, 1024), BF16),
    ("hgr", (8, 32, 1024), BF16),
    ("hgx", (2, 32, 1024), BF16),
    ("fos", (4, 64, 1024), BF16),
    ("fors", (8, 32, 1024), BF16),
    ("fox", (2, 32, 1024), BF16),
    ("gus", (8, 128, 256), BF16),
    ("gur", (8, 128, 256), BF16),
    ("guo", (8, 128, 256), F32),
    ("gu", (8, 128, 256), BF16),
    ("gua", (8, 128, 256), BF16),
    ("gds", (256, 1024), BF16),
    ("gdr", (256, 1024), BF16),
    ("gdo", (256, 1024), F32),
    ("gd", (256, 1024), BF16),
    ("gda", (8, 256, 128), BF16),
    ("midg", (64, 1024), F32),
    ("lowb", (64, 1024), BF16),
    ("mgr", (2, 64, 256), BF16),
    ("kvg", (1344, 1024), BF16),
    ("qg", (2, 64, 256), BF16),
    ("cgs", (8, 128, 512), BF16),
    ("cgr", (8, 128, 512), BF16),
    ("gown", (1024, 512), F32),
    ("g1", (4, 2, 128, 512), BF16),
    ("yr", (4, 128, 512), BF16),
    ("g2", (4, 128, 512), BF16),
    ("zr", (4, 128, 512), BF16),
    ("dxs", (1344, 1024), F32),
    ("accg", (8, 1024), F32),
    ("accb", (8, 1024), F32),
    ("mgo", (1280, 1024), BF16),
    ("outl", (64, 1024), BF16),
    ("outg", (64, 1024), BF16),
    ("vgs", (8, 8, 128), F32),
    ("vgc", (8, 8, 128), F32),
    ("vgt", (8, 8, 128), F32),
    ("vga", (8, 8, 128), F32),
)


def fused(media, latents, cotangent, image_counts, wq, wk, wv, wo, up, down, *gains):
    anyspace = pl.BlockSpec(memory_space=pl.ANY)
    vmem = pl.BlockSpec(memory_space=pltpu.VMEM)
    smem = pl.BlockSpec(memory_space=pltpu.SMEM)
    shape = jax.ShapeDtypeStruct
    outs = pl.pallas_call(
        layer_kernel,
        out_shape=[
            shape(latents.shape, BF16),
            shape(media.shape, BF16),
            shape(latents.shape, BF16),
            shape(wq.shape, F32),
            shape(wk.shape, F32),
            shape(wv.shape, F32),
            shape(wo.shape, F32),
            shape(up.shape, F32),
            shape(down.shape, F32),
        ]
        + [shape((1, 128), F32)] * 6,
        in_specs=[smem] + [anyspace] * 9 + [vmem] * 6,
        out_specs=[anyspace] * 3 + [vmem] * 12,
        scratch_shapes=[
            pltpu.SemaphoreType.DMA((SEMS,)),
            pltpu.SemaphoreType.DMA((SEMS,)),
            pltpu.SemaphoreType.DMA((32,)),
        ]
        + [pltpu.VMEM(size, kind) for _, size, kind in SCRATCH],
        compiler_params=pltpu.CompilerParams(
            collective_id=0, has_side_effects=True, vmem_limit_bytes=60 * 2**20
        ),
        cost_estimate=pl.CostEstimate(
            flops=14 * 10**9, bytes_accessed=20 * 10**6, transcendentals=10**6
        ),
    )(
        image_counts,
        media,
        latents,
        cotangent,
        wq,
        wk,
        wv,
        wo,
        up,
        down,
        *[v.reshape(1, 128) for v in gains],
    )
    return tuple(outs[:9]) + tuple(v.reshape(128) for v in outs[9:])


def fits(mesh):
    return mesh.shape["dp"] == 8 and mesh.shape["mp"] == 4


MB = 2
SB = 1


def layer_norm(inputs, gain, bias):
    center = inputs - jnp.mean(inputs, axis=-1, keepdims=True)
    spread = jnp.mean(center * center, axis=-1, keepdims=True)
    return center * lax.rsqrt(spread + 1e-05) * gain + bias


def gelu_exact(inputs):
    return jax.nn.gelu(inputs, approximate=False)


def add_tuples(left, right):
    return tuple((first + second for first, second in zip(left, right)))


def micro_step(gathered, media, latents, cotangent, counts):
    (
        query_matrix,
        k_weight,
        v_weight,
        output_projection_weight,
        up_projection_weight,
        down_projection_weight,
        media_gain,
        media_bias,
        latent_gain,
        latent_bias,
        ff_gain,
        ff_bias,
    ) = gathered
    samples = media.shape[0]
    media_len = media.shape[1]
    latent_len = latents.shape[1]
    keys_len = media_len + latent_len
    span = query_matrix.shape[1]
    local_heads = span // HEAD
    wide_rows = jnp.float32
    key_matrix = jnp.concatenate([k_weight, v_weight], axis=1)
    latent_full = latents.astype(wide_rows)
    latent_norm32, latent_pull = jax.vjp(
        layer_norm, latent_full, latent_gain.astype(wide_rows), latent_bias.astype(wide_rows)
    )
    latent_normed_rows = latent_norm32.astype(jnp.bfloat16)
    media_norm32, media_pull = jax.vjp(
        layer_norm,
        media.astype(wide_rows),
        media_gain.astype(wide_rows),
        media_bias.astype(wide_rows),
    )
    media_norm = media_norm32.astype(jnp.bfloat16)
    media_kv = jnp.einsum(
        "snd,dh->snh", media_norm, key_matrix, preferred_element_type=wide_rows
    ).astype(jnp.bfloat16)
    query_rows = jnp.einsum(
        "gjm,mu->gju", latent_normed_rows, query_matrix, preferred_element_type=wide_rows
    ).astype(jnp.bfloat16)
    latent_kv = jnp.einsum(
        "gjm,mu->gju", latent_normed_rows, key_matrix, preferred_element_type=wide_rows
    ).astype(jnp.bfloat16)
    both_kv = jnp.concatenate([media_kv, latent_kv], axis=1)
    head_queries = query_rows.reshape(samples, latent_len, local_heads, HEAD)
    head_keys = both_kv[:, :, :span].reshape(samples, keys_len, local_heads, HEAD)
    head_values = both_kv[:, :, span:].reshape(samples, keys_len, local_heads, HEAD)
    places = jnp.arange(keys_len)
    valid = jnp.logical_or(places[None, :] // PATCH < counts[:, None], places[None, :] >= media_len)

    def scores_of():
        raw = (
            jnp.einsum("slhe,snhe->shln", head_queries, head_keys, preferred_element_type=wide_rows)
            * 0.125
        )
        return jnp.where(valid[:, None, None, :], raw, -1e30)

    scores = scores_of()
    row_max = jnp.max(scores, axis=-1, keepdims=True)
    logsum = row_max + jnp.log(jnp.sum(jnp.exp(scores - row_max), axis=-1, keepdims=True))
    attend_low = jnp.exp(scores - logsum).astype(jnp.bfloat16)
    mixed_rows = jnp.einsum(
        "shln,snhe->slhe", attend_low, head_values, preferred_element_type=wide_rows
    )
    mixed_rows = mixed_rows.reshape(samples, latent_len, span).astype(jnp.bfloat16)
    attn_out = lax.psum(
        jnp.einsum(
            "rwa,ax->rwx", mixed_rows, output_projection_weight, preferred_element_type=wide_rows
        ),
        "mp",
    )
    middle = latent_full + attn_out
    hidden32, ff_pull = jax.vjp(
        layer_norm, middle, ff_gain.astype(wide_rows), ff_bias.astype(wide_rows)
    )
    hidden_rows = hidden32.astype(jnp.bfloat16)
    inner_rows = jnp.einsum(
        "qab,bo->qao", hidden_rows, up_projection_weight, preferred_element_type=wide_rows
    )
    active32, gelu_pull = jax.vjp(gelu_exact, inner_rows)
    active_units = active32.astype(jnp.bfloat16)
    ff_out = lax.psum(
        jnp.einsum(
            "pye,ej->pyj", active_units, down_projection_weight, preferred_element_type=wide_rows
        ).astype(jnp.bfloat16),
        "mp",
    ).astype(jnp.float32)
    result = (middle + ff_out).astype(jnp.bfloat16)
    down_projection_grad = jnp.einsum(
        "kje,kju->eu", active_units, cotangent, preferred_element_type=wide_rows
    )
    active_units_grad = jnp.einsum(
        "jvw,ow->jvo", cotangent, down_projection_weight, preferred_element_type=wide_rows
    )
    (inner_grad,) = gelu_pull(active_units_grad)
    inner_rows_reduced = inner_grad.astype(jnp.bfloat16)
    up_projection_grad = jnp.einsum(
        "imw,imk->wk", hidden_rows, inner_rows_reduced, preferred_element_type=wide_rows
    )
    hidden_grad = lax.psum(
        jnp.einsum(
            "xvm,nm->xvn",
            inner_rows_reduced,
            up_projection_weight,
            preferred_element_type=wide_rows,
        ).astype(jnp.bfloat16),
        "mp",
    ).astype(jnp.float32)
    middle_part, ff_gain_grad, ff_bias_grad = ff_pull(hidden_grad)
    middle_grad = cotangent.astype(wide_rows) + middle_part
    middle_rows_reduced = middle_grad.astype(jnp.bfloat16)
    output_projection_grad = jnp.einsum(
        "gfb,gfw->bw", mixed_rows, middle_rows_reduced, preferred_element_type=wide_rows
    )
    mixed_grad = jnp.einsum(
        "kzw,nw->kzn",
        middle_rows_reduced,
        output_projection_weight,
        preferred_element_type=wide_rows,
    ).astype(jnp.bfloat16)
    mixed_grad = mixed_grad.reshape(samples, latent_len, local_heads, HEAD)
    attend = jnp.exp(scores_of() - logsum)
    attend_grad = jnp.einsum(
        "slhe,snhe->shln", mixed_grad, head_values, preferred_element_type=wide_rows
    )
    score_grad = attend * (attend_grad - jnp.sum(attend * attend_grad, axis=-1, keepdims=True))
    score_grad = score_grad.astype(jnp.bfloat16)
    query_rows_grad = (
        jnp.einsum("shln,snhe->slhe", score_grad, head_keys, preferred_element_type=wide_rows)
        * 0.125
    )
    query_rows_grad = query_rows_grad.astype(jnp.bfloat16).reshape(samples, latent_len, span)
    key_grad = (
        jnp.einsum("shln,slhe->snhe", score_grad, head_queries, preferred_element_type=wide_rows)
        * 0.125
    )
    key_grad = key_grad.astype(jnp.bfloat16).reshape(samples, keys_len, span)
    value_grad = jnp.einsum(
        "shln,slhe->snhe", attend_low, mixed_grad, preferred_element_type=wide_rows
    )
    value_grad = value_grad.astype(jnp.bfloat16).reshape(samples, keys_len, span)
    kv_grad = jnp.concatenate([key_grad, value_grad], axis=2)
    media_kv_grad = kv_grad[:, :media_len]
    latent_key_value_grad = kv_grad[:, media_len:]
    query_weight_grad = jnp.einsum(
        "cbi,cbu->iu", latent_normed_rows, query_rows_grad, preferred_element_type=wide_rows
    )
    latent_wgrad = jnp.einsum(
        "cbi,cbu->iu", latent_normed_rows, latent_key_value_grad, preferred_element_type=wide_rows
    )
    latent_portion = jnp.einsum(
        "kwt,gt->kwg", query_rows_grad, query_matrix, preferred_element_type=wide_rows
    )
    latent_portion = latent_portion + jnp.einsum(
        "kwt,gt->kwg", latent_key_value_grad, key_matrix, preferred_element_type=wide_rows
    )
    media_part = jnp.einsum(
        "snh,dh->snd", media_kv_grad, key_matrix, preferred_element_type=wide_rows
    )
    media_wgrad = jnp.einsum(
        "snd,snh->dh", media_norm, media_kv_grad, preferred_element_type=wide_rows
    )
    kv_weight_grad = media_wgrad + latent_wgrad
    media_sum, latent_sum = (
        lax.psum(media_part.astype(jnp.bfloat16), "mp").astype(jnp.float32),
        lax.psum(latent_portion.astype(jnp.bfloat16), "mp").astype(jnp.float32),
    )
    media_back, media_gain_grad, media_bias_grad = media_pull(media_sum)
    media_out = media_back.astype(jnp.bfloat16)
    latent_back, latent_gain_grad, latent_bias_grad = latent_pull(latent_sum)
    latent_grad = middle_grad + latent_back
    grads = (
        query_weight_grad,
        kv_weight_grad[:, :span],
        kv_weight_grad[:, span:],
        output_projection_grad,
        up_projection_grad,
        down_projection_grad,
        media_gain_grad,
        media_bias_grad,
        latent_gain_grad,
        latent_bias_grad,
        ff_gain_grad,
        ff_bias_grad,
    )
    return (result, media_out, latent_grad.astype(jnp.bfloat16), grads)


def local(
    media,
    latents,
    cotangent,
    image_counts,
    query_matrix,
    k_weight,
    v_weight,
    output_projection_weight,
    up_projection_weight,
    down_projection_weight,
    media_gain,
    media_bias,
    latent_gain,
    latent_bias,
    ff_gain,
    ff_bias,
):
    results = []
    media_grads = []
    latent_grads = []
    totals = ()
    for micro_index in range(MB):
        gathered = (
            lax.all_gather(query_matrix, "dp", axis=0, tiled=True),
            lax.all_gather(k_weight, "dp", axis=0, tiled=True),
            lax.all_gather(v_weight, "dp", axis=0, tiled=True),
            lax.all_gather(output_projection_weight, "dp", axis=1, tiled=True),
            lax.all_gather(up_projection_weight, "dp", axis=0, tiled=True),
            lax.all_gather(down_projection_weight, "dp", axis=1, tiled=True),
            lax.all_gather(media_gain, "dp", axis=0, tiled=True),
            lax.all_gather(media_bias, "dp", axis=0, tiled=True),
            lax.all_gather(latent_gain, "dp", axis=0, tiled=True),
            lax.all_gather(latent_bias, "dp", axis=0, tiled=True),
            lax.all_gather(ff_gain, "dp", axis=0, tiled=True),
            lax.all_gather(ff_bias, "dp", axis=0, tiled=True),
        )
        lower = micro_index * SB
        upper = lower + SB
        result, media_back, latent_back, grads = micro_step(
            gathered,
            media[lower:upper],
            latents[lower:upper],
            cotangent[lower:upper],
            image_counts[lower:upper],
        )
        grads = (
            lax.psum_scatter(grads[0], "dp", scatter_dimension=0, tiled=True),
            lax.psum_scatter(grads[1], "dp", scatter_dimension=0, tiled=True),
            lax.psum_scatter(grads[2], "dp", scatter_dimension=0, tiled=True),
            lax.psum_scatter(grads[3], "dp", scatter_dimension=1, tiled=True),
            lax.psum_scatter(grads[4], "dp", scatter_dimension=0, tiled=True),
            lax.psum_scatter(grads[5], "dp", scatter_dimension=1, tiled=True),
            lax.psum_scatter(grads[6], "dp", scatter_dimension=0, tiled=True),
            lax.psum_scatter(grads[7], "dp", scatter_dimension=0, tiled=True),
            lax.psum_scatter(grads[8], "dp", scatter_dimension=0, tiled=True),
            lax.psum_scatter(grads[9], "dp", scatter_dimension=0, tiled=True),
            lax.psum_scatter(grads[10], "dp", scatter_dimension=0, tiled=True),
            lax.psum_scatter(grads[11], "dp", scatter_dimension=0, tiled=True),
        )
        totals = grads if micro_index == 0 else add_tuples(totals, grads)
        results.append(result)
        media_grads.append(media_back)
        latent_grads.append(latent_back)
    return (
        jnp.concatenate(results, axis=0),
        jnp.concatenate(media_grads, axis=0),
        jnp.concatenate(latent_grads, axis=0),
        totals[0],
        totals[1],
        totals[2],
        totals[3],
        totals[4],
        totals[5],
        totals[6],
        totals[7],
        totals[8],
        totals[9],
        totals[10],
        totals[11],
    )


def solution(mesh):
    placed = (
        P("dp", None, None),
        P("dp", None, None),
        P("dp", None, None),
        P("dp"),
        P("dp", "mp"),
        P("dp", "mp"),
        P("dp", "mp"),
        P("mp", "dp"),
        P("dp", "mp"),
        P("mp", "dp"),
        P("dp"),
        P("dp"),
        P("dp"),
        P("dp"),
        P("dp"),
        P("dp"),
    )
    return jax.shard_map(
        fused if fits(mesh) else local,
        mesh=mesh,
        in_specs=placed,
        out_specs=(
            P("dp", None, None),
            P("dp", None, None),
            P("dp", None, None),
            P("dp", "mp"),
            P("dp", "mp"),
            P("dp", "mp"),
            P("mp", "dp"),
            P("dp", "mp"),
            P("mp", "dp"),
            P("dp"),
            P("dp"),
            P("dp"),
            P("dp"),
            P("dp"),
            P("dp"),
        ),
        check_vma=False,
    )
```

```python
import functools

import jax
import jax.numpy as jnp
from jax import lax
from jax.experimental import pallas as pl
from jax.experimental.pallas import tpu as pltpu
from jax.sharding import PartitionSpec as P

HEAD = 64
PATCH = 256
EPS = 1e-05
F32 = jnp.float32
BF16 = jnp.bfloat16
MESH = pl.DeviceIdType.MESH
NN = (((1,), (0,)), ((), ()))
NT = (((1,), (1,)), ((), ()))
TN = (((0,), (0,)), ((), ()))
SEMS = 112


def dot(a, b, dims):
    return lax.dot_general(a, b, dims, preferred_element_type=F32)


def at(start, size):
    return pl.ds(pl.multiple_of(start, size), size)


class Wire:
    def __init__(self, send_sem, recv_sem):
        self.send_sem, self.recv_sem = send_sem, recv_sem
        self.used, self.sent = 0, []

    def take(self, count=1):
        first = self.used
        self.used += count
        assert self.used <= SEMS
        return first

    def make(self, slot, src, dst, dev):
        return pltpu.make_async_remote_copy(
            src_ref=src,
            dst_ref=dst,
            send_sem=self.send_sem.at[slot],
            recv_sem=self.recv_sem.at[slot],
            device_id=dev,
            device_id_type=MESH,
        )

    def send(self, src, dst, dev):
        copy = self.make(self.take(), src, dst, dev)
        copy.start()
        self.sent.append(copy)
        return copy

    def drain(self):
        for copy in self.sent:
            copy.wait_send()


def norm_back(z, mean, rstd, gain, dy):
    zhat = (z - mean) * rstd
    t = dy * gain
    mt = jnp.mean(t, axis=-1, keepdims=True)
    mz = jnp.mean(t * zhat, axis=-1, keepdims=True)
    return rstd * (t - mt - zhat * mz), zhat


def layer_kernel(
    counts,
    media,
    latents,
    cot,
    wq,
    wk,
    wv,
    wo,
    up,
    down,
    mg,
    mb,
    lg,
    lb,
    fg,
    fb,
    lat_out,
    media_out,
    lgrad_out,
    gmat,
    gup,
    gdown,
    vecs,
    send_sem,
    recv_sem,
    local_sem,
    prm_own,
    prm,
    vec,
    xin,
    lat,
    kin,
    mu,
    rs,
    w3,
    wob,
    upb,
    dnb,
    kb,
    vb,
    qb,
    att,
    attl,
    mix,
    mid,
    hid,
    cota,
    act,
    ig,
    hgs,
    hgr,
    hgx,
    fos,
    fors,
    fox,
    gus,
    gur,
    guo,
    gu,
    gua,
    gds,
    gdr,
    gdo,
    gd,
    gda,
    midg,
    lowb,
    mgr,
    kg,
    vg,
    qg,
    cgs,
    cgr,
    gown,
    g1,
    yr,
    g2,
    zr,
    dxs,
    accg,
    accb,
    mgo,
    outl,
    outg,
    wsc,
    gupv,
    gdnv,
    gmv,
    vsum,
    vgs,
    vgc,
    vgt,
    vga,
):
    i = lax.axis_index("dp")
    j = lax.axis_index("mp")
    x, c = j // 2, j % 2
    yy, z = i % 2, i // 2
    zlo, zhi = z % 2, z // 2
    r = i % 4

    def peer(k):
        a = 1 - yy if k & 1 else yy
        b = 1 - zlo if k & 2 else zlo
        d = 1 - zhi if k & 4 else zhi
        return d * 4 + b * 2 + a

    jx = j + 2 - 4 * x
    jc = j + 1 - 2 * c
    ox = 1 - x
    oc = 1 - c
    xpart = (i, jx)
    cpart = (i, jc)
    ypart = (peer(1), j)
    wire = Wire(send_sem, recv_sem)

    def w3b(ii, xx, cc):
        return w3.at[xx, ii // 2, ii % 2, :, :, at(cc * 128, 128)]

    def w3col(xx, y_, cc):
        return w3.at[xx, :, y_, :, :, at(cc * 128, 128)]

    local = []

    def bring(src, dst):
        copy = pltpu.make_async_copy(src, dst, local_sem.at[len(local)])
        copy.start()
        local.append(copy)
        return copy

    bring(wk, w3.at[x, z, yy, 0, :, at(c * 128, 128)])
    bring(wv, w3.at[x, z, yy, 1, :, at(c * 128, 128)])
    bring(wq, w3.at[x, z, yy, 2, :, at(c * 128, 128)])
    bring(wo, wob.at[j, :, at(i * 128, 128)])
    in_lat = bring(latents.at[c], lat)
    in_media = bring(media.at[c], xin)
    in_cot = bring(cot.at[c], cota.at[r])
    in_up = bring(up.at[:, at(r * 256, 256)], upb.at[i, :, at(c * 256, 256)])
    in_dn = bring(down.at[at(r * 256, 256), :], dnb.at[c, :, at(i * 128, 128)])
    for row, ref in enumerate((mg, mb, lg, lb, fg, fb)):
        prm_own[row : row + 1, :] = ref[...].astype(F32)
    prm_own[6:8, :] = jnp.zeros((2, 128), F32)
    prm[i] = prm_own[...]

    barrier = pltpu.get_barrier_semaphore()
    partners = [(peer(k), j) for k in range(1, 8)] + [xpart, cpart]
    partners += [(peer(k), jx) for k in range(1, 4)]
    for dev in partners:
        pl.semaphore_signal(barrier, inc=1, device_id=dev, device_id_type=MESH)

    in_lat.wait()
    lat32 = lat[...].astype(F32)
    lmean = jnp.mean(lat32, axis=-1, keepdims=True)
    lcen = lat32 - lmean
    mu[1280:1344, :] = lmean
    rs[1280:1344, :] = lax.rsqrt(jnp.mean(lcen * lcen, axis=-1, keepdims=True) + EPS)
    in_media.wait()

    def stat(t, carry):
        rows = at(t * 64, 64)
        v = xin[rows, :].astype(F32)
        m = jnp.mean(v, axis=-1, keepdims=True)
        cen = v - m
        mu[rows, :] = m
        rs[rows, :] = lax.rsqrt(jnp.mean(cen * cen, axis=-1, keepdims=True) + EPS)
        return carry

    lax.fori_loop(0, 20, stat, 0, unroll=4)
    pl.semaphore_wait(barrier, len(partners))

    got_prm = [wire.send(prm_own, prm.at[i], (peer(k), j)) for k in range(1, 8)]
    for copy in local[:4]:
        copy.wait()

    def wo_at(ii, jj):
        return wob.at[jj, :, at(ii * 128, 128)]

    def same(view, dev):
        return wire.send(view, view, dev)

    z3 = [same(w3b(i, x, c), (peer(2 * k), j)) for k in (1, 2, 3)]
    y3 = [same(w3b(i, x, c), ypart)]
    zo = [same(wo_at(i, j), (peer(2 * k), j)) for k in (1, 2, 3)]
    yo = [same(wo_at(i, j), ypart)]
    for copy in got_prm:
        copy.wait_recv()
    for ii in range(8):
        vec[:, ii * 128 : (ii + 1) * 128] = prm[ii]

    def media_norm(lo, hi):
        def strip(t, carry):
            rows = at(t * 64, 64)
            v = (xin[rows, :].astype(F32) - mu[rows, :]) * rs[rows, :]
            kin[rows, :] = (v * vec[0:1, :] + vec[1:2, :]).astype(BF16)
            return carry

        lax.fori_loop(lo, hi, strip, 0, unroll=2)

    kin[1280:1344, :] = (
        (lat[...].astype(F32) - mu[1280:1344, :]) * rs[1280:1344, :] * vec[2:3, :] + vec[3:4, :]
    ).astype(BF16)
    media_norm(0, 10)
    for k in (1, 2, 3):
        z3[k - 1].wait_recv()
        y3.append(same(w3b(peer(2 * k), x, c), ypart))
    c3 = [same(w3col(x, yy, c), cpart)]
    x3 = [same(w3col(x, yy, c), xpart)]
    for k in (1, 2, 3):
        zo[k - 1].wait_recv()
        yo.append(same(wo_at(peer(2 * k), j), ypart))
    in_cot.wait()
    cots = [wire.send(cota.at[r], cota.at[r], (peer(k), j)) for k in (1, 2, 3)]
    ups, dns = [], []
    for k in (4, 5, 6, 7, 2, 3, 1):
        rk = peer(k) % 4
        ups.append(
            wire.send(
                up.at[:, at(rk * 256, 256)], upb.at[i, :, at(c * 256, 256)], (peer(k), j)
            )
        )
    for k in (4, 5, 6, 7, 2, 3, 1):
        rk = peer(k) % 4
        dns.append(
            wire.send(
                down.at[at(rk * 256, 256), :], dnb.at[c, :, at(i * 128, 128)], (peer(k), j)
            )
        )
    media_norm(10, 20)
    for copy in y3:
        copy.wait_recv()
    c3.append(same(w3col(x, 1 - yy, c), cpart))
    for copy in yo:
        copy.wait_recv()
    xo = same(wob.at[j], xpart)
    co = same(wob.at[j], cpart)
    x3.append(same(w3col(x, 1 - yy, c), xpart))
    for copy in c3:
        copy.wait_recv()

    count = counts[c]
    head_of_lane = lax.broadcasted_iota(jnp.int32, (256, 256), 1) // HEAD
    head_of_row = lax.broadcasted_iota(jnp.int32, (256, 256), 0) // HEAD
    own_head = head_of_lane == head_of_row
    lane64 = lax.broadcasted_iota(jnp.int32, (64, 256), 1) // HEAD

    def spread(v):
        v = v.astype(F32)
        return jnp.where(own_head, jnp.concatenate([v, v, v, v], axis=0), 0.0).astype(BF16)

    def gather_heads(v):
        out = jnp.zeros((64, 256), F32)
        for h in range(4):
            out = jnp.where(lane64 == h, v[h * 64 : (h + 1) * 64, :], out)
        return out

    def weight(g, m):
        return w3[g, :, :, m].reshape(1024, 256)

    def attention(g, mixing=True):
        a = kin[...]
        kb[g] = dot(a, weight(g, 0), NN).astype(BF16)
        vb[g] = dot(a, weight(g, 1), NN).astype(BF16)
        qb[g] = dot(kin[1280:1344, :], weight(g, 2), NN).astype(BF16)
        s = dot(kb[g], spread(qb[g]), NT) * 0.125
        key = lax.broadcasted_iota(jnp.int32, (1344, 256), 0)
        s = jnp.where(jnp.logical_or(key < count * PATCH, key >= 1280), s, -1e30)
        att[g] = s
        top = jnp.max(s, axis=0, keepdims=True)
        e = jnp.exp(att[g] - top)
        att[g] = e
        scale = 1.0 / jnp.sum(e, axis=0, keepdims=True)
        p = att[g] * scale
        att[g] = p
        attl[g] = p.astype(BF16)
        if mixing:
            mixed = dot(attl[g], vb[g], TN)
            mix[g] = gather_heads(mixed).astype(BF16)

    attention(x)
    mx = same(mix.at[x], xpart)
    xo.wait_recv()
    cob = same(wob.at[jx], cpart)
    mx.wait_recv()
    co.wait_recv()
    cob.wait_recv()

    wo_all = wob[...].reshape(512, 1024)
    middle = lat[...].astype(F32) + dot(jnp.concatenate([mix[0], mix[1]], axis=1), wo_all, NN)
    mid[...] = middle
    fmean = jnp.mean(middle, axis=-1, keepdims=True)
    fcen = middle - fmean
    frs = lax.rsqrt(jnp.mean(fcen * fcen, axis=-1, keepdims=True) + EPS)
    hid[r] = (fcen * frs * vec[4:5, :] + vec[5:6, :]).astype(BF16)
    hids = [wire.send(hid.at[r], hid.at[r], (peer(k), j)) for k in (3, 2, 1)]

    c3b = []
    for copy, y_ in zip(x3, (yy, 1 - yy)):
        copy.wait_recv()
        c3b.append(same(w3col(ox, y_, c), cpart))
    for copy in c3b:
        copy.wait_recv()
    attention(ox, False)

    in_up.wait()
    in_dn.wait()
    for copy in ups:
        copy.wait_recv()
    cup = same(upb.at[:, :, at(c * 256, 256)], cpart)
    for copy in dns:
        copy.wait_recv()
    cdn = same(dnb.at[c], cpart)
    for copy in hids:
        copy.wait_recv()
    for copy in cots:
        copy.wait_recv()
    cup.wait_recv()
    cdn.wait_recv()

    hid_all = hid[...].reshape(256, 1024)
    cot_all = cota[...].reshape(256, 1024)
    up_all = upb[...].reshape(1024, 512)
    dn_all = dnb[...].reshape(512, 1024)
    inner = dot(hid_all, up_all, NN)
    phi = 0.5 * (1.0 + lax.erf(inner * (0.5**0.5)))
    act[...] = (inner * phi).astype(BF16)
    agrad = dot(cot_all, dn_all, NT)
    dens = jnp.exp(inner * inner * -0.5) * 0.3989422804014327
    ig[...] = (agrad * (phi + inner * dens)).astype(BF16)
    hgs[...] = dot(ig[...], up_all, NT).astype(BF16).reshape(4, 64, 1024)

    def reduce_sends(src, dst):
        out = []
        slot = x * 4 + r
        for k in (7, 6, 5, 3, 2, 1, 4):
            kx, kr = k // 4, k % 4
            tx = ox if kx else x
            tr = peer(kr) % 4
            dev = (peer(kr), jx if kx else j)
            out.append(wire.send(src.at[tr, at(tx * 32, 32), :], dst.at[slot], dev))
        keep = pltpu.make_async_copy(
            src.at[r, at(x * 32, 32), :], dst.at[slot], local_sem.at[len(local)]
        )
        keep.start()
        local.append(keep)
        return out, keep

    hg_in, hg_keep = reduce_sends(hgs, hgr)

    gus[...] = dot(hid_all, ig[:, at(oc * 256, 256)], TN).astype(BF16).reshape(8, 128, 256)
    gu_in = wire.send(gus, gur, cpart)
    gds[...] = dot(act[:, at(oc * 256, 256)], cot_all, TN).astype(BF16)
    gd_in = wire.send(gds, gdr, cpart)
    guo[...] = dot(hid_all, ig[:, at(c * 256, 256)], TN).reshape(8, 128, 256)
    gdo[...] = dot(act[:, at(c * 256, 256)], cot_all, TN)

    hg_keep.wait()
    for copy in hg_in:
        copy.wait_recv()

    def sum_of(ref, n):
        total = ref[0].astype(F32)
        for s in range(1, n):
            total = total + ref[s].astype(F32)
        return total

    hgx[x] = sum_of(hgr, 8).astype(BF16)
    hgx_in = same(hgx.at[x], xpart)

    fos[...] = dot(act[...], dn_all, NN).astype(BF16).reshape(4, 64, 1024)
    gu_in.wait_recv()
    gu[...] = (guo[...] + gur[...].astype(F32)).astype(BF16)
    gua[i] = gu[i]
    gu_out = [wire.send(gu.at[peer(k)], gua.at[i], (peer(k), j)) for k in (4, 5, 6, 7, 1, 2, 3)]
    gd_in.wait_recv()
    gd[...] = (gdo[...] + gdr[...].astype(F32)).astype(BF16)
    gda[i] = gd[:, at(i * 128, 128)]
    gd_out = [
        wire.send(gd.at[:, at(peer(k) * 128, 128)], gda.at[i], (peer(k), j))
        for k in (4, 5, 6, 7, 1, 2, 3)
    ]

    hgx_in.wait_recv()
    fo_in, fo_keep = reduce_sends(fos, fors)
    dy = hgx[...].reshape(64, 1024).astype(F32)
    middle = mid[...]
    fmean = jnp.mean(middle, axis=-1, keepdims=True)
    fcen = middle - fmean
    frs = lax.rsqrt(jnp.mean(fcen * fcen, axis=-1, keepdims=True) + EPS)
    dz, zhat = norm_back(middle, fmean, frs, vec[4:5, :], dy)

    def put_vec(k, v):
        for ii in range(8):
            vgs[ii, k : k + 1, :] = v[:, ii * 128 : (ii + 1) * 128]

    put_vec(4, jnp.sum(dy * zhat, axis=0, keepdims=True))
    put_vec(5, jnp.sum(dy, axis=0, keepdims=True))
    middle_grad = cota[r].astype(F32) + dz
    midg[...] = middle_grad
    low = middle_grad.astype(BF16)
    wo_all = wob[...].reshape(512, 1024)
    mgr_all = dot(low, wo_all, NT).astype(BF16)
    for g in (0, 1):
        mgr[g] = mgr_all[:, g * 256 : (g + 1) * 256]
    lowb[...] = low

    def back_values(g):
        m4 = spread(mgr[g])

        vg[g] = dot(attl[g], m4, NN).astype(BF16)
        pa = att[g] * dot(vb[g], m4, NT)
        dxs[:, 0:256] = pa
        return jnp.sum(pa, axis=0, keepdims=True)

    def back_keys(g, delta):
        q4 = spread(qb[g])

        sg = (dxs[:, 0:256] - att[g] * delta).astype(BF16)
        attl[g] = sg
        kg[g] = (dot(sg, q4, NN) * 0.125).astype(BF16)
        total = dot(attl[g], kb[g], TN)
        qg[g] = (gather_heads(total) * 0.125).astype(BF16)

    def split(m, wide):
        wsc[...] = wide
        mine, other = wsc[at(c * 128, 128), :], wsc[at(oc * 128, 128), :]
        for ii in range(8):
            cols = slice(ii * 128, (ii + 1) * 128)
            gown[ii // 2, ii % 2, m] = mine[:, cols]
            cgs[ii // 2, ii % 2, m] = other[:, cols].astype(BF16)

    def two(ref, p):
        return ref.at[:, :, 2 * p : 2 * p + 2]

    def chip_sum(p):
        two(g1, p)[...] = (two(gown, p)[...] + two(cgr, p)[...].astype(F32)).astype(BF16)
        return wire.send(g1.at[:, 1 - yy, 2 * p : 2 * p + 2], yr.at[:, 2 * p : 2 * p + 2], ypart)

    delta = back_values(x)
    split(0, dot(vg[x], kin[...], TN))
    split(1, dot(mix[x], lowb[...], TN))
    cg_in = [wire.send(two(cgs, 0), two(cgr, 0), cpart)]
    back_keys(x, delta)
    split(2, dot(kg[x], kin[...], TN))
    split(3, dot(qg[x], kin[1280:1344, :], TN))
    cg_in.append(wire.send(two(cgs, 1), two(cgr, 1), cpart))
    y_in = []
    for p in (0, 1):
        cg_in[p].wait_recv()
        y_in.append(chip_sum(p))
    back_keys(ox, back_values(ox))

    def dx_tile(rows):
        return (
            dot(kg[0, rows, :], weight(0, 0), NT)
            + dot(kg[1, rows, :], weight(1, 0), NT)
            + dot(vg[0, rows, :], weight(0, 1), NT)
            + dot(vg[1, rows, :], weight(1, 1), NT)
        )

    accg[...] = jnp.zeros((8, 1024), F32)
    accb[...] = jnp.zeros((8, 1024), F32)
    out_base = wire.take(5)

    def out_copy(t, slot):
        rows = at(t * 256, 256)
        return wire.make(slot, mgo.at[rows, :], media_out.at[c, rows, :], cpart)

    def keep_copy(t):
        rows = at(t * 256, 256)
        return pltpu.make_async_copy(
            mgo.at[rows, :], media_out.at[c, rows, :], local_sem.at[20 + t]
        )

    def media_back(t, carry):
        dxs[0:256, :] = dx_tile(at(t * 256, 256))

        rows = at(t * 256, 256)
        v = xin[rows, :].astype(F32)
        dy = dxs[0:256, :]
        dz, zhat = norm_back(v, mu[rows, :], rs[rows, :], vec[0:1, :], dy)
        mgo[rows, :] = dz.astype(BF16)
        accg[...] += (dy * zhat).reshape(32, 8, 1024).sum(0)
        accb[...] += dy.reshape(32, 8, 1024).sum(0)
        out_copy(t, out_base + t).start()
        keep_copy(t).start()
        return carry

    def pass_on(p):
        y_in[p].wait_recv()
        here = slice(2 * p, 2 * p + 2)
        g2[:, here] = (g1[:, yy, here].astype(F32) + yr[:, here].astype(F32)).astype(BF16)
        zr[z, here] = g2[z, here]
        return [
            wire.send(g2.at[peer(2 * k) // 2, here], zr.at[z, here], (peer(2 * k), j))
            for k in (2, 3, 1)
        ]

    lax.fori_loop(0, 1, media_back, 0)
    z_in = pass_on(0)
    lax.fori_loop(1, 3, media_back, 0)
    z_in += pass_on(1)
    lax.fori_loop(3, 5, media_back, 0)
    put_vec(0, jnp.sum(accg[...], axis=0, keepdims=True))
    put_vec(1, jnp.sum(accb[...], axis=0, keepdims=True))
    dxs[0:64, :] = dx_tile(pl.ds(1280, 64))
    lsum = dxs[0:64, :] + dot(qg[0], weight(0, 2), NT) + dot(qg[1], weight(1, 2), NT)
    lat32 = lat[...].astype(F32)
    dz, zhat = norm_back(lat32, mu[1280:1344, :], rs[1280:1344, :], vec[2:3, :], lsum)
    outg[...] = (midg[...] + dz).astype(BF16)
    lg_in = wire.send(outg, lgrad_out.at[c], cpart)
    lg_keep = pltpu.make_async_copy(outg, lgrad_out.at[c], local_sem.at[25])
    lg_keep.start()
    put_vec(2, jnp.sum(lsum * zhat, axis=0, keepdims=True))
    put_vec(3, jnp.sum(lsum, axis=0, keepdims=True))
    for ii in range(8):
        vgs[ii, 6:8, :] = jnp.zeros((2, 128), F32)
    vg_in = wire.send(vgs, vgc, cpart)

    vg_in.wait_recv()
    vgt[...] = vgs[...] + vgc[...]
    vga[i] = vgt[i]
    v_in = [wire.send(vgt.at[peer(k)], vga.at[i], (peer(k), j)) for k in range(1, 8)]

    fo_keep.wait()
    for copy in fo_in:
        copy.wait_recv()
    fox[x] = sum_of(fors, 8).astype(BF16)
    fox_in = same(fox.at[x], xpart)

    for copy in gu_out:
        copy.wait_recv()
    for q in range(4):
        gupv[:, q * 256 : (q + 1) * 256] = gua[q].astype(F32) + gua[4 + q].astype(F32)
    gup_keep = pltpu.make_async_copy(gupv, gup, local_sem.at[27])
    gup_keep.start()
    for copy in gd_out:
        copy.wait_recv()
    for q in range(4):
        gdnv[q * 256 : (q + 1) * 256, :] = gda[q].astype(F32) + gda[4 + q].astype(F32)
    gdn_keep = pltpu.make_async_copy(gdnv, gdown, local_sem.at[28])
    gdn_keep.start()

    fox_in.wait_recv()
    outl[...] = (mid[...] + fox[...].reshape(64, 1024).astype(F32)).astype(BF16)
    lo_in = wire.send(outl, lat_out.at[c], cpart)
    lo_keep = pltpu.make_async_copy(outl, lat_out.at[c], local_sem.at[26])
    lo_keep.start()

    for copy in z_in:
        copy.wait_recv()
    last = sum_of(zr, 4)
    gmv[0] = last[3].T
    gmv[1] = last[2].T
    gmv[2] = last[0].T
    gmv[3] = last[1]
    gm_keep = pltpu.make_async_copy(gmv, gmat, local_sem.at[29])
    gm_keep.start()
    for copy in v_in:
        copy.wait_recv()
    vsum[...] = sum_of(vga, 8)
    v_keep = pltpu.make_async_copy(vsum, vecs, local_sem.at[30])
    v_keep.start()

    for t in range(5):
        keep_copy(t).wait()
        out = out_copy(t, out_base + t)
        out.wait_send()
        out.wait_recv()
    lg_keep.wait()
    lo_keep.wait()
    gup_keep.wait()
    gdn_keep.wait()
    gm_keep.wait()
    v_keep.wait()
    lg_in.wait_recv()
    lo_in.wait_recv()
    wire.drain()


SCRATCH = (
    ("prm_own", (8, 128), F32),
    ("prm", (8, 8, 128), F32),
    ("vec", (8, 1024), F32),
    ("xin", (1280, 1024), BF16),
    ("lat", (64, 1024), BF16),
    ("kin", (1344, 1024), BF16),
    ("mu", (1344, 1), F32),
    ("rs", (1344, 1), F32),
    ("w3", (2, 4, 2, 3, 128, 256), BF16),
    ("wob", (4, 128, 1024), BF16),
    ("upb", (8, 128, 512), BF16),
    ("dnb", (2, 256, 1024), BF16),
    ("kb", (2, 1344, 256), BF16),
    ("vb", (2, 1344, 256), BF16),
    ("qb", (2, 64, 256), BF16),
    ("att", (2, 1344, 256), F32),
    ("attl", (2, 1344, 256), BF16),
    ("mix", (2, 64, 256), BF16),
    ("mid", (64, 1024), F32),
    ("hid", (4, 64, 1024), BF16),
    ("cota", (4, 64, 1024), BF16),
    ("act", (256, 512), BF16),
    ("ig", (256, 512), BF16),
    ("hgs", (4, 64, 1024), BF16),
    ("hgr", (8, 32, 1024), BF16),
    ("hgx", (2, 32, 1024), BF16),
    ("fos", (4, 64, 1024), BF16),
    ("fors", (8, 32, 1024), BF16),
    ("fox", (2, 32, 1024), BF16),
    ("gus", (8, 128, 256), BF16),
    ("gur", (8, 128, 256), BF16),
    ("guo", (8, 128, 256), F32),
    ("gu", (8, 128, 256), BF16),
    ("gua", (8, 128, 256), BF16),
    ("gds", (256, 1024), BF16),
    ("gdr", (256, 1024), BF16),
    ("gdo", (256, 1024), F32),
    ("gd", (256, 1024), BF16),
    ("gda", (8, 256, 128), BF16),
    ("midg", (64, 1024), F32),
    ("lowb", (64, 1024), BF16),
    ("mgr", (2, 64, 256), BF16),
    ("kg", (2, 1344, 256), BF16),
    ("vg", (2, 1344, 256), BF16),
    ("qg", (2, 64, 256), BF16),
    ("cgs", (4, 2, 4, 128, 128), BF16),
    ("cgr", (4, 2, 4, 128, 128), BF16),
    ("gown", (4, 2, 4, 128, 128), F32),
    ("g1", (4, 2, 4, 128, 128), BF16),
    ("yr", (4, 4, 128, 128), BF16),
    ("g2", (4, 4, 128, 128), BF16),
    ("zr", (4, 4, 128, 128), BF16),
    ("dxs", (1344, 1024), F32),
    ("accg", (8, 1024), F32),
    ("accb", (8, 1024), F32),
    ("mgo", (1280, 1024), BF16),
    ("outl", (64, 1024), BF16),
    ("outg", (64, 1024), BF16),
    ("wsc", (256, 1024), F32),
    ("gupv", (128, 1024), F32),
    ("gdnv", (1024, 128), F32),
    ("gmv", (4, 128, 128), F32),
    ("vsum", (8, 128), F32),
    ("vgs", (8, 8, 128), F32),
    ("vgc", (8, 8, 128), F32),
    ("vgt", (8, 8, 128), F32),
    ("vga", (8, 8, 128), F32),
)


CHUNKS = 10


def hand_out(lat, med, lgr, gmat, gup, gdown, vecs, *rest):
    outs, (v_lat, v_med, v_lgr, v_gmat, v_gup, v_gdown, v_vecs, sem_in, sem_out) = rest[:15], rest[15:]
    rows = med.shape[0] * med.shape[1] // CHUNKS
    per = med.shape[1] // rows
    moves = []
    for k in range(CHUNKS):
        part = (k // per, pl.ds((k % per) * rows, rows))
        moves.append((med.at[part], v_med.at[part], [(v_med.at[part], outs[1].at[part])]))
    moves.append((gup, v_gup, [(v_gup, outs[7])]))
    moves.append((gdown, v_gdown, [(v_gdown, outs[8])]))
    moves.append((lat, v_lat, [(v_lat, outs[0])]))
    moves.append((lgr, v_lgr, [(v_lgr, outs[2])]))
    moves.append((gmat, v_gmat, [(v_gmat.at[k], outs[3 + k]) for k in range(4)]))
    moves.append((vecs, v_vecs, [(v_vecs.at[k : k + 1], outs[9 + k]) for k in range(6)]))
    first = [pltpu.make_async_copy(a, b, sem_in.at[k]) for k, (a, b, _) in enumerate(moves)]
    for copy in first:
        copy.start()
    second = []
    for copy, (_, _, then) in zip(first, moves):
        copy.wait()
        for a, b in then:
            second.append(pltpu.make_async_copy(a, b, sem_out.at[len(second)]))
            second[-1].start()
    for copy in second:
        copy.wait()


def fused(media, latents, cotangent, image_counts, wq, wk, wv, wo, up, down, *gains):
    anyspace = pl.BlockSpec(memory_space=pl.ANY)
    vmem = pl.BlockSpec(memory_space=pltpu.VMEM)
    smem = pl.BlockSpec(memory_space=pltpu.SMEM)
    shape = jax.ShapeDtypeStruct
    outs = pl.pallas_call(
        layer_kernel,
        out_shape=[
            shape(latents.shape, BF16),
            shape(media.shape, BF16),
            shape(latents.shape, BF16),
            shape((4, 128, 128), F32),
            shape(up.shape, F32),
            shape(down.shape, F32),
            shape((8, 128), F32),
        ],
        in_specs=[smem] + [anyspace] * 9 + [vmem] * 6,
        out_specs=[anyspace] * 7,
        scratch_shapes=[
            pltpu.SemaphoreType.DMA((SEMS,)),
            pltpu.SemaphoreType.DMA((SEMS,)),
            pltpu.SemaphoreType.DMA((32,)),
        ]
        + [pltpu.VMEM(size, kind) for _, size, kind in SCRATCH],
        compiler_params=pltpu.CompilerParams(
            collective_id=0, has_side_effects=True, vmem_limit_bytes=60 * 2**20
        ),
        cost_estimate=pl.CostEstimate(
            flops=14 * 10**9, bytes_accessed=20 * 10**6, transcendentals=10**6
        ),
    )(
        image_counts,
        media,
        latents,
        cotangent,
        wq,
        wk,
        wv,
        wo,
        up,
        down,
        *[v.reshape(1, 128) for v in gains],
    )
    outs = pl.pallas_call(
        hand_out,
        out_shape=[shape(v.shape, v.dtype) for v in outs[:3]]
        + [shape(v.shape, F32) for v in (wq, wk, wv, wo, up, down)]
        + [shape((1, 128), F32)] * 6,
        in_specs=[anyspace] * 7,
        out_specs=[anyspace] * 15,
        scratch_shapes=[pltpu.VMEM(v.shape, v.dtype) for v in outs]
        + [pltpu.SemaphoreType.DMA((CHUNKS + 6,)), pltpu.SemaphoreType.DMA((CHUNKS + 14,))],
        compiler_params=pltpu.CompilerParams(vmem_limit_bytes=60 * 2**20),
    )(*outs)
    return tuple(outs[:9]) + tuple(v.reshape(128) for v in outs[9:])


def fits(mesh):
    return mesh.shape["dp"] == 8 and mesh.shape["mp"] == 4


MB = 2
SB = 1


def layer_norm(inputs, gain, bias):
    center = inputs - jnp.mean(inputs, axis=-1, keepdims=True)
    spread = jnp.mean(center * center, axis=-1, keepdims=True)
    return center * lax.rsqrt(spread + 1e-05) * gain + bias


def gelu_exact(inputs):
    return jax.nn.gelu(inputs, approximate=False)


def add_tuples(left, right):
    return tuple((first + second for first, second in zip(left, right)))


def micro_step(gathered, media, latents, cotangent, counts):
    (
        query_matrix,
        k_weight,
        v_weight,
        output_projection_weight,
        up_projection_weight,
        down_projection_weight,
        media_gain,
        media_bias,
        latent_gain,
        latent_bias,
        ff_gain,
        ff_bias,
    ) = gathered
    samples = media.shape[0]
    media_len = media.shape[1]
    latent_len = latents.shape[1]
    keys_len = media_len + latent_len
    span = query_matrix.shape[1]
    local_heads = span // HEAD
    wide_rows = jnp.float32
    key_matrix = jnp.concatenate([k_weight, v_weight], axis=1)
    latent_full = latents.astype(wide_rows)
    latent_norm32, latent_pull = jax.vjp(
        layer_norm, latent_full, latent_gain.astype(wide_rows), latent_bias.astype(wide_rows)
    )
    latent_normed_rows = latent_norm32.astype(jnp.bfloat16)
    media_norm32, media_pull = jax.vjp(
        layer_norm,
        media.astype(wide_rows),
        media_gain.astype(wide_rows),
        media_bias.astype(wide_rows),
    )
    media_norm = media_norm32.astype(jnp.bfloat16)
    media_kv = jnp.einsum(
        "snd,dh->snh", media_norm, key_matrix, preferred_element_type=wide_rows
    ).astype(jnp.bfloat16)
    query_rows = jnp.einsum(
        "gjm,mu->gju", latent_normed_rows, query_matrix, preferred_element_type=wide_rows
    ).astype(jnp.bfloat16)
    latent_kv = jnp.einsum(
        "gjm,mu->gju", latent_normed_rows, key_matrix, preferred_element_type=wide_rows
    ).astype(jnp.bfloat16)
    both_kv = jnp.concatenate([media_kv, latent_kv], axis=1)
    head_queries = query_rows.reshape(samples, latent_len, local_heads, HEAD)
    head_keys = both_kv[:, :, :span].reshape(samples, keys_len, local_heads, HEAD)
    head_values = both_kv[:, :, span:].reshape(samples, keys_len, local_heads, HEAD)
    places = jnp.arange(keys_len)
    valid = jnp.logical_or(places[None, :] // PATCH < counts[:, None], places[None, :] >= media_len)

    def scores_of():
        raw = (
            jnp.einsum("slhe,snhe->shln", head_queries, head_keys, preferred_element_type=wide_rows)
            * 0.125
        )
        return jnp.where(valid[:, None, None, :], raw, -1e30)

    scores = scores_of()
    row_max = jnp.max(scores, axis=-1, keepdims=True)
    logsum = row_max + jnp.log(jnp.sum(jnp.exp(scores - row_max), axis=-1, keepdims=True))
    attend_low = jnp.exp(scores - logsum).astype(jnp.bfloat16)
    mixed_rows = jnp.einsum(
        "shln,snhe->slhe", attend_low, head_values, preferred_element_type=wide_rows
    )
    mixed_rows = mixed_rows.reshape(samples, latent_len, span).astype(jnp.bfloat16)
    attn_out = lax.psum(
        jnp.einsum(
            "rwa,ax->rwx", mixed_rows, output_projection_weight, preferred_element_type=wide_rows
        ),
        "mp",
    )
    middle = latent_full + attn_out
    hidden32, ff_pull = jax.vjp(
        layer_norm, middle, ff_gain.astype(wide_rows), ff_bias.astype(wide_rows)
    )
    hidden_rows = hidden32.astype(jnp.bfloat16)
    inner_rows = jnp.einsum(
        "qab,bo->qao", hidden_rows, up_projection_weight, preferred_element_type=wide_rows
    )
    active32, gelu_pull = jax.vjp(gelu_exact, inner_rows)
    active_units = active32.astype(jnp.bfloat16)
    ff_out = lax.psum(
        jnp.einsum(
            "pye,ej->pyj", active_units, down_projection_weight, preferred_element_type=wide_rows
        ).astype(jnp.bfloat16),
        "mp",
    ).astype(jnp.float32)
    result = (middle + ff_out).astype(jnp.bfloat16)
    down_projection_grad = jnp.einsum(
        "kje,kju->eu", active_units, cotangent, preferred_element_type=wide_rows
    )
    active_units_grad = jnp.einsum(
        "jvw,ow->jvo", cotangent, down_projection_weight, preferred_element_type=wide_rows
    )
    (inner_grad,) = gelu_pull(active_units_grad)
    inner_rows_reduced = inner_grad.astype(jnp.bfloat16)
    up_projection_grad = jnp.einsum(
        "imw,imk->wk", hidden_rows, inner_rows_reduced, preferred_element_type=wide_rows
    )
    hidden_grad = lax.psum(
        jnp.einsum(
            "xvm,nm->xvn",
            inner_rows_reduced,
            up_projection_weight,
            preferred_element_type=wide_rows,
        ).astype(jnp.bfloat16),
        "mp",
    ).astype(jnp.float32)
    middle_part, ff_gain_grad, ff_bias_grad = ff_pull(hidden_grad)
    middle_grad = cotangent.astype(wide_rows) + middle_part
    middle_rows_reduced = middle_grad.astype(jnp.bfloat16)
    output_projection_grad = jnp.einsum(
        "gfb,gfw->bw", mixed_rows, middle_rows_reduced, preferred_element_type=wide_rows
    )
    mixed_grad = jnp.einsum(
        "kzw,nw->kzn",
        middle_rows_reduced,
        output_projection_weight,
        preferred_element_type=wide_rows,
    ).astype(jnp.bfloat16)
    mixed_grad = mixed_grad.reshape(samples, latent_len, local_heads, HEAD)
    attend = jnp.exp(scores_of() - logsum)
    attend_grad = jnp.einsum(
        "slhe,snhe->shln", mixed_grad, head_values, preferred_element_type=wide_rows
    )
    score_grad = attend * (attend_grad - jnp.sum(attend * attend_grad, axis=-1, keepdims=True))
    score_grad = score_grad.astype(jnp.bfloat16)
    query_rows_grad = (
        jnp.einsum("shln,snhe->slhe", score_grad, head_keys, preferred_element_type=wide_rows)
        * 0.125
    )
    query_rows_grad = query_rows_grad.astype(jnp.bfloat16).reshape(samples, latent_len, span)
    key_grad = (
        jnp.einsum("shln,slhe->snhe", score_grad, head_queries, preferred_element_type=wide_rows)
        * 0.125
    )
    key_grad = key_grad.astype(jnp.bfloat16).reshape(samples, keys_len, span)
    value_grad = jnp.einsum(
        "shln,slhe->snhe", attend_low, mixed_grad, preferred_element_type=wide_rows
    )
    value_grad = value_grad.astype(jnp.bfloat16).reshape(samples, keys_len, span)
    kv_grad = jnp.concatenate([key_grad, value_grad], axis=2)
    media_kv_grad = kv_grad[:, :media_len]
    latent_key_value_grad = kv_grad[:, media_len:]
    query_weight_grad = jnp.einsum(
        "cbi,cbu->iu", latent_normed_rows, query_rows_grad, preferred_element_type=wide_rows
    )
    latent_wgrad = jnp.einsum(
        "cbi,cbu->iu", latent_normed_rows, latent_key_value_grad, preferred_element_type=wide_rows
    )
    latent_portion = jnp.einsum(
        "kwt,gt->kwg", query_rows_grad, query_matrix, preferred_element_type=wide_rows
    )
    latent_portion = latent_portion + jnp.einsum(
        "kwt,gt->kwg", latent_key_value_grad, key_matrix, preferred_element_type=wide_rows
    )
    media_part = jnp.einsum(
        "snh,dh->snd", media_kv_grad, key_matrix, preferred_element_type=wide_rows
    )
    media_wgrad = jnp.einsum(
        "snd,snh->dh", media_norm, media_kv_grad, preferred_element_type=wide_rows
    )
    kv_weight_grad = media_wgrad + latent_wgrad
    media_sum, latent_sum = (
        lax.psum(media_part.astype(jnp.bfloat16), "mp").astype(jnp.float32),
        lax.psum(latent_portion.astype(jnp.bfloat16), "mp").astype(jnp.float32),
    )
    media_back, media_gain_grad, media_bias_grad = media_pull(media_sum)
    media_out = media_back.astype(jnp.bfloat16)
    latent_back, latent_gain_grad, latent_bias_grad = latent_pull(latent_sum)
    latent_grad = middle_grad + latent_back
    grads = (
        query_weight_grad,
        kv_weight_grad[:, :span],
        kv_weight_grad[:, span:],
        output_projection_grad,
        up_projection_grad,
        down_projection_grad,
        media_gain_grad,
        media_bias_grad,
        latent_gain_grad,
        latent_bias_grad,
        ff_gain_grad,
        ff_bias_grad,
    )
    return (result, media_out, latent_grad.astype(jnp.bfloat16), grads)


def local(
    media,
    latents,
    cotangent,
    image_counts,
    query_matrix,
    k_weight,
    v_weight,
    output_projection_weight,
    up_projection_weight,
    down_projection_weight,
    media_gain,
    media_bias,
    latent_gain,
    latent_bias,
    ff_gain,
    ff_bias,
):
    results = []
    media_grads = []
    latent_grads = []
    totals = ()
    for micro_index in range(MB):
        gathered = (
            lax.all_gather(query_matrix, "dp", axis=0, tiled=True),
            lax.all_gather(k_weight, "dp", axis=0, tiled=True),
            lax.all_gather(v_weight, "dp", axis=0, tiled=True),
            lax.all_gather(output_projection_weight, "dp", axis=1, tiled=True),
            lax.all_gather(up_projection_weight, "dp", axis=0, tiled=True),
            lax.all_gather(down_projection_weight, "dp", axis=1, tiled=True),
            lax.all_gather(media_gain, "dp", axis=0, tiled=True),
            lax.all_gather(media_bias, "dp", axis=0, tiled=True),
            lax.all_gather(latent_gain, "dp", axis=0, tiled=True),
            lax.all_gather(latent_bias, "dp", axis=0, tiled=True),
            lax.all_gather(ff_gain, "dp", axis=0, tiled=True),
            lax.all_gather(ff_bias, "dp", axis=0, tiled=True),
        )
        lower = micro_index * SB
        upper = lower + SB
        result, media_back, latent_back, grads = micro_step(
            gathered,
            media[lower:upper],
            latents[lower:upper],
            cotangent[lower:upper],
            image_counts[lower:upper],
        )
        grads = (
            lax.psum_scatter(grads[0], "dp", scatter_dimension=0, tiled=True),
            lax.psum_scatter(grads[1], "dp", scatter_dimension=0, tiled=True),
            lax.psum_scatter(grads[2], "dp", scatter_dimension=0, tiled=True),
            lax.psum_scatter(grads[3], "dp", scatter_dimension=1, tiled=True),
            lax.psum_scatter(grads[4], "dp", scatter_dimension=0, tiled=True),
            lax.psum_scatter(grads[5], "dp", scatter_dimension=1, tiled=True),
            lax.psum_scatter(grads[6], "dp", scatter_dimension=0, tiled=True),
            lax.psum_scatter(grads[7], "dp", scatter_dimension=0, tiled=True),
            lax.psum_scatter(grads[8], "dp", scatter_dimension=0, tiled=True),
            lax.psum_scatter(grads[9], "dp", scatter_dimension=0, tiled=True),
            lax.psum_scatter(grads[10], "dp", scatter_dimension=0, tiled=True),
            lax.psum_scatter(grads[11], "dp", scatter_dimension=0, tiled=True),
        )
        totals = grads if micro_index == 0 else add_tuples(totals, grads)
        results.append(result)
        media_grads.append(media_back)
        latent_grads.append(latent_back)
    return (
        jnp.concatenate(results, axis=0),
        jnp.concatenate(media_grads, axis=0),
        jnp.concatenate(latent_grads, axis=0),
        totals[0],
        totals[1],
        totals[2],
        totals[3],
        totals[4],
        totals[5],
        totals[6],
        totals[7],
        totals[8],
        totals[9],
        totals[10],
        totals[11],
    )


def solution(mesh):
    placed = (
        P("dp", None, None),
        P("dp", None, None),
        P("dp", None, None),
        P("dp"),
        P("dp", "mp"),
        P("dp", "mp"),
        P("dp", "mp"),
        P("mp", "dp"),
        P("dp", "mp"),
        P("mp", "dp"),
        P("dp"),
        P("dp"),
        P("dp"),
        P("dp"),
        P("dp"),
        P("dp"),
    )
    return jax.shard_map(
        fused if fits(mesh) else local,
        mesh=mesh,
        in_specs=placed,
        out_specs=(
            P("dp", None, None),
            P("dp", None, None),
            P("dp", None, None),
            P("dp", "mp"),
            P("dp", "mp"),
            P("dp", "mp"),
            P("mp", "dp"),
            P("dp", "mp"),
            P("mp", "dp"),
            P("dp"),
            P("dp"),
            P("dp"),
            P("dp"),
            P("dp"),
            P("dp"),
        ),
        check_vma=False,
    )
```

```python
import functools

import jax
import jax.numpy as jnp
from jax import lax
from jax.experimental import pallas as pl
from jax.experimental.pallas import tpu as pltpu
from jax.sharding import PartitionSpec as P

HEAD = 64
PATCH = 256
EPS = 1e-05
F32 = jnp.float32
BF16 = jnp.bfloat16
MESH = pl.DeviceIdType.MESH
NN = (((1,), (0,)), ((), ()))
NT = (((1,), (1,)), ((), ()))
TN = (((0,), (0,)), ((), ()))
LIMIT = 54
SEMS = 68


def dot(a, b, dims):
    return lax.dot_general(a, b, dims, preferred_element_type=F32)


def at(start, size):
    return pl.ds(pl.multiple_of(start, size), size)


class Wire:
    def __init__(self, send_sem, recv_sem):
        self.send_sem, self.recv_sem = send_sem, recv_sem
        self.used, self.sent = 0, []

    def take(self, count=1):
        first = self.used
        self.used += count
        assert self.used <= SEMS
        return first

    def make(self, slot, src, dst, dev):
        return pltpu.make_async_remote_copy(
            src_ref=src,
            dst_ref=dst,
            send_sem=self.send_sem.at[slot],
            recv_sem=self.recv_sem.at[slot],
            device_id=dev,
            device_id_type=MESH,
        )

    def send(self, src, dst, dev):
        copy = self.make(self.take(), src, dst, dev)
        copy.start()
        self.sent.append(copy)
        return copy

    def send_all(self, parts, whole):
        slot = self.take()
        for src, dst, dev in parts:
            self.make(slot, src, dst, dev).start()
        copy = self.make(slot, whole, whole, parts[0][2])
        self.sent.append(copy)
        return copy

    def drain(self):
        for copy in self.sent:
            copy.wait_send()


def norm_back(z, mean, rstd, gain, dy):
    zhat = (z - mean) * rstd
    t = dy * gain
    mt = jnp.mean(t, axis=-1, keepdims=True)
    mz = jnp.mean(t * zhat, axis=-1, keepdims=True)
    return rstd * (t - mt - zhat * mz), zhat


def layer_kernel(
    counts,
    media,
    latents,
    cot,
    wq,
    wk,
    wv,
    wo,
    up,
    down,
    mg,
    mb,
    lg,
    lb,
    fg,
    fb,
    lat_out,
    media_out,
    lgrad_out,
    gmat,
    gup,
    gdown,
    vecs,
    send_sem,
    recv_sem,
    local_sem,
    prm_own,
    prm,
    vec,
    xin,
    lat,
    kin,
    mu,
    rs,
    w4,
    wo_own,
    upb,
    dnb,
    kb,
    vb,
    qb,
    att,
    attl,
    mix,
    mid,
    hid,
    cota,
    act,
    ig,
    hgs,
    hgr,
    hgx,
    fos,
    fxr,
    fos2,
    fors,
    fox,
    gus,
    gur,
    guo,
    gu,
    gua,
    gds,
    gdr,
    gdo,
    gd,
    gda,
    midg,
    lowb,
    mgr,
    kg,
    vg,
    qg,
    cgs,
    cgr,
    gown,
    g1,
    yr,
    g2,
    zr,
    zs,
    dxs,
    accg,
    accb,
    wsc,
    vgs,
    vgc,
    vgt,
    vga,
):
    i = lax.axis_index("dp")
    j = lax.axis_index("mp")
    x, c = j // 2, j % 2
    yy, z = i % 2, i // 2
    zlo, zhi = z % 2, z // 2
    r = i % 4

    def peer(k):
        a = 1 - yy if k & 1 else yy
        b = 1 - zlo if k & 2 else zlo
        d = 1 - zhi if k & 4 else zhi
        return d * 4 + b * 2 + a

    jx = j + 2 - 4 * x
    jc = j + 1 - 2 * c
    ox = 1 - x
    oc = 1 - c
    xpart = (i, jx)
    cpart = (i, jc)
    ypart = (peer(1), j)
    wire = Wire(send_sem, recv_sem)

    def w3b(ii, xx, cc):
        return w4.at[xx, ii // 2, ii % 2, :, :, at(cc * 128, 128)]

    out_w, kqv = slice(3, 4), slice(0, 3)

    def w3col(xx, y_, cc, mats=kqv):
        return w4.at[xx, :, y_, mats, :, at(cc * 128, 128)]

    local = []

    def bring(src, dst):
        copy = pltpu.make_async_copy(src, dst, local_sem.at[len(local)])
        copy.start()
        local.append(copy)
        return copy

    bring(wk, w4.at[x, z, yy, 0, :, at(c * 128, 128)])
    bring(wv, w4.at[x, z, yy, 1, :, at(c * 128, 128)])
    bring(wq, w4.at[x, z, yy, 2, :, at(c * 128, 128)])
    bring(wo, wo_own)
    in_lat = bring(latents.at[c], lat)
    in_media = bring(media.at[c], xin)
    in_cot = bring(cot.at[c], cota.at[r])
    in_up = bring(up.at[:, at(r * 256, 256)], upb.at[i, :, at(c * 256, 256)])
    in_dn = bring(down.at[at(r * 256, 256), :], dnb.at[c, :, at(i * 128, 128)])
    for row, ref in enumerate((mg, mb, lg, lb, fg, fb)):
        prm_own[row : row + 1, :] = ref[...].astype(F32)
    prm_own[6:8, :] = jnp.zeros((2, 128), F32)
    prm[i] = prm_own[...]

    barrier = pltpu.get_barrier_semaphore()
    partners = [(peer(k), j) for k in range(1, 8)] + [xpart, cpart]
    partners += [(peer(k), jx) for k in range(1, 4)]
    for dev in partners:
        pl.semaphore_signal(barrier, inc=1, device_id=dev, device_id_type=MESH)

    in_lat.wait()
    lat32 = lat[...].astype(F32)
    lmean = jnp.mean(lat32, axis=-1, keepdims=True)
    lcen = lat32 - lmean
    mu[1280:1344, :] = lmean
    rs[1280:1344, :] = lax.rsqrt(jnp.mean(lcen * lcen, axis=-1, keepdims=True) + EPS)
    in_media.wait()

    def stat(t, carry):
        rows = at(t * 64, 64)
        v = xin[rows, :].astype(F32)
        m = jnp.mean(v, axis=-1, keepdims=True)
        cen = v - m
        mu[rows, :] = m
        rs[rows, :] = lax.rsqrt(jnp.mean(cen * cen, axis=-1, keepdims=True) + EPS)
        return carry

    lax.fori_loop(0, 20, stat, 0, unroll=4)
    pl.semaphore_wait(barrier, len(partners))

    for copy in local[:4]:
        copy.wait()
    w4[x, z, yy, 3, :, at(c * 128, 128)] = wo_own[...].astype(F32).T.astype(BF16)
    others = range(1, 8)
    got_prm = wire.send_all([(prm_own, prm.at[i], (peer(k), j)) for k in others], prm.at[0:7])

    def same(view, dev):
        return wire.send(view, view, dev)

    z_near = same(w3b(i, x, c), (peer(2), j))
    z_far = same(w3b(i, x, c), (peer(4), j))
    y3 = [same(w3b(i, x, c), ypart)]
    got_prm.wait_recv()
    for ii in range(8):
        vec[:, ii * 128 : (ii + 1) * 128] = prm[ii]

    def media_norm(lo, hi):
        def strip(t, carry):
            rows = at(t * 64, 64)
            v = (xin[rows, :].astype(F32) - mu[rows, :]) * rs[rows, :]
            kin[rows, :] = (v * vec[0:1, :] + vec[1:2, :]).astype(BF16)
            return carry

        lax.fori_loop(lo, hi, strip, 0, unroll=2)

    kin[1280:1344, :] = (
        (lat[...].astype(F32) - mu[1280:1344, :]) * rs[1280:1344, :] * vec[2:3, :] + vec[3:4, :]
    ).astype(BF16)
    media_norm(0, 10)
    z_far.wait_recv()
    z_relay = same(w3b(peer(4), x, c), (peer(2), j))
    y3.append(same(w3b(peer(4), x, c), ypart))
    z_near.wait_recv()
    y3.append(same(w3b(peer(2), x, c), ypart))
    z_relay.wait_recv()
    y3.append(same(w3b(peer(6), x, c), ypart))
    everything = slice(0, 4)
    c3 = [same(w3col(x, yy, c, everything), cpart)]
    xo = [same(w3col(x, yy, c, out_w), xpart)]
    x3 = [same(w3col(x, yy, c), xpart)]
    def up_part(k):
        return up.at[:, at(peer(k) % 4 * 256, 256)], upb.at[i, :, at(c * 256, 256)], (peer(k), j)

    def down_part(k):
        return down.at[at(peer(k) % 4 * 256, 256), :], dnb.at[c, :, at(i * 128, 128)], (peer(k), j)

    near, crossing = (4, 6, 2), (5, 7, 3, 1)
    ups = [wire.send_all([up_part(k) for k in near], upb.at[0:3, :, 0:256])]
    dns = [wire.send_all([down_part(k) for k in near], dnb.at[0, :, 0:384])]
    ups.append(wire.send_all([up_part(k) for k in crossing], upb.at[0:4, :, 0:256]))
    dns.append(wire.send_all([down_part(k) for k in crossing], dnb.at[0, :, 0:512]))
    in_cot.wait()
    cots = wire.send_all(
        [(cota.at[r], cota.at[r], (peer(k), j)) for k in (1, 2, 3)], cota.at[0:3]
    )

    media_norm(10, 20)
    for copy in y3:
        copy.wait_recv()
    c3.append(same(w3col(x, 1 - yy, c, everything), cpart))
    xo.append(same(w3col(x, 1 - yy, c, out_w), xpart))
    for copy in c3:
        copy.wait_recv()

    count = counts[c]
    head_of_lane = lax.broadcasted_iota(jnp.int32, (256, 256), 1) // HEAD
    head_of_row = lax.broadcasted_iota(jnp.int32, (256, 256), 0) // HEAD
    own_head = head_of_lane == head_of_row
    lane64 = lax.broadcasted_iota(jnp.int32, (64, 256), 1) // HEAD

    def spread(v):
        v = v.astype(F32)
        return jnp.where(own_head, jnp.concatenate([v, v, v, v], axis=0), 0.0).astype(BF16)

    def gather_heads(v):
        out = jnp.zeros((64, 256), F32)
        for h in range(4):
            out = jnp.where(lane64 == h, v[h * 64 : (h + 1) * 64, :], out)
        return out

    def weight(g, m):
        return w4[g, :, :, m].reshape(1024, 256)

    def attention(g, mixing=True):
        a = kin[...]
        kb[g] = dot(a, weight(g, 0), NN).astype(BF16)
        vb[g] = dot(a, weight(g, 1), NN).astype(BF16)
        qb[g] = dot(kin[1280:1344, :], weight(g, 2), NN).astype(BF16)
        s = dot(kb[g], spread(qb[g]), NT) * 0.125
        key = lax.broadcasted_iota(jnp.int32, (1344, 256), 0)
        s = jnp.where(jnp.logical_or(key < count * PATCH, key >= 1280), s, -1e30)
        att[g] = s
        top = jnp.max(s, axis=0, keepdims=True)
        e = jnp.exp(att[g] - top)
        att[g] = e
        scale = 1.0 / jnp.sum(e, axis=0, keepdims=True)
        p = att[g] * scale
        att[g] = p
        attl[g] = p.astype(BF16)
        if mixing:
            mixed = dot(attl[g], vb[g], TN)
            mix[g] = gather_heads(mixed).astype(BF16)

    attention(x)
    mx = same(mix.at[x], xpart)
    x3.append(same(w3col(x, 1 - yy, c), xpart))
    cob = []
    for copy, y_ in zip(xo, (yy, 1 - yy)):
        copy.wait_recv()
        cob.append(same(w3col(ox, y_, c, out_w), cpart))
    mx.wait_recv()
    for copy in cob:
        copy.wait_recv()

    middle = lat[...].astype(F32) + (dot(mix[0], weight(0, 3), NT) + dot(mix[1], weight(1, 3), NT))
    mid[...] = middle
    fmean = jnp.mean(middle, axis=-1, keepdims=True)
    fcen = middle - fmean
    frs = lax.rsqrt(jnp.mean(fcen * fcen, axis=-1, keepdims=True) + EPS)
    hid[r] = (fcen * frs * vec[4:5, :] + vec[5:6, :]).astype(BF16)
    hids = wire.send_all([(hid.at[r], hid.at[r], (peer(k), j)) for k in (3, 2, 1)], hid.at[0:3])

    in_up.wait()
    in_dn.wait()
    for copy in ups:
        copy.wait_recv()
    cup = same(upb.at[:, :, at(c * 256, 256)], cpart)
    for copy in dns:
        copy.wait_recv()
    cdn = same(dnb.at[c], cpart)
    hids.wait_recv()
    cots.wait_recv()
    cup.wait_recv()
    cdn.wait_recv()

    hid_all = hid[...].reshape(256, 1024)
    cot_all = cota[...].reshape(256, 1024)
    up_all = upb[...].reshape(1024, 512)
    dn_all = dnb[...].reshape(512, 1024)
    inner = dot(hid_all, up_all, NN)
    phi = 0.5 * (1.0 + lax.erf(inner * (0.5**0.5)))
    act[...] = (inner * phi).astype(BF16)
    agrad = dot(cot_all, dn_all, NT)
    dens = jnp.exp(inner * inner * -0.5) * 0.3989422804014327
    ig[...] = (agrad * (phi + inner * dens)).astype(BF16)
    hgs[...] = dot(ig[...], up_all, NT).astype(BF16).reshape(4, 64, 1024)

    slot = x * 4 + r
    parts = []
    for k in (7, 6, 5, 3, 2, 1, 4):
        tx, tj = (ox, jx) if k >= 4 else (x, j)
        src = hgs.at[peer(k % 4) % 4, at(tx * 32, 32), :]
        parts.append((src, hgr.at[slot], (peer(k % 4), tj)))
    hg_in = wire.send_all(parts, hgr.at[0:7])
    hgr[slot] = hgs[r, at(x * 32, 32), :]

    gus[...] = dot(hid_all, ig[:, at(oc * 256, 256)], TN).astype(BF16).reshape(8, 128, 256)
    gu_in = wire.send(gus, gur, cpart)
    gds[...] = dot(act[:, at(oc * 256, 256)], cot_all, TN).astype(BF16)
    gd_in = wire.send(gds, gdr, cpart)
    guo[...] = dot(hid_all, ig[:, at(c * 256, 256)], TN).reshape(8, 128, 256)
    gdo[...] = dot(act[:, at(c * 256, 256)], cot_all, TN)

    def sum_of(ref, n):
        total = ref[0].astype(F32)
        for s in range(1, n):
            total = total + ref[s].astype(F32)
        return total

    fos[...] = dot(act[...], dn_all, NN).astype(BF16).reshape(4, 64, 1024)

    def up_back(ks):
        return wire.send_all([(gu.at[peer(k)], gua.at[i], (peer(k), j)) for k in ks], gua.at[0 : len(ks)])

    def down_back(ks):
        return wire.send_all(
            [(gd.at[:, at(peer(k) * 128, 128)], gda.at[i], (peer(k), j)) for k in ks],
            gda.at[0 : len(ks)],
        )

    gu_in.wait_recv()
    gu[...] = (guo[...] + gur[...].astype(F32)).astype(BF16)
    gua[i] = gu[i]
    gu_out = [up_back(near), up_back(crossing)]
    gd_in.wait_recv()
    gd[...] = (gdo[...] + gdr[...].astype(F32)).astype(BF16)
    gda[i] = gd[:, at(i * 128, 128)]
    gd_out = [down_back(near)]
    c3b = []
    for copy, y_ in zip(x3, (yy, 1 - yy)):
        copy.wait_recv()
        c3b.append(same(w3col(ox, y_, c), cpart))
    for copy in c3b:
        copy.wait_recv()
    attention(ox, False)

    hg_in.wait_recv()
    hgx[x] = sum_of(hgr, 8).astype(BF16)
    hgx_in = same(hgx.at[x], xpart)
    fx_in = wire.send(fos.at[:, at(ox * 32, 32), :], fxr, xpart)
    hgx_in.wait_recv()
    dy = hgx[...].reshape(64, 1024).astype(F32)
    middle = mid[...]
    fmean = jnp.mean(middle, axis=-1, keepdims=True)
    fcen = middle - fmean
    frs = lax.rsqrt(jnp.mean(fcen * fcen, axis=-1, keepdims=True) + EPS)
    dz, zhat = norm_back(middle, fmean, frs, vec[4:5, :], dy)

    def put_vec(k, v):
        for ii in range(8):
            vgs[ii, k : k + 1, :] = v[:, ii * 128 : (ii + 1) * 128]

    put_vec(4, jnp.sum(dy * zhat, axis=0, keepdims=True))
    put_vec(5, jnp.sum(dy, axis=0, keepdims=True))
    middle_grad = cota[r].astype(F32) + dz
    midg[...] = middle_grad
    low = middle_grad.astype(BF16)
    for g in (0, 1):
        mgr[g] = dot(low, weight(g, 3), NN).astype(BF16)
    lowb[...] = low

    def back_values(g):
        m4 = spread(mgr[g])

        vg[g] = dot(attl[g], m4, NN).astype(BF16)
        pa = att[g] * dot(vb[g], m4, NT)
        dxs[:, 0:256] = pa
        return jnp.sum(pa, axis=0, keepdims=True)

    def back_keys(g, delta):
        q4 = spread(qb[g])

        sg = (dxs[:, 0:256] - att[g] * delta).astype(BF16)
        attl[g] = sg
        kg[g] = (dot(sg, q4, NN) * 0.125).astype(BF16)
        total = dot(attl[g], kb[g], TN)
        qg[g] = (gather_heads(total) * 0.125).astype(BF16)

    def split(m, wide):
        wsc[...] = wide
        mine, other = wsc[at(c * 128, 128), :], wsc[at(oc * 128, 128), :]
        for ii in range(8):
            cols = slice(ii * 128, (ii + 1) * 128)
            gown[ii // 2, ii % 2, m] = mine[:, cols]
            cgs[ii // 2, ii % 2, m] = other[:, cols].astype(BF16)

    def one(ref, p):
        return ref.at[:, :, p]

    def chip_sum(p):
        one(g1, p)[...] = (one(gown, p)[...] + one(cgr, p)[...].astype(F32)).astype(BF16)
        return wire.send(g1.at[:, 1 - yy, p], yr.at[:, p], ypart)

    def to_core(p):
        return wire.send(one(cgs, p), one(cgr, p), cpart)

    delta = back_values(x)
    split(0, dot(vg[x], kin[...], TN))
    cg_in = [to_core(0)]
    split(1, dot(mix[x], lowb[...], TN))
    cg_in.append(to_core(1))
    back_keys(x, delta)
    y_in = []

    def to_y(p):
        cg_in[p].wait_recv()
        y_in.append(chip_sum(p))

    to_y(0)
    split(2, dot(kg[x], kin[...], TN))
    cg_in.append(to_core(2))
    to_y(1)
    split(3, dot(qg[x], kin[1280:1344, :], TN))
    cg_in.append(to_core(3))
    to_y(2)
    to_y(3)
    fx_in.wait_recv()
    fos2[...] = (fos[:, at(x * 32, 32), :].astype(F32) + fxr[...].astype(F32)).astype(BF16)
    fors[r] = fos2[r]
    fo_in = wire.send_all(
        [(fos2.at[peer(k) % 4], fors.at[r], (peer(k), j)) for k in (3, 2, 1)], fors.at[0:3]
    )
    gd_out.append(down_back(crossing))
    back_keys(ox, back_values(ox))

    def dx_tile(rows):
        return (
            dot(kg[0, rows, :], weight(0, 0), NT)
            + dot(kg[1, rows, :], weight(1, 0), NT)
            + dot(vg[0, rows, :], weight(0, 1), NT)
            + dot(vg[1, rows, :], weight(1, 1), NT)
        )

    accg[...] = jnp.zeros((8, 1024), F32)
    accb[...] = jnp.zeros((8, 1024), F32)
    out_base = wire.take(5)

    def out_copy(t, slot):
        rows = at(t * 256, 256)
        return wire.make(slot, media_out.at[c, rows, :], media_out.at[c, rows, :], cpart)

    def media_back(t, carry):
        dxs[0:256, :] = dx_tile(at(t * 256, 256))

        rows = at(t * 256, 256)
        v = xin[rows, :].astype(F32)
        dy = dxs[0:256, :]
        dz, zhat = norm_back(v, mu[rows, :], rs[rows, :], vec[0:1, :], dy)
        media_out[c, rows, :] = dz.astype(BF16)
        accg[...] += (dy * zhat).reshape(32, 8, 1024).sum(0)
        accb[...] += dy.reshape(32, 8, 1024).sum(0)
        out_copy(t, out_base + t).start()
        return carry

    zn, zf = peer(2) // 2, peer(4) // 2
    zd = peer(6) // 2

    def to_near(p):
        y_in[p].wait_recv()
        g2[:, p] = (g1[:, yy, p].astype(F32) + yr[:, p].astype(F32)).astype(BF16)
        parts = [(g2.at[zn, p], zr.at[0, p], (peer(2), j)), (g2.at[zd, p], zr.at[1, p], (peer(2), j))]
        return wire.send_all(parts, zr.at[0:2, 0])

    def to_far(p):
        n_in[p].wait_recv()
        zs[p] = (g2[zf, p].astype(F32) + zr[1, p].astype(F32)).astype(BF16)
        return wire.send(zs.at[p], zr.at[2, p], (peer(4), j))

    n_in, f_in = [], []
    lax.fori_loop(0, 2, media_back, 0)
    n_in.append(to_near(0))
    lax.fori_loop(2, 4, media_back, 0)
    n_in.append(to_near(1))
    f_in.append(to_far(0))
    lax.fori_loop(4, 5, media_back, 0)
    put_vec(0, jnp.sum(accg[...], axis=0, keepdims=True))
    put_vec(1, jnp.sum(accb[...], axis=0, keepdims=True))
    dxs[0:64, :] = dx_tile(pl.ds(1280, 64))
    lsum = dxs[0:64, :] + dot(qg[0], weight(0, 2), NT) + dot(qg[1], weight(1, 2), NT)
    lat32 = lat[...].astype(F32)
    dz, zhat = norm_back(lat32, mu[1280:1344, :], rs[1280:1344, :], vec[2:3, :], lsum)
    lgrad_out[c] = (midg[...] + dz).astype(BF16)
    lg_in = same(lgrad_out.at[c], cpart)
    put_vec(2, jnp.sum(lsum * zhat, axis=0, keepdims=True))
    put_vec(3, jnp.sum(lsum, axis=0, keepdims=True))
    for ii in range(8):
        vgs[ii, 6:8, :] = jnp.zeros((2, 128), F32)
    vg_in = wire.send(vgs, vgc, cpart)

    n_in.append(to_near(2))
    f_in.append(to_far(1))
    fo_in.wait_recv()
    fox[x] = sum_of(fors, 4).astype(BF16)
    fox_in = same(fox.at[x], xpart)
    n_in.append(to_near(3))
    f_in.append(to_far(2))
    vg_in.wait_recv()
    vgt[...] = vgs[...] + vgc[...]
    vga[i] = vgt[i]
    v_in = wire.send_all([(vgt.at[peer(k)], vga.at[i], (peer(k), j)) for k in others], vga.at[0:7])

    fox_in.wait_recv()
    lat_out[c] = (mid[...] + fox[...].reshape(64, 1024).astype(F32)).astype(BF16)
    lo_in = same(lat_out.at[c], cpart)

    f_in.append(to_far(3))
    for copy in gu_out:
        copy.wait_recv()
    for q in range(4):
        gup[:, q * 256 : (q + 1) * 256] = gua[q].astype(F32) + gua[4 + q].astype(F32)
    for copy in gd_out:
        copy.wait_recv()
    for q in range(4):
        gdown[q * 256 : (q + 1) * 256, :] = gda[q].astype(F32) + gda[4 + q].astype(F32)

    for copy in f_in:
        copy.wait_recv()
    last = g2[z].astype(F32) + zr[0].astype(F32) + zr[2].astype(F32)
    gmat[0] = last[3].T
    gmat[1] = last[2].T
    gmat[2] = last[0].T
    gmat[3] = last[1]
    v_in.wait_recv()
    vecs[...] = sum_of(vga, 8)

    for t in range(5):
        out = out_copy(t, out_base + t)
        out.wait_send()
        out.wait_recv()
    lg_in.wait_recv()
    lo_in.wait_recv()
    wire.drain()


SCRATCH = (
    ("prm_own", (8, 128), F32),
    ("prm", (8, 8, 128), F32),
    ("vec", (8, 1024), F32),
    ("xin", (1280, 1024), BF16),
    ("lat", (64, 1024), BF16),
    ("kin", (1344, 1024), BF16),
    ("mu", (1344, 1), F32),
    ("rs", (1344, 1), F32),
    ("w4", (2, 4, 2, 4, 128, 256), BF16),
    ("wo_own", (128, 128), BF16),
    ("upb", (8, 128, 512), BF16),
    ("dnb", (2, 256, 1024), BF16),
    ("kb", (2, 1344, 256), BF16),
    ("vb", (2, 1344, 256), BF16),
    ("qb", (2, 64, 256), BF16),
    ("att", (2, 1344, 256), F32),
    ("attl", (2, 1344, 256), BF16),
    ("mix", (2, 64, 256), BF16),
    ("mid", (64, 1024), F32),
    ("hid", (4, 64, 1024), BF16),
    ("cota", (4, 64, 1024), BF16),
    ("act", (256, 512), BF16),
    ("ig", (256, 512), BF16),
    ("hgs", (4, 64, 1024), BF16),
    ("hgr", (8, 32, 1024), BF16),
    ("hgx", (2, 32, 1024), BF16),
    ("fos", (4, 64, 1024), BF16),
    ("fxr", (4, 32, 1024), BF16),
    ("fos2", (4, 32, 1024), BF16),
    ("fors", (4, 32, 1024), BF16),
    ("fox", (2, 32, 1024), BF16),
    ("gus", (8, 128, 256), BF16),
    ("gur", (8, 128, 256), BF16),
    ("guo", (8, 128, 256), F32),
    ("gu", (8, 128, 256), BF16),
    ("gua", (8, 128, 256), BF16),
    ("gds", (256, 1024), BF16),
    ("gdr", (256, 1024), BF16),
    ("gdo", (256, 1024), F32),
    ("gd", (256, 1024), BF16),
    ("gda", (8, 256, 128), BF16),
    ("midg", (64, 1024), F32),
    ("lowb", (64, 1024), BF16),
    ("mgr", (2, 64, 256), BF16),
    ("kg", (2, 1344, 256), BF16),
    ("vg", (2, 1344, 256), BF16),
    ("qg", (2, 64, 256), BF16),
    ("cgs", (4, 2, 4, 128, 128), BF16),
    ("cgr", (4, 2, 4, 128, 128), BF16),
    ("gown", (4, 2, 4, 128, 128), F32),
    ("g1", (4, 2, 4, 128, 128), BF16),
    ("yr", (4, 4, 128, 128), BF16),
    ("g2", (4, 4, 128, 128), BF16),
    ("zr", (3, 4, 128, 128), BF16),
    ("zs", (4, 128, 128), BF16),
    ("dxs", (1344, 1024), F32),
    ("accg", (8, 1024), F32),
    ("accb", (8, 1024), F32),
    ("wsc", (256, 1024), F32),
    ("vgs", (8, 8, 128), F32),
    ("vgc", (8, 8, 128), F32),
    ("vgt", (8, 8, 128), F32),
    ("vga", (8, 8, 128), F32),
)


def hand_out(lat, med, lgr, gmat, gup, gdown, vecs, *rest):
    outs, sem = rest[:15], rest[15]
    moves = [(med, outs[1]), (gup, outs[7]), (gdown, outs[8]), (lat, outs[0]), (lgr, outs[2])]
    moves += [(gmat.at[k], outs[3 + k]) for k in range(4)]
    moves += [(vecs.at[k : k + 1], outs[9 + k]) for k in range(6)]
    copies = [pltpu.make_async_copy(a, b, sem.at[k]) for k, (a, b) in enumerate(moves)]
    for copy in copies:
        copy.start()
    for copy in copies:
        copy.wait()


def fused(media, latents, cotangent, image_counts, wq, wk, wv, wo, up, down, *gains):
    anyspace = pl.BlockSpec(memory_space=pl.ANY)
    vmem = pl.BlockSpec(memory_space=pltpu.VMEM)
    smem = pl.BlockSpec(memory_space=pltpu.SMEM)
    shape = jax.ShapeDtypeStruct
    outs = pl.pallas_call(
        layer_kernel,
        out_shape=[
            pltpu.VMEM(latents.shape, BF16),
            pltpu.VMEM(media.shape, BF16),
            pltpu.VMEM(latents.shape, BF16),
            pltpu.VMEM((4, 128, 128), F32),
            pltpu.VMEM(up.shape, F32),
            pltpu.VMEM(down.shape, F32),
            pltpu.VMEM((8, 128), F32),
        ],
        in_specs=[smem] + [anyspace] * 9 + [vmem] * 6,
        out_specs=[vmem] * 7,
        scratch_shapes=[
            pltpu.SemaphoreType.DMA((SEMS,)),
            pltpu.SemaphoreType.DMA((SEMS,)),
            pltpu.SemaphoreType.DMA((9,)),
        ]
        + [pltpu.VMEM(size, kind) for _, size, kind in SCRATCH],
        compiler_params=pltpu.CompilerParams(
            collective_id=0, has_side_effects=True, vmem_limit_bytes=LIMIT * 2**20
        ),
        cost_estimate=pl.CostEstimate(
            flops=14 * 10**9, bytes_accessed=20 * 10**6, transcendentals=10**6
        ),
    )(
        image_counts,
        media,
        latents,
        cotangent,
        wq,
        wk,
        wv,
        wo,
        up,
        down,
        *[v.reshape(1, 128) for v in gains],
    )
    outs = pl.pallas_call(
        hand_out,
        out_shape=[shape(v.shape, BF16) for v in (latents, media, latents)]
        + [shape(v.shape, F32) for v in (wq, wk, wv, wo, up, down)]
        + [shape((1, 128), F32)] * 6,
        in_specs=[vmem] * 7,
        out_specs=[anyspace] * 15,
        scratch_shapes=[pltpu.SemaphoreType.DMA((15,))],
        compiler_params=pltpu.CompilerParams(vmem_limit_bytes=4 * 2**20),
    )(*[pltpu.with_memory_space_constraint(v, pltpu.VMEM) for v in outs])
    return tuple(outs[:9]) + tuple(v.reshape(128) for v in outs[9:])


def fits(mesh):
    return mesh.shape["dp"] == 8 and mesh.shape["mp"] == 4


MB = 2
SB = 1


def layer_norm(inputs, gain, bias):
    center = inputs - jnp.mean(inputs, axis=-1, keepdims=True)
    spread = jnp.mean(center * center, axis=-1, keepdims=True)
    return center * lax.rsqrt(spread + 1e-05) * gain + bias


def gelu_exact(inputs):
    return jax.nn.gelu(inputs, approximate=False)


def add_tuples(left, right):
    return tuple((first + second for first, second in zip(left, right)))


def micro_step(gathered, media, latents, cotangent, counts):
    (
        query_matrix,
        k_weight,
        v_weight,
        output_projection_weight,
        up_projection_weight,
        down_projection_weight,
        media_gain,
        media_bias,
        latent_gain,
        latent_bias,
        ff_gain,
        ff_bias,
    ) = gathered
    samples = media.shape[0]
    media_len = media.shape[1]
    latent_len = latents.shape[1]
    keys_len = media_len + latent_len
    span = query_matrix.shape[1]
    local_heads = span // HEAD
    wide_rows = jnp.float32
    key_matrix = jnp.concatenate([k_weight, v_weight], axis=1)
    latent_full = latents.astype(wide_rows)
    latent_norm32, latent_pull = jax.vjp(
        layer_norm, latent_full, latent_gain.astype(wide_rows), latent_bias.astype(wide_rows)
    )
    latent_normed_rows = latent_norm32.astype(jnp.bfloat16)
    media_norm32, media_pull = jax.vjp(
        layer_norm,
        media.astype(wide_rows),
        media_gain.astype(wide_rows),
        media_bias.astype(wide_rows),
    )
    media_norm = media_norm32.astype(jnp.bfloat16)
    media_kv = jnp.einsum(
        "snd,dh->snh", media_norm, key_matrix, preferred_element_type=wide_rows
    ).astype(jnp.bfloat16)
    query_rows = jnp.einsum(
        "gjm,mu->gju", latent_normed_rows, query_matrix, preferred_element_type=wide_rows
    ).astype(jnp.bfloat16)
    latent_kv = jnp.einsum(
        "gjm,mu->gju", latent_normed_rows, key_matrix, preferred_element_type=wide_rows
    ).astype(jnp.bfloat16)
    both_kv = jnp.concatenate([media_kv, latent_kv], axis=1)
    head_queries = query_rows.reshape(samples, latent_len, local_heads, HEAD)
    head_keys = both_kv[:, :, :span].reshape(samples, keys_len, local_heads, HEAD)
    head_values = both_kv[:, :, span:].reshape(samples, keys_len, local_heads, HEAD)
    places = jnp.arange(keys_len)
    valid = jnp.logical_or(places[None, :] // PATCH < counts[:, None], places[None, :] >= media_len)

    def scores_of():
        raw = (
            jnp.einsum("slhe,snhe->shln", head_queries, head_keys, preferred_element_type=wide_rows)
            * 0.125
        )
        return jnp.where(valid[:, None, None, :], raw, -1e30)

    scores = scores_of()
    row_max = jnp.max(scores, axis=-1, keepdims=True)
    logsum = row_max + jnp.log(jnp.sum(jnp.exp(scores - row_max), axis=-1, keepdims=True))
    attend_low = jnp.exp(scores - logsum).astype(jnp.bfloat16)
    mixed_rows = jnp.einsum(
        "shln,snhe->slhe", attend_low, head_values, preferred_element_type=wide_rows
    )
    mixed_rows = mixed_rows.reshape(samples, latent_len, span).astype(jnp.bfloat16)
    attn_out = lax.psum(
        jnp.einsum(
            "rwa,ax->rwx", mixed_rows, output_projection_weight, preferred_element_type=wide_rows
        ),
        "mp",
    )
    middle = latent_full + attn_out
    hidden32, ff_pull = jax.vjp(
        layer_norm, middle, ff_gain.astype(wide_rows), ff_bias.astype(wide_rows)
    )
    hidden_rows = hidden32.astype(jnp.bfloat16)
    inner_rows = jnp.einsum(
        "qab,bo->qao", hidden_rows, up_projection_weight, preferred_element_type=wide_rows
    )
    active32, gelu_pull = jax.vjp(gelu_exact, inner_rows)
    active_units = active32.astype(jnp.bfloat16)
    ff_out = lax.psum(
        jnp.einsum(
            "pye,ej->pyj", active_units, down_projection_weight, preferred_element_type=wide_rows
        ).astype(jnp.bfloat16),
        "mp",
    ).astype(jnp.float32)
    result = (middle + ff_out).astype(jnp.bfloat16)
    down_projection_grad = jnp.einsum(
        "kje,kju->eu", active_units, cotangent, preferred_element_type=wide_rows
    )
    active_units_grad = jnp.einsum(
        "jvw,ow->jvo", cotangent, down_projection_weight, preferred_element_type=wide_rows
    )
    (inner_grad,) = gelu_pull(active_units_grad)
    inner_rows_reduced = inner_grad.astype(jnp.bfloat16)
    up_projection_grad = jnp.einsum(
        "imw,imk->wk", hidden_rows, inner_rows_reduced, preferred_element_type=wide_rows
    )
    hidden_grad = lax.psum(
        jnp.einsum(
            "xvm,nm->xvn",
            inner_rows_reduced,
            up_projection_weight,
            preferred_element_type=wide_rows,
        ).astype(jnp.bfloat16),
        "mp",
    ).astype(jnp.float32)
    middle_part, ff_gain_grad, ff_bias_grad = ff_pull(hidden_grad)
    middle_grad = cotangent.astype(wide_rows) + middle_part
    middle_rows_reduced = middle_grad.astype(jnp.bfloat16)
    output_projection_grad = jnp.einsum(
        "gfb,gfw->bw", mixed_rows, middle_rows_reduced, preferred_element_type=wide_rows
    )
    mixed_grad = jnp.einsum(
        "kzw,nw->kzn",
        middle_rows_reduced,
        output_projection_weight,
        preferred_element_type=wide_rows,
    ).astype(jnp.bfloat16)
    mixed_grad = mixed_grad.reshape(samples, latent_len, local_heads, HEAD)
    attend = jnp.exp(scores_of() - logsum)
    attend_grad = jnp.einsum(
        "slhe,snhe->shln", mixed_grad, head_values, preferred_element_type=wide_rows
    )
    score_grad = attend * (attend_grad - jnp.sum(attend * attend_grad, axis=-1, keepdims=True))
    score_grad = score_grad.astype(jnp.bfloat16)
    query_rows_grad = (
        jnp.einsum("shln,snhe->slhe", score_grad, head_keys, preferred_element_type=wide_rows)
        * 0.125
    )
    query_rows_grad = query_rows_grad.astype(jnp.bfloat16).reshape(samples, latent_len, span)
    key_grad = (
        jnp.einsum("shln,slhe->snhe", score_grad, head_queries, preferred_element_type=wide_rows)
        * 0.125
    )
    key_grad = key_grad.astype(jnp.bfloat16).reshape(samples, keys_len, span)
    value_grad = jnp.einsum(
        "shln,slhe->snhe", attend_low, mixed_grad, preferred_element_type=wide_rows
    )
    value_grad = value_grad.astype(jnp.bfloat16).reshape(samples, keys_len, span)
    kv_grad = jnp.concatenate([key_grad, value_grad], axis=2)
    media_kv_grad = kv_grad[:, :media_len]
    latent_key_value_grad = kv_grad[:, media_len:]
    query_weight_grad = jnp.einsum(
        "cbi,cbu->iu", latent_normed_rows, query_rows_grad, preferred_element_type=wide_rows
    )
    latent_wgrad = jnp.einsum(
        "cbi,cbu->iu", latent_normed_rows, latent_key_value_grad, preferred_element_type=wide_rows
    )
    latent_portion = jnp.einsum(
        "kwt,gt->kwg", query_rows_grad, query_matrix, preferred_element_type=wide_rows
    )
    latent_portion = latent_portion + jnp.einsum(
        "kwt,gt->kwg", latent_key_value_grad, key_matrix, preferred_element_type=wide_rows
    )
    media_part = jnp.einsum(
        "snh,dh->snd", media_kv_grad, key_matrix, preferred_element_type=wide_rows
    )
    media_wgrad = jnp.einsum(
        "snd,snh->dh", media_norm, media_kv_grad, preferred_element_type=wide_rows
    )
    kv_weight_grad = media_wgrad + latent_wgrad
    media_sum, latent_sum = (
        lax.psum(media_part.astype(jnp.bfloat16), "mp").astype(jnp.float32),
        lax.psum(latent_portion.astype(jnp.bfloat16), "mp").astype(jnp.float32),
    )
    media_back, media_gain_grad, media_bias_grad = media_pull(media_sum)
    media_out = media_back.astype(jnp.bfloat16)
    latent_back, latent_gain_grad, latent_bias_grad = latent_pull(latent_sum)
    latent_grad = middle_grad + latent_back
    grads = (
        query_weight_grad,
        kv_weight_grad[:, :span],
        kv_weight_grad[:, span:],
        output_projection_grad,
        up_projection_grad,
        down_projection_grad,
        media_gain_grad,
        media_bias_grad,
        latent_gain_grad,
        latent_bias_grad,
        ff_gain_grad,
        ff_bias_grad,
    )
    return (result, media_out, latent_grad.astype(jnp.bfloat16), grads)


def local(
    media,
    latents,
    cotangent,
    image_counts,
    query_matrix,
    k_weight,
    v_weight,
    output_projection_weight,
    up_projection_weight,
    down_projection_weight,
    media_gain,
    media_bias,
    latent_gain,
    latent_bias,
    ff_gain,
    ff_bias,
):
    results = []
    media_grads = []
    latent_grads = []
    totals = ()
    for micro_index in range(MB):
        gathered = (
            lax.all_gather(query_matrix, "dp", axis=0, tiled=True),
            lax.all_gather(k_weight, "dp", axis=0, tiled=True),
            lax.all_gather(v_weight, "dp", axis=0, tiled=True),
            lax.all_gather(output_projection_weight, "dp", axis=1, tiled=True),
            lax.all_gather(up_projection_weight, "dp", axis=0, tiled=True),
            lax.all_gather(down_projection_weight, "dp", axis=1, tiled=True),
            lax.all_gather(media_gain, "dp", axis=0, tiled=True),
            lax.all_gather(media_bias, "dp", axis=0, tiled=True),
            lax.all_gather(latent_gain, "dp", axis=0, tiled=True),
            lax.all_gather(latent_bias, "dp", axis=0, tiled=True),
            lax.all_gather(ff_gain, "dp", axis=0, tiled=True),
            lax.all_gather(ff_bias, "dp", axis=0, tiled=True),
        )
        lower = micro_index * SB
        upper = lower + SB
        result, media_back, latent_back, grads = micro_step(
            gathered,
            media[lower:upper],
            latents[lower:upper],
            cotangent[lower:upper],
            image_counts[lower:upper],
        )
        grads = (
            lax.psum_scatter(grads[0], "dp", scatter_dimension=0, tiled=True),
            lax.psum_scatter(grads[1], "dp", scatter_dimension=0, tiled=True),
            lax.psum_scatter(grads[2], "dp", scatter_dimension=0, tiled=True),
            lax.psum_scatter(grads[3], "dp", scatter_dimension=1, tiled=True),
            lax.psum_scatter(grads[4], "dp", scatter_dimension=0, tiled=True),
            lax.psum_scatter(grads[5], "dp", scatter_dimension=1, tiled=True),
            lax.psum_scatter(grads[6], "dp", scatter_dimension=0, tiled=True),
            lax.psum_scatter(grads[7], "dp", scatter_dimension=0, tiled=True),
            lax.psum_scatter(grads[8], "dp", scatter_dimension=0, tiled=True),
            lax.psum_scatter(grads[9], "dp", scatter_dimension=0, tiled=True),
            lax.psum_scatter(grads[10], "dp", scatter_dimension=0, tiled=True),
            lax.psum_scatter(grads[11], "dp", scatter_dimension=0, tiled=True),
        )
        totals = grads if micro_index == 0 else add_tuples(totals, grads)
        results.append(result)
        media_grads.append(media_back)
        latent_grads.append(latent_back)
    return (
        jnp.concatenate(results, axis=0),
        jnp.concatenate(media_grads, axis=0),
        jnp.concatenate(latent_grads, axis=0),
        totals[0],
        totals[1],
        totals[2],
        totals[3],
        totals[4],
        totals[5],
        totals[6],
        totals[7],
        totals[8],
        totals[9],
        totals[10],
        totals[11],
    )


def solution(mesh):
    placed = (
        P("dp", None, None),
        P("dp", None, None),
        P("dp", None, None),
        P("dp"),
        P("dp", "mp"),
        P("dp", "mp"),
        P("dp", "mp"),
        P("mp", "dp"),
        P("dp", "mp"),
        P("mp", "dp"),
        P("dp"),
        P("dp"),
        P("dp"),
        P("dp"),
        P("dp"),
        P("dp"),
    )
    return jax.shard_map(
        fused if fits(mesh) else local,
        mesh=mesh,
        in_specs=placed,
        out_specs=(
            P("dp", None, None),
            P("dp", None, None),
            P("dp", None, None),
            P("dp", "mp"),
            P("dp", "mp"),
            P("dp", "mp"),
            P("mp", "dp"),
            P("dp", "mp"),
            P("mp", "dp"),
            P("dp"),
            P("dp"),
            P("dp"),
            P("dp"),
            P("dp"),
            P("dp"),
        ),
        check_vma=False,
    )
```

```python
import functools

import jax
import jax.numpy as jnp
from jax import lax
from jax.experimental import pallas as pl
from jax.experimental.pallas import tpu as pltpu
from jax.sharding import PartitionSpec as P

HEAD = 64
PATCH = 256
EPS = 1e-05
F32 = jnp.float32
BF16 = jnp.bfloat16
MESH = pl.DeviceIdType.MESH
NN = (((1,), (0,)), ((), ()))
NT = (((1,), (1,)), ((), ()))
TN = (((0,), (0,)), ((), ()))
LIMIT = 54
SEMS = 70


def dot(a, b, dims):
    return lax.dot_general(a, b, dims, preferred_element_type=F32)


def at(start, size):
    return pl.ds(pl.multiple_of(start, size), size)


class Wire:
    def __init__(self, send_sem, recv_sem):
        self.send_sem, self.recv_sem = send_sem, recv_sem
        self.used, self.sent = 0, []

    def take(self, count=1):
        first = self.used
        self.used += count
        assert self.used <= SEMS
        return first

    def make(self, slot, src, dst, dev):
        return pltpu.make_async_remote_copy(
            src_ref=src,
            dst_ref=dst,
            send_sem=self.send_sem.at[slot],
            recv_sem=self.recv_sem.at[slot],
            device_id=dev,
            device_id_type=MESH,
        )

    def send(self, src, dst, dev):
        copy = self.make(self.take(), src, dst, dev)
        copy.start()
        self.sent.append(copy)
        return copy

    def send_all(self, parts, whole):
        slot = self.take()
        for src, dst, dev in parts:
            self.make(slot, src, dst, dev).start()
        copy = self.make(slot, whole, whole, parts[0][2])
        self.sent.append(copy)
        return copy

    def drain(self):
        for copy in self.sent:
            copy.wait_send()


def norm_back(z, mean, rstd, gain, dy):
    zhat = (z - mean) * rstd
    t = dy * gain
    mt = jnp.mean(t, axis=-1, keepdims=True)
    mz = jnp.mean(t * zhat, axis=-1, keepdims=True)
    return rstd * (t - mt - zhat * mz), zhat


def layer_kernel(
    counts,
    media,
    latents,
    cot,
    wq,
    wk,
    wv,
    wo,
    up,
    down,
    mg,
    mb,
    lg,
    lb,
    fg,
    fb,
    lat_out,
    media_out,
    lgrad_out,
    gmat,
    gup,
    gdown,
    vecs,
    send_sem,
    recv_sem,
    local_sem,
    prm_own,
    prm,
    vec,
    xin,
    lat,
    kin,
    mu,
    rs,
    w4,
    wo_own,
    upb,
    dnb,
    kb,
    vb,
    qb,
    att,
    attl,
    mix,
    mid,
    hid,
    cota,
    act,
    ig,
    hgs,
    hgr,
    hgx,
    fos,
    fxr,
    fos2,
    fors,
    fox,
    gus,
    gur,
    guo,
    gu,
    gua,
    gds,
    gdr,
    gdo,
    gd,
    gda,
    midg,
    lowb,
    mgr,
    kg,
    vg,
    qg,
    cgs,
    cgr,
    gown,
    g1,
    yr,
    g2,
    zr,
    zs,
    dxs,
    accg,
    accb,
    wsc,
    vgs,
    vgc,
    vgt,
    vga,
):
    i = lax.axis_index("dp")
    j = lax.axis_index("mp")
    x, c = j // 2, j % 2
    yy, z = i % 2, i // 2
    zlo, zhi = z % 2, z // 2
    r = i % 4

    def peer(k):
        a = 1 - yy if k & 1 else yy
        b = 1 - zlo if k & 2 else zlo
        d = 1 - zhi if k & 4 else zhi
        return d * 4 + b * 2 + a

    jx = j + 2 - 4 * x
    jc = j + 1 - 2 * c
    ox = 1 - x
    oc = 1 - c
    xpart = (i, jx)
    cpart = (i, jc)
    ypart = (peer(1), j)
    wire = Wire(send_sem, recv_sem)

    def w3b(ii, xx, cc):
        return w4.at[xx, ii // 2, ii % 2, :, :, at(cc * 128, 128)]

    out_w, kqv = slice(3, 4), slice(0, 3)

    def w3col(xx, y_, cc, mats=kqv):
        return w4.at[xx, :, y_, mats, :, at(cc * 128, 128)]

    local = []

    def bring(src, dst):
        copy = pltpu.make_async_copy(src, dst, local_sem.at[len(local)])
        copy.start()
        local.append(copy)
        return copy

    bring(wk, w4.at[x, z, yy, 0, :, at(c * 128, 128)])
    bring(wv, w4.at[x, z, yy, 1, :, at(c * 128, 128)])
    bring(wq, w4.at[x, z, yy, 2, :, at(c * 128, 128)])
    bring(wo, wo_own)
    in_lat = bring(latents.at[c], lat)
    in_media = bring(media.at[c], xin)
    in_cot = bring(cot.at[c], cota.at[r])
    in_up = bring(up.at[:, at(r * 256, 256)], upb.at[i, :, at(c * 256, 256)])
    in_dn = bring(down.at[at(r * 256, 256), :], dnb.at[c, :, at(i * 128, 128)])
    for row, ref in enumerate((mg, mb, lg, lb, fg, fb)):
        prm_own[row : row + 1, :] = ref[...].astype(F32)
    prm_own[6:8, :] = jnp.zeros((2, 128), F32)
    prm[i] = prm_own[...]

    barrier = pltpu.get_barrier_semaphore()
    partners = [(peer(k), j) for k in range(1, 8)] + [xpart, cpart]
    partners += [(peer(k), jx) for k in range(1, 4)]
    for dev in partners:
        pl.semaphore_signal(barrier, inc=1, device_id=dev, device_id_type=MESH)

    in_lat.wait()
    lat32 = lat[...].astype(F32)
    lmean = jnp.mean(lat32, axis=-1, keepdims=True)
    lcen = lat32 - lmean
    mu[1280:1344, :] = lmean
    rs[1280:1344, :] = lax.rsqrt(jnp.mean(lcen * lcen, axis=-1, keepdims=True) + EPS)
    in_media.wait()

    def stat(t, carry):
        rows = at(t * 64, 64)
        v = xin[rows, :].astype(F32)
        m = jnp.mean(v, axis=-1, keepdims=True)
        cen = v - m
        mu[rows, :] = m
        rs[rows, :] = lax.rsqrt(jnp.mean(cen * cen, axis=-1, keepdims=True) + EPS)
        return carry

    lax.fori_loop(0, 20, stat, 0, unroll=4)
    pl.semaphore_wait(barrier, len(partners))

    for copy in local[:4]:
        copy.wait()
    w4[x, z, yy, 3, :, at(c * 128, 128)] = wo_own[...].astype(F32).T.astype(BF16)
    others = range(1, 8)
    got_prm = wire.send_all([(prm_own, prm.at[i], (peer(k), j)) for k in others], prm.at[0:7])

    def same(view, dev):
        return wire.send(view, view, dev)

    z_near = same(w3b(i, x, c), (peer(2), j))
    z_far = same(w3b(i, x, c), (peer(4), j))
    y3 = [same(w3b(i, x, c), ypart)]
    got_prm.wait_recv()
    for ii in range(8):
        vec[:, ii * 128 : (ii + 1) * 128] = prm[ii]

    def media_norm(lo, hi):
        def strip(t, carry):
            rows = at(t * 64, 64)
            v = (xin[rows, :].astype(F32) - mu[rows, :]) * rs[rows, :]
            kin[rows, :] = (v * vec[0:1, :] + vec[1:2, :]).astype(BF16)
            return carry

        lax.fori_loop(lo, hi, strip, 0, unroll=2)

    kin[1280:1344, :] = (
        (lat[...].astype(F32) - mu[1280:1344, :]) * rs[1280:1344, :] * vec[2:3, :] + vec[3:4, :]
    ).astype(BF16)
    media_norm(0, 10)
    z_far.wait_recv()
    z_relay = same(w3b(peer(4), x, c), (peer(2), j))
    y3.append(same(w3b(peer(4), x, c), ypart))
    z_near.wait_recv()
    y3.append(same(w3b(peer(2), x, c), ypart))
    z_relay.wait_recv()
    y3.append(same(w3b(peer(6), x, c), ypart))
    everything = slice(0, 4)
    c3 = [same(w3col(x, yy, c, everything), cpart)]
    xo = [same(w3col(x, yy, c, out_w), xpart)]
    x3 = [same(w3col(x, yy, c), xpart)]
    in_cot.wait()
    half = at(x * 32, 32)
    cots = wire.send_all(
        [(cota.at[r, half], cota.at[r, half], (peer(k), j)) for k in (3, 2, 1)], cota.at[0:3, 0:32]
    )
    def up_part(k):
        return up.at[:, at(peer(k) % 4 * 256, 256)], upb.at[i, :, at(c * 256, 256)], (peer(k), j)

    def down_part(k):
        return down.at[at(peer(k) % 4 * 256, 256), :], dnb.at[c, :, at(i * 128, 128)], (peer(k), j)

    near, crossing = (4, 6, 2), (5, 7, 3, 1)
    ups = [wire.send_all([up_part(k) for k in near], upb.at[0:3, :, 0:256])]
    dns = [wire.send_all([down_part(k) for k in near], dnb.at[0, :, 0:384])]
    ups.append(wire.send_all([up_part(k) for k in crossing], upb.at[0:4, :, 0:256]))
    dns.append(wire.send_all([down_part(k) for k in crossing], dnb.at[0, :, 0:512]))
    media_norm(10, 20)
    for copy in y3:
        copy.wait_recv()
    c3.append(same(w3col(x, 1 - yy, c, everything), cpart))
    xo.append(same(w3col(x, 1 - yy, c, out_w), xpart))
    for copy in c3:
        copy.wait_recv()

    count = counts[c]
    head_of_lane = lax.broadcasted_iota(jnp.int32, (256, 256), 1) // HEAD
    head_of_row = lax.broadcasted_iota(jnp.int32, (256, 256), 0) // HEAD
    own_head = head_of_lane == head_of_row
    lane64 = lax.broadcasted_iota(jnp.int32, (64, 256), 1) // HEAD

    def spread(v):
        v = v.astype(F32)
        return jnp.where(own_head, jnp.concatenate([v, v, v, v], axis=0), 0.0).astype(BF16)

    def gather_heads(v):
        out = jnp.zeros((64, 256), F32)
        for h in range(4):
            out = jnp.where(lane64 == h, v[h * 64 : (h + 1) * 64, :], out)
        return out

    def weight(g, m):
        return w4[g, :, :, m].reshape(1024, 256)

    def attention(g, mixing=True):
        a = kin[...]
        kb[g] = dot(a, weight(g, 0), NN).astype(BF16)
        vb[g] = dot(a, weight(g, 1), NN).astype(BF16)
        qb[g] = dot(kin[1280:1344, :], weight(g, 2), NN).astype(BF16)
        s = dot(kb[g], spread(qb[g]), NT) * 0.125
        key = lax.broadcasted_iota(jnp.int32, (1344, 256), 0)
        s = jnp.where(jnp.logical_or(key < count * PATCH, key >= 1280), s, -1e30)
        att[g] = s
        top = jnp.max(s, axis=0, keepdims=True)
        e = jnp.exp(att[g] - top)
        att[g] = e
        scale = 1.0 / jnp.sum(e, axis=0, keepdims=True)
        p = att[g] * scale
        att[g] = p
        attl[g] = p.astype(BF16)
        if mixing:
            mixed = dot(attl[g], vb[g], TN)
            mix[g] = gather_heads(mixed).astype(BF16)

    attention(x)
    mx = same(mix.at[x], xpart)
    cots.wait_recv()
    halves = [cota.at[peer(k) % 4, half] for k in (3, 2, 1)]
    cots_x = wire.send_all([(v, v, xpart) for v in halves], cota.at[0:3, 0:32])
    x3.append(same(w3col(x, 1 - yy, c), xpart))
    cob = []
    for copy, y_ in zip(xo, (yy, 1 - yy)):
        copy.wait_recv()
        cob.append(same(w3col(ox, y_, c, out_w), cpart))
    mx.wait_recv()
    for copy in cob:
        copy.wait_recv()

    middle = lat[...].astype(F32) + (dot(mix[0], weight(0, 3), NT) + dot(mix[1], weight(1, 3), NT))
    mid[...] = middle
    fmean = jnp.mean(middle, axis=-1, keepdims=True)
    fcen = middle - fmean
    frs = lax.rsqrt(jnp.mean(fcen * fcen, axis=-1, keepdims=True) + EPS)
    hid[r] = (fcen * frs * vec[4:5, :] + vec[5:6, :]).astype(BF16)
    hids = wire.send_all([(hid.at[r], hid.at[r], (peer(k), j)) for k in (3, 2, 1)], hid.at[0:3])

    in_up.wait()
    in_dn.wait()
    for copy in ups:
        copy.wait_recv()
    cup = same(upb.at[:, :, at(c * 256, 256)], cpart)
    for copy in dns:
        copy.wait_recv()
    cdn = same(dnb.at[c], cpart)
    hids.wait_recv()
    cots_x.wait_recv()
    cup.wait_recv()
    cdn.wait_recv()

    hid_all = hid[...].reshape(256, 1024)
    cot_all = cota[...].reshape(256, 1024)
    up_all = upb[...].reshape(1024, 512)
    dn_all = dnb[...].reshape(512, 1024)
    inner = dot(hid_all, up_all, NN)
    phi = 0.5 * (1.0 + lax.erf(inner * (0.5**0.5)))
    act[...] = (inner * phi).astype(BF16)
    agrad = dot(cot_all, dn_all, NT)
    dens = jnp.exp(inner * inner * -0.5) * 0.3989422804014327
    ig[...] = (agrad * (phi + inner * dens)).astype(BF16)
    hgs[...] = dot(ig[...], up_all, NT).astype(BF16).reshape(4, 64, 1024)

    slot = x * 4 + r
    parts = []
    for k in (7, 6, 5, 3, 2, 1, 4):
        tx, tj = (ox, jx) if k >= 4 else (x, j)
        src = hgs.at[peer(k % 4) % 4, at(tx * 32, 32), :]
        parts.append((src, hgr.at[slot], (peer(k % 4), tj)))
    hg_in = wire.send_all(parts, hgr.at[0:7])
    hgr[slot] = hgs[r, at(x * 32, 32), :]

    gus[...] = dot(hid_all, ig[:, at(oc * 256, 256)], TN).astype(BF16).reshape(8, 128, 256)
    gu_in = wire.send(gus, gur, cpart)
    gds[...] = dot(act[:, at(oc * 256, 256)], cot_all, TN).astype(BF16)
    gd_in = wire.send(gds, gdr, cpart)
    guo[...] = dot(hid_all, ig[:, at(c * 256, 256)], TN).reshape(8, 128, 256)
    gdo[...] = dot(act[:, at(c * 256, 256)], cot_all, TN)

    def sum_of(ref, n):
        total = ref[0].astype(F32)
        for s in range(1, n):
            total = total + ref[s].astype(F32)
        return total

    fos[...] = dot(act[...], dn_all, NN).astype(BF16).reshape(4, 64, 1024)

    def up_back(ks):
        return wire.send_all([(gu.at[peer(k)], gua.at[i], (peer(k), j)) for k in ks], gua.at[0 : len(ks)])

    def down_back(ks):
        return wire.send_all(
            [(gd.at[:, at(peer(k) * 128, 128)], gda.at[i], (peer(k), j)) for k in ks],
            gda.at[0 : len(ks)],
        )

    gu_in.wait_recv()
    gu[...] = (guo[...] + gur[...].astype(F32)).astype(BF16)
    gua[i] = gu[i]
    gu_out = [up_back(near), up_back(crossing)]
    gd_in.wait_recv()
    gd[...] = (gdo[...] + gdr[...].astype(F32)).astype(BF16)
    gda[i] = gd[:, at(i * 128, 128)]
    gd_out = [down_back(near)]
    c3b = []
    for copy, y_ in zip(x3, (yy, 1 - yy)):
        copy.wait_recv()
        c3b.append(same(w3col(ox, y_, c), cpart))
    for copy in c3b:
        copy.wait_recv()
    attention(ox, False)

    hg_in.wait_recv()
    hgx[x] = sum_of(hgr, 8).astype(BF16)
    hgx_in = same(hgx.at[x], xpart)
    fx_in = wire.send(fos.at[:, at(ox * 32, 32), :], fxr, xpart)
    hgx_in.wait_recv()
    dy = hgx[...].reshape(64, 1024).astype(F32)
    middle = mid[...]
    fmean = jnp.mean(middle, axis=-1, keepdims=True)
    fcen = middle - fmean
    frs = lax.rsqrt(jnp.mean(fcen * fcen, axis=-1, keepdims=True) + EPS)
    dz, zhat = norm_back(middle, fmean, frs, vec[4:5, :], dy)

    def put_vec(k, v):
        for ii in range(8):
            vgs[ii, k : k + 1, :] = v[:, ii * 128 : (ii + 1) * 128]

    put_vec(4, jnp.sum(dy * zhat, axis=0, keepdims=True))
    put_vec(5, jnp.sum(dy, axis=0, keepdims=True))
    middle_grad = cota[r].astype(F32) + dz
    midg[...] = middle_grad
    low = middle_grad.astype(BF16)
    for g in (0, 1):
        mgr[g] = dot(low, weight(g, 3), NN).astype(BF16)
    lowb[...] = low

    def back_values(g):
        m4 = spread(mgr[g])

        vg[g] = dot(attl[g], m4, NN).astype(BF16)
        pa = att[g] * dot(vb[g], m4, NT)
        dxs[:, 0:256] = pa
        return jnp.sum(pa, axis=0, keepdims=True)

    def back_keys(g, delta):
        q4 = spread(qb[g])

        sg = (dxs[:, 0:256] - att[g] * delta).astype(BF16)
        attl[g] = sg
        kg[g] = (dot(sg, q4, NN) * 0.125).astype(BF16)
        total = dot(attl[g], kb[g], TN)
        qg[g] = (gather_heads(total) * 0.125).astype(BF16)

    def split(m, wide):
        wsc[...] = wide
        mine, other = wsc[at(c * 128, 128), :], wsc[at(oc * 128, 128), :]
        for ii in range(8):
            cols = slice(ii * 128, (ii + 1) * 128)
            gown[ii // 2, ii % 2, m] = mine[:, cols]
            cgs[ii // 2, ii % 2, m] = other[:, cols].astype(BF16)

    def one(ref, p):
        return ref.at[:, :, p]

    def chip_sum(p):
        one(g1, p)[...] = (one(gown, p)[...] + one(cgr, p)[...].astype(F32)).astype(BF16)
        return wire.send(g1.at[:, 1 - yy, p], yr.at[:, p], ypart)

    def to_core(p):
        return wire.send(one(cgs, p), one(cgr, p), cpart)

    delta = back_values(x)
    split(0, dot(vg[x], kin[...], TN))
    cg_in = [to_core(0)]
    split(1, dot(mix[x], lowb[...], TN))
    cg_in.append(to_core(1))
    back_keys(x, delta)
    y_in = []

    def to_y(p):
        cg_in[p].wait_recv()
        y_in.append(chip_sum(p))

    to_y(0)
    split(2, dot(kg[x], kin[...], TN))
    cg_in.append(to_core(2))
    to_y(1)
    split(3, dot(qg[x], kin[1280:1344, :], TN))
    cg_in.append(to_core(3))
    to_y(2)
    to_y(3)
    fx_in.wait_recv()
    fos2[...] = (fos[:, at(x * 32, 32), :].astype(F32) + fxr[...].astype(F32)).astype(BF16)
    fors[r] = fos2[r]
    fo_in = wire.send_all(
        [(fos2.at[peer(k) % 4], fors.at[r], (peer(k), j)) for k in (3, 2, 1)], fors.at[0:3]
    )
    gd_out.append(down_back(crossing))
    back_keys(ox, back_values(ox))

    def dx_tile(rows):
        return (
            dot(kg[0, rows, :], weight(0, 0), NT)
            + dot(kg[1, rows, :], weight(1, 0), NT)
            + dot(vg[0, rows, :], weight(0, 1), NT)
            + dot(vg[1, rows, :], weight(1, 1), NT)
        )

    accg[...] = jnp.zeros((8, 1024), F32)
    accb[...] = jnp.zeros((8, 1024), F32)
    out_base = wire.take(5)

    def out_copy(t, slot):
        rows = at(t * 256, 256)
        return wire.make(slot, media_out.at[c, rows, :], media_out.at[c, rows, :], cpart)

    def media_back(t, carry):
        dxs[0:256, :] = dx_tile(at(t * 256, 256))

        rows = at(t * 256, 256)
        v = xin[rows, :].astype(F32)
        dy = dxs[0:256, :]
        dz, zhat = norm_back(v, mu[rows, :], rs[rows, :], vec[0:1, :], dy)
        media_out[c, rows, :] = dz.astype(BF16)
        accg[...] += (dy * zhat).reshape(32, 8, 1024).sum(0)
        accb[...] += dy.reshape(32, 8, 1024).sum(0)
        out_copy(t, out_base + t).start()
        return carry

    zn, zf = peer(2) // 2, peer(4) // 2
    zd = peer(6) // 2

    def to_near(p):
        y_in[p].wait_recv()
        g2[:, p] = (g1[:, yy, p].astype(F32) + yr[:, p].astype(F32)).astype(BF16)
        parts = [(g2.at[zn, p], zr.at[0, p], (peer(2), j)), (g2.at[zd, p], zr.at[1, p], (peer(2), j))]
        return wire.send_all(parts, zr.at[0:2, 0])

    def to_far(p):
        n_in[p].wait_recv()
        zs[p] = (g2[zf, p].astype(F32) + zr[1, p].astype(F32)).astype(BF16)
        return wire.send(zs.at[p], zr.at[2, p], (peer(4), j))

    n_in, f_in = [], []
    lax.fori_loop(0, 2, media_back, 0)
    n_in.append(to_near(0))
    lax.fori_loop(2, 4, media_back, 0)
    n_in.append(to_near(1))
    lax.fori_loop(4, 5, media_back, 0)
    f_in.append(to_far(0))
    n_in.append(to_near(2))
    put_vec(0, jnp.sum(accg[...], axis=0, keepdims=True))
    put_vec(1, jnp.sum(accb[...], axis=0, keepdims=True))
    dxs[0:64, :] = dx_tile(pl.ds(1280, 64))
    lsum = dxs[0:64, :] + dot(qg[0], weight(0, 2), NT) + dot(qg[1], weight(1, 2), NT)
    lat32 = lat[...].astype(F32)
    dz, zhat = norm_back(lat32, mu[1280:1344, :], rs[1280:1344, :], vec[2:3, :], lsum)
    lgrad_out[c] = (midg[...] + dz).astype(BF16)
    lg_in = same(lgrad_out.at[c], cpart)
    put_vec(2, jnp.sum(lsum * zhat, axis=0, keepdims=True))
    put_vec(3, jnp.sum(lsum, axis=0, keepdims=True))
    for ii in range(8):
        vgs[ii, 6:8, :] = jnp.zeros((2, 128), F32)
    vg_in = wire.send(vgs, vgc, cpart)

    f_in.append(to_far(1))
    n_in.append(to_near(3))
    vg_in.wait_recv()
    vgt[...] = vgs[...] + vgc[...]
    vga[i] = vgt[i]
    v_in = wire.send_all([(vgt.at[peer(k)], vga.at[i], (peer(k), j)) for k in others], vga.at[0:7])
    f_in.append(to_far(2))
    fo_in.wait_recv()
    fox[x] = sum_of(fors, 4).astype(BF16)
    fox_in = same(fox.at[x], xpart)
    f_in.append(to_far(3))
    for copy in gu_out:
        copy.wait_recv()
    for q in range(4):
        gup[:, q * 256 : (q + 1) * 256] = gua[q].astype(F32) + gua[4 + q].astype(F32)
    for copy in gd_out:
        copy.wait_recv()
    for q in range(4):
        gdown[q * 256 : (q + 1) * 256, :] = gda[q].astype(F32) + gda[4 + q].astype(F32)

    fox_in.wait_recv()
    lat_out[c] = (mid[...] + fox[...].reshape(64, 1024).astype(F32)).astype(BF16)
    lo_in = same(lat_out.at[c], cpart)
    for copy in f_in:
        copy.wait_recv()
    last = g2[z].astype(F32) + zr[0].astype(F32) + zr[2].astype(F32)
    gmat[0] = last[3].T
    gmat[1] = last[2].T
    gmat[2] = last[0].T
    gmat[3] = last[1]
    v_in.wait_recv()
    vecs[...] = sum_of(vga, 8)

    for t in range(5):
        out = out_copy(t, out_base + t)
        out.wait_send()
        out.wait_recv()
    lg_in.wait_recv()
    lo_in.wait_recv()
    wire.drain()


SCRATCH = (
    ("prm_own", (8, 128), F32),
    ("prm", (8, 8, 128), F32),
    ("vec", (8, 1024), F32),
    ("xin", (1280, 1024), BF16),
    ("lat", (64, 1024), BF16),
    ("kin", (1344, 1024), BF16),
    ("mu", (1344, 1), F32),
    ("rs", (1344, 1), F32),
    ("w4", (2, 4, 2, 4, 128, 256), BF16),
    ("wo_own", (128, 128), BF16),
    ("upb", (8, 128, 512), BF16),
    ("dnb", (2, 256, 1024), BF16),
    ("kb", (2, 1344, 256), BF16),
    ("vb", (2, 1344, 256), BF16),
    ("qb", (2, 64, 256), BF16),
    ("att", (2, 1344, 256), F32),
    ("attl", (2, 1344, 256), BF16),
    ("mix", (2, 64, 256), BF16),
    ("mid", (64, 1024), F32),
    ("hid", (4, 64, 1024), BF16),
    ("cota", (4, 64, 1024), BF16),
    ("act", (256, 512), BF16),
    ("ig", (256, 512), BF16),
    ("hgs", (4, 64, 1024), BF16),
    ("hgr", (8, 32, 1024), BF16),
    ("hgx", (2, 32, 1024), BF16),
    ("fos", (4, 64, 1024), BF16),
    ("fxr", (4, 32, 1024), BF16),
    ("fos2", (4, 32, 1024), BF16),
    ("fors", (4, 32, 1024), BF16),
    ("fox", (2, 32, 1024), BF16),
    ("gus", (8, 128, 256), BF16),
    ("gur", (8, 128, 256), BF16),
    ("guo", (8, 128, 256), F32),
    ("gu", (8, 128, 256), BF16),
    ("gua", (8, 128, 256), BF16),
    ("gds", (256, 1024), BF16),
    ("gdr", (256, 1024), BF16),
    ("gdo", (256, 1024), F32),
    ("gd", (256, 1024), BF16),
    ("gda", (8, 256, 128), BF16),
    ("midg", (64, 1024), F32),
    ("lowb", (64, 1024), BF16),
    ("mgr", (2, 64, 256), BF16),
    ("kg", (2, 1344, 256), BF16),
    ("vg", (2, 1344, 256), BF16),
    ("qg", (2, 64, 256), BF16),
    ("cgs", (4, 2, 4, 128, 128), BF16),
    ("cgr", (4, 2, 4, 128, 128), BF16),
    ("gown", (4, 2, 4, 128, 128), F32),
    ("g1", (4, 2, 4, 128, 128), BF16),
    ("yr", (4, 4, 128, 128), BF16),
    ("g2", (4, 4, 128, 128), BF16),
    ("zr", (3, 4, 128, 128), BF16),
    ("zs", (4, 128, 128), BF16),
    ("dxs", (1344, 1024), F32),
    ("accg", (8, 1024), F32),
    ("accb", (8, 1024), F32),
    ("wsc", (256, 1024), F32),
    ("vgs", (8, 8, 128), F32),
    ("vgc", (8, 8, 128), F32),
    ("vgt", (8, 8, 128), F32),
    ("vga", (8, 8, 128), F32),
)


def hand_out(lat, med, lgr, gmat, gup, gdown, vecs, *rest):
    outs, sem = rest[:15], rest[15]
    moves = [(med, outs[1]), (gup, outs[7]), (gdown, outs[8]), (lat, outs[0]), (lgr, outs[2])]
    moves += [(gmat.at[k], outs[3 + k]) for k in range(4)]
    moves += [(vecs.at[k : k + 1], outs[9 + k]) for k in range(6)]
    copies = [pltpu.make_async_copy(a, b, sem.at[k]) for k, (a, b) in enumerate(moves)]
    for copy in copies:
        copy.start()
    for copy in copies:
        copy.wait()


def fused(media, latents, cotangent, image_counts, wq, wk, wv, wo, up, down, *gains):
    anyspace = pl.BlockSpec(memory_space=pl.ANY)
    vmem = pl.BlockSpec(memory_space=pltpu.VMEM)
    smem = pl.BlockSpec(memory_space=pltpu.SMEM)
    shape = jax.ShapeDtypeStruct
    outs = pl.pallas_call(
        layer_kernel,
        out_shape=[
            pltpu.VMEM(latents.shape, BF16),
            pltpu.VMEM(media.shape, BF16),
            pltpu.VMEM(latents.shape, BF16),
            pltpu.VMEM((4, 128, 128), F32),
            pltpu.VMEM(up.shape, F32),
            pltpu.VMEM(down.shape, F32),
            pltpu.VMEM((8, 128), F32),
        ],
        in_specs=[smem] + [anyspace] * 9 + [vmem] * 6,
        out_specs=[vmem] * 7,
        scratch_shapes=[
            pltpu.SemaphoreType.DMA((SEMS,)),
            pltpu.SemaphoreType.DMA((SEMS,)),
            pltpu.SemaphoreType.DMA((9,)),
        ]
        + [pltpu.VMEM(size, kind) for _, size, kind in SCRATCH],
        compiler_params=pltpu.CompilerParams(
            collective_id=0, has_side_effects=True, vmem_limit_bytes=LIMIT * 2**20
        ),
        cost_estimate=pl.CostEstimate(
            flops=14 * 10**9, bytes_accessed=20 * 10**6, transcendentals=10**6
        ),
    )(
        image_counts,
        media,
        latents,
        cotangent,
        wq,
        wk,
        wv,
        wo,
        up,
        down,
        *[v.reshape(1, 128) for v in gains],
    )
    outs = pl.pallas_call(
        hand_out,
        out_shape=[shape(v.shape, BF16) for v in (latents, media, latents)]
        + [shape(v.shape, F32) for v in (wq, wk, wv, wo, up, down)]
        + [shape((1, 128), F32)] * 6,
        in_specs=[vmem] * 7,
        out_specs=[anyspace] * 15,
        scratch_shapes=[pltpu.SemaphoreType.DMA((15,))],
        compiler_params=pltpu.CompilerParams(vmem_limit_bytes=4 * 2**20),
    )(*[pltpu.with_memory_space_constraint(v, pltpu.VMEM) for v in outs])
    return tuple(outs[:9]) + tuple(v.reshape(128) for v in outs[9:])


def fits(mesh):
    return mesh.shape["dp"] == 8 and mesh.shape["mp"] == 4


MB = 2
SB = 1


def layer_norm(inputs, gain, bias):
    center = inputs - jnp.mean(inputs, axis=-1, keepdims=True)
    spread = jnp.mean(center * center, axis=-1, keepdims=True)
    return center * lax.rsqrt(spread + 1e-05) * gain + bias


def gelu_exact(inputs):
    return jax.nn.gelu(inputs, approximate=False)


def add_tuples(left, right):
    return tuple((first + second for first, second in zip(left, right)))


def micro_step(gathered, media, latents, cotangent, counts):
    (
        query_matrix,
        k_weight,
        v_weight,
        output_projection_weight,
        up_projection_weight,
        down_projection_weight,
        media_gain,
        media_bias,
        latent_gain,
        latent_bias,
        ff_gain,
        ff_bias,
    ) = gathered
    samples = media.shape[0]
    media_len = media.shape[1]
    latent_len = latents.shape[1]
    keys_len = media_len + latent_len
    span = query_matrix.shape[1]
    local_heads = span // HEAD
    wide_rows = jnp.float32
    key_matrix = jnp.concatenate([k_weight, v_weight], axis=1)
    latent_full = latents.astype(wide_rows)
    latent_norm32, latent_pull = jax.vjp(
        layer_norm, latent_full, latent_gain.astype(wide_rows), latent_bias.astype(wide_rows)
    )
    latent_normed_rows = latent_norm32.astype(jnp.bfloat16)
    media_norm32, media_pull = jax.vjp(
        layer_norm,
        media.astype(wide_rows),
        media_gain.astype(wide_rows),
        media_bias.astype(wide_rows),
    )
    media_norm = media_norm32.astype(jnp.bfloat16)
    media_kv = jnp.einsum(
        "snd,dh->snh", media_norm, key_matrix, preferred_element_type=wide_rows
    ).astype(jnp.bfloat16)
    query_rows = jnp.einsum(
        "gjm,mu->gju", latent_normed_rows, query_matrix, preferred_element_type=wide_rows
    ).astype(jnp.bfloat16)
    latent_kv = jnp.einsum(
        "gjm,mu->gju", latent_normed_rows, key_matrix, preferred_element_type=wide_rows
    ).astype(jnp.bfloat16)
    both_kv = jnp.concatenate([media_kv, latent_kv], axis=1)
    head_queries = query_rows.reshape(samples, latent_len, local_heads, HEAD)
    head_keys = both_kv[:, :, :span].reshape(samples, keys_len, local_heads, HEAD)
    head_values = both_kv[:, :, span:].reshape(samples, keys_len, local_heads, HEAD)
    places = jnp.arange(keys_len)
    valid = jnp.logical_or(places[None, :] // PATCH < counts[:, None], places[None, :] >= media_len)

    def scores_of():
        raw = (
            jnp.einsum("slhe,snhe->shln", head_queries, head_keys, preferred_element_type=wide_rows)
            * 0.125
        )
        return jnp.where(valid[:, None, None, :], raw, -1e30)

    scores = scores_of()
    row_max = jnp.max(scores, axis=-1, keepdims=True)
    logsum = row_max + jnp.log(jnp.sum(jnp.exp(scores - row_max), axis=-1, keepdims=True))
    attend_low = jnp.exp(scores - logsum).astype(jnp.bfloat16)
    mixed_rows = jnp.einsum(
        "shln,snhe->slhe", attend_low, head_values, preferred_element_type=wide_rows
    )
    mixed_rows = mixed_rows.reshape(samples, latent_len, span).astype(jnp.bfloat16)
    attn_out = lax.psum(
        jnp.einsum(
            "rwa,ax->rwx", mixed_rows, output_projection_weight, preferred_element_type=wide_rows
        ),
        "mp",
    )
    middle = latent_full + attn_out
    hidden32, ff_pull = jax.vjp(
        layer_norm, middle, ff_gain.astype(wide_rows), ff_bias.astype(wide_rows)
    )
    hidden_rows = hidden32.astype(jnp.bfloat16)
    inner_rows = jnp.einsum(
        "qab,bo->qao", hidden_rows, up_projection_weight, preferred_element_type=wide_rows
    )
    active32, gelu_pull = jax.vjp(gelu_exact, inner_rows)
    active_units = active32.astype(jnp.bfloat16)
    ff_out = lax.psum(
        jnp.einsum(
            "pye,ej->pyj", active_units, down_projection_weight, preferred_element_type=wide_rows
        ).astype(jnp.bfloat16),
        "mp",
    ).astype(jnp.float32)
    result = (middle + ff_out).astype(jnp.bfloat16)
    down_projection_grad = jnp.einsum(
        "kje,kju->eu", active_units, cotangent, preferred_element_type=wide_rows
    )
    active_units_grad = jnp.einsum(
        "jvw,ow->jvo", cotangent, down_projection_weight, preferred_element_type=wide_rows
    )
    (inner_grad,) = gelu_pull(active_units_grad)
    inner_rows_reduced = inner_grad.astype(jnp.bfloat16)
    up_projection_grad = jnp.einsum(
        "imw,imk->wk", hidden_rows, inner_rows_reduced, preferred_element_type=wide_rows
    )
    hidden_grad = lax.psum(
        jnp.einsum(
            "xvm,nm->xvn",
            inner_rows_reduced,
            up_projection_weight,
            preferred_element_type=wide_rows,
        ).astype(jnp.bfloat16),
        "mp",
    ).astype(jnp.float32)
    middle_part, ff_gain_grad, ff_bias_grad = ff_pull(hidden_grad)
    middle_grad = cotangent.astype(wide_rows) + middle_part
    middle_rows_reduced = middle_grad.astype(jnp.bfloat16)
    output_projection_grad = jnp.einsum(
        "gfb,gfw->bw", mixed_rows, middle_rows_reduced, preferred_element_type=wide_rows
    )
    mixed_grad = jnp.einsum(
        "kzw,nw->kzn",
        middle_rows_reduced,
        output_projection_weight,
        preferred_element_type=wide_rows,
    ).astype(jnp.bfloat16)
    mixed_grad = mixed_grad.reshape(samples, latent_len, local_heads, HEAD)
    attend = jnp.exp(scores_of() - logsum)
    attend_grad = jnp.einsum(
        "slhe,snhe->shln", mixed_grad, head_values, preferred_element_type=wide_rows
    )
    score_grad = attend * (attend_grad - jnp.sum(attend * attend_grad, axis=-1, keepdims=True))
    score_grad = score_grad.astype(jnp.bfloat16)
    query_rows_grad = (
        jnp.einsum("shln,snhe->slhe", score_grad, head_keys, preferred_element_type=wide_rows)
        * 0.125
    )
    query_rows_grad = query_rows_grad.astype(jnp.bfloat16).reshape(samples, latent_len, span)
    key_grad = (
        jnp.einsum("shln,slhe->snhe", score_grad, head_queries, preferred_element_type=wide_rows)
        * 0.125
    )
    key_grad = key_grad.astype(jnp.bfloat16).reshape(samples, keys_len, span)
    value_grad = jnp.einsum(
        "shln,slhe->snhe", attend_low, mixed_grad, preferred_element_type=wide_rows
    )
    value_grad = value_grad.astype(jnp.bfloat16).reshape(samples, keys_len, span)
    kv_grad = jnp.concatenate([key_grad, value_grad], axis=2)
    media_kv_grad = kv_grad[:, :media_len]
    latent_key_value_grad = kv_grad[:, media_len:]
    query_weight_grad = jnp.einsum(
        "cbi,cbu->iu", latent_normed_rows, query_rows_grad, preferred_element_type=wide_rows
    )
    latent_wgrad = jnp.einsum(
        "cbi,cbu->iu", latent_normed_rows, latent_key_value_grad, preferred_element_type=wide_rows
    )
    latent_portion = jnp.einsum(
        "kwt,gt->kwg", query_rows_grad, query_matrix, preferred_element_type=wide_rows
    )
    latent_portion = latent_portion + jnp.einsum(
        "kwt,gt->kwg", latent_key_value_grad, key_matrix, preferred_element_type=wide_rows
    )
    media_part = jnp.einsum(
        "snh,dh->snd", media_kv_grad, key_matrix, preferred_element_type=wide_rows
    )
    media_wgrad = jnp.einsum(
        "snd,snh->dh", media_norm, media_kv_grad, preferred_element_type=wide_rows
    )
    kv_weight_grad = media_wgrad + latent_wgrad
    media_sum, latent_sum = (
        lax.psum(media_part.astype(jnp.bfloat16), "mp").astype(jnp.float32),
        lax.psum(latent_portion.astype(jnp.bfloat16), "mp").astype(jnp.float32),
    )
    media_back, media_gain_grad, media_bias_grad = media_pull(media_sum)
    media_out = media_back.astype(jnp.bfloat16)
    latent_back, latent_gain_grad, latent_bias_grad = latent_pull(latent_sum)
    latent_grad = middle_grad + latent_back
    grads = (
        query_weight_grad,
        kv_weight_grad[:, :span],
        kv_weight_grad[:, span:],
        output_projection_grad,
        up_projection_grad,
        down_projection_grad,
        media_gain_grad,
        media_bias_grad,
        latent_gain_grad,
        latent_bias_grad,
        ff_gain_grad,
        ff_bias_grad,
    )
    return (result, media_out, latent_grad.astype(jnp.bfloat16), grads)


def local(
    media,
    latents,
    cotangent,
    image_counts,
    query_matrix,
    k_weight,
    v_weight,
    output_projection_weight,
    up_projection_weight,
    down_projection_weight,
    media_gain,
    media_bias,
    latent_gain,
    latent_bias,
    ff_gain,
    ff_bias,
):
    results = []
    media_grads = []
    latent_grads = []
    totals = ()
    for micro_index in range(MB):
        gathered = (
            lax.all_gather(query_matrix, "dp", axis=0, tiled=True),
            lax.all_gather(k_weight, "dp", axis=0, tiled=True),
            lax.all_gather(v_weight, "dp", axis=0, tiled=True),
            lax.all_gather(output_projection_weight, "dp", axis=1, tiled=True),
            lax.all_gather(up_projection_weight, "dp", axis=0, tiled=True),
            lax.all_gather(down_projection_weight, "dp", axis=1, tiled=True),
            lax.all_gather(media_gain, "dp", axis=0, tiled=True),
            lax.all_gather(media_bias, "dp", axis=0, tiled=True),
            lax.all_gather(latent_gain, "dp", axis=0, tiled=True),
            lax.all_gather(latent_bias, "dp", axis=0, tiled=True),
            lax.all_gather(ff_gain, "dp", axis=0, tiled=True),
            lax.all_gather(ff_bias, "dp", axis=0, tiled=True),
        )
        lower = micro_index * SB
        upper = lower + SB
        result, media_back, latent_back, grads = micro_step(
            gathered,
            media[lower:upper],
            latents[lower:upper],
            cotangent[lower:upper],
            image_counts[lower:upper],
        )
        grads = (
            lax.psum_scatter(grads[0], "dp", scatter_dimension=0, tiled=True),
            lax.psum_scatter(grads[1], "dp", scatter_dimension=0, tiled=True),
            lax.psum_scatter(grads[2], "dp", scatter_dimension=0, tiled=True),
            lax.psum_scatter(grads[3], "dp", scatter_dimension=1, tiled=True),
            lax.psum_scatter(grads[4], "dp", scatter_dimension=0, tiled=True),
            lax.psum_scatter(grads[5], "dp", scatter_dimension=1, tiled=True),
            lax.psum_scatter(grads[6], "dp", scatter_dimension=0, tiled=True),
            lax.psum_scatter(grads[7], "dp", scatter_dimension=0, tiled=True),
            lax.psum_scatter(grads[8], "dp", scatter_dimension=0, tiled=True),
            lax.psum_scatter(grads[9], "dp", scatter_dimension=0, tiled=True),
            lax.psum_scatter(grads[10], "dp", scatter_dimension=0, tiled=True),
            lax.psum_scatter(grads[11], "dp", scatter_dimension=0, tiled=True),
        )
        totals = grads if micro_index == 0 else add_tuples(totals, grads)
        results.append(result)
        media_grads.append(media_back)
        latent_grads.append(latent_back)
    return (
        jnp.concatenate(results, axis=0),
        jnp.concatenate(media_grads, axis=0),
        jnp.concatenate(latent_grads, axis=0),
        totals[0],
        totals[1],
        totals[2],
        totals[3],
        totals[4],
        totals[5],
        totals[6],
        totals[7],
        totals[8],
        totals[9],
        totals[10],
        totals[11],
    )


def solution(mesh):
    placed = (
        P("dp", None, None),
        P("dp", None, None),
        P("dp", None, None),
        P("dp"),
        P("dp", "mp"),
        P("dp", "mp"),
        P("dp", "mp"),
        P("mp", "dp"),
        P("dp", "mp"),
        P("mp", "dp"),
        P("dp"),
        P("dp"),
        P("dp"),
        P("dp"),
        P("dp"),
        P("dp"),
    )
    return jax.shard_map(
        fused if fits(mesh) else local,
        mesh=mesh,
        in_specs=placed,
        out_specs=(
            P("dp", None, None),
            P("dp", None, None),
            P("dp", None, None),
            P("dp", "mp"),
            P("dp", "mp"),
            P("dp", "mp"),
            P("mp", "dp"),
            P("dp", "mp"),
            P("mp", "dp"),
            P("dp"),
            P("dp"),
            P("dp"),
            P("dp"),
            P("dp"),
            P("dp"),
        ),
        check_vma=False,
    )
```

```python
import functools

import jax
import jax.numpy as jnp
from jax import lax
from jax.experimental import pallas as pl
from jax.experimental.pallas import tpu as pltpu
from jax.sharding import PartitionSpec as P

HEAD = 64
PATCH = 256
EPS = 1e-05
F32 = jnp.float32
BF16 = jnp.bfloat16
MESH = pl.DeviceIdType.MESH
NN = (((1,), (0,)), ((), ()))
NT = (((1,), (1,)), ((), ()))
TN = (((0,), (0,)), ((), ()))
LIMIT = 54
SEMS = 70


def dot(a, b, dims):
    return lax.dot_general(a, b, dims, preferred_element_type=F32)


def at(start, size):
    return pl.ds(pl.multiple_of(start, size), size)


class Wire:
    def __init__(self, send_sem, recv_sem):
        self.send_sem, self.recv_sem = send_sem, recv_sem
        self.used, self.sent = 0, []

    def take(self, count=1):
        first = self.used
        self.used += count
        assert self.used <= SEMS
        return first

    def make(self, slot, src, dst, dev):
        return pltpu.make_async_remote_copy(
            src_ref=src,
            dst_ref=dst,
            send_sem=self.send_sem.at[slot],
            recv_sem=self.recv_sem.at[slot],
            device_id=dev,
            device_id_type=MESH,
        )

    def send(self, src, dst, dev):
        copy = self.make(self.take(), src, dst, dev)
        copy.start()
        self.sent.append(copy)
        return copy

    def send_all(self, parts, whole):
        slot = self.take()
        for src, dst, dev in parts:
            self.make(slot, src, dst, dev).start()
        copy = self.make(slot, whole, whole, parts[0][2])
        self.sent.append(copy)
        return copy

    def drain(self):
        for copy in self.sent:
            copy.wait_send()


def norm_back(z, mean, rstd, gain, dy):
    zhat = (z - mean) * rstd
    t = dy * gain
    mt = jnp.mean(t, axis=-1, keepdims=True)
    mz = jnp.mean(t * zhat, axis=-1, keepdims=True)
    return rstd * (t - mt - zhat * mz), zhat


def layer_kernel(
    counts,
    media,
    latents,
    cot,
    wq,
    wk,
    wv,
    wo,
    up,
    down,
    mg,
    mb,
    lg,
    lb,
    fg,
    fb,
    lat_out,
    media_out,
    lgrad_out,
    gmat,
    gup,
    gdown,
    vecs,
    send_sem,
    recv_sem,
    local_sem,
    prm_own,
    prm,
    vec,
    xin,
    lat,
    kin,
    mu,
    rs,
    w4,
    wo_own,
    upb,
    dnb,
    kb,
    vb,
    qb,
    att,
    attl,
    mix,
    mid,
    hid,
    cota,
    act,
    ig,
    hgs,
    hgr,
    hgx,
    fos,
    fxr,
    fos2,
    fors,
    fox,
    gus,
    gur,
    guo,
    gu,
    gua,
    gds,
    gdr,
    gdo,
    gd,
    gda,
    midg,
    lowb,
    mgr,
    kg,
    vg,
    qg,
    cgs,
    cgr,
    gown,
    g1,
    yr,
    g2,
    zr,
    zs,
    dxs,
    accg,
    accb,
    wsc,
    vgs,
    vgc,
    vgt,
    vga,
):
    i = lax.axis_index("dp")
    j = lax.axis_index("mp")
    x, c = j // 2, j % 2
    yy, z = i % 2, i // 2
    zlo, zhi = z % 2, z // 2
    r = i % 4

    def peer(k):
        a = 1 - yy if k & 1 else yy
        b = 1 - zlo if k & 2 else zlo
        d = 1 - zhi if k & 4 else zhi
        return d * 4 + b * 2 + a

    jx = j + 2 - 4 * x
    jc = j + 1 - 2 * c
    ox = 1 - x
    oc = 1 - c
    xpart = (i, jx)
    cpart = (i, jc)
    ypart = (peer(1), j)
    wire = Wire(send_sem, recv_sem)

    def w3b(ii, xx, cc):
        return w4.at[xx, ii // 2, ii % 2, :, :, at(cc * 128, 128)]

    out_w, kqv = slice(3, 4), slice(0, 3)

    def w3col(xx, y_, cc, mats=kqv):
        return w4.at[xx, :, y_, mats, :, at(cc * 128, 128)]

    local = []

    def bring(src, dst):
        copy = pltpu.make_async_copy(src, dst, local_sem.at[len(local)])
        copy.start()
        local.append(copy)
        return copy

    bring(wk, w4.at[x, z, yy, 0, :, at(c * 128, 128)])
    bring(wv, w4.at[x, z, yy, 1, :, at(c * 128, 128)])
    bring(wq, w4.at[x, z, yy, 2, :, at(c * 128, 128)])
    bring(wo, wo_own)
    in_lat = bring(latents.at[c], lat)
    in_media = bring(media.at[c], xin)
    in_cot = bring(cot.at[c], cota.at[r])
    in_up = bring(up.at[:, at(r * 256, 256)], upb.at[i, :, at(c * 256, 256)])
    in_dn = bring(down.at[at(r * 256, 256), :], dnb.at[c, :, at(i * 128, 128)])
    for row, ref in enumerate((mg, mb, lg, lb, fg, fb)):
        prm_own[row : row + 1, :] = ref[...].astype(F32)
    prm_own[6:8, :] = jnp.zeros((2, 128), F32)
    prm[i] = prm_own[...]

    barrier = pltpu.get_barrier_semaphore()
    partners = [(peer(k), j) for k in range(1, 8)] + [xpart, cpart]
    partners += [(peer(k), jx) for k in range(1, 4)]
    for dev in partners:
        pl.semaphore_signal(barrier, inc=1, device_id=dev, device_id_type=MESH)

    in_lat.wait()
    lat32 = lat[...].astype(F32)
    lmean = jnp.mean(lat32, axis=-1, keepdims=True)
    lcen = lat32 - lmean
    mu[1280:1344, :] = lmean
    rs[1280:1344, :] = lax.rsqrt(jnp.mean(lcen * lcen, axis=-1, keepdims=True) + EPS)
    in_media.wait()

    def stat(t, carry):
        rows = at(t * 64, 64)
        v = xin[rows, :].astype(F32)
        m = jnp.mean(v, axis=-1, keepdims=True)
        cen = v - m
        mu[rows, :] = m
        rs[rows, :] = lax.rsqrt(jnp.mean(cen * cen, axis=-1, keepdims=True) + EPS)
        return carry

    lax.fori_loop(0, 20, stat, 0, unroll=4)
    pl.semaphore_wait(barrier, len(partners))

    for copy in local[:4]:
        copy.wait()
    w4[x, z, yy, 3, :, at(c * 128, 128)] = wo_own[...].astype(F32).T.astype(BF16)
    others = range(1, 8)
    got_prm = wire.send_all([(prm_own, prm.at[i], (peer(k), j)) for k in others], prm.at[0:7])

    def same(view, dev):
        return wire.send(view, view, dev)

    z_near = same(w3b(i, x, c), (peer(2), j))
    z_far = same(w3b(i, x, c), (peer(4), j))
    y3 = [same(w3b(i, x, c), ypart)]
    got_prm.wait_recv()
    for ii in range(8):
        vec[:, ii * 128 : (ii + 1) * 128] = prm[ii]

    def media_norm(lo, hi):
        def strip(t, carry):
            rows = at(t * 64, 64)
            v = (xin[rows, :].astype(F32) - mu[rows, :]) * rs[rows, :]
            kin[rows, :] = (v * vec[0:1, :] + vec[1:2, :]).astype(BF16)
            return carry

        lax.fori_loop(lo, hi, strip, 0, unroll=2)

    kin[1280:1344, :] = (
        (lat[...].astype(F32) - mu[1280:1344, :]) * rs[1280:1344, :] * vec[2:3, :] + vec[3:4, :]
    ).astype(BF16)
    media_norm(0, 10)
    z_far.wait_recv()
    z_relay = same(w3b(peer(4), x, c), (peer(2), j))
    y3.append(same(w3b(peer(4), x, c), ypart))
    z_near.wait_recv()
    y3.append(same(w3b(peer(2), x, c), ypart))
    z_relay.wait_recv()
    y3.append(same(w3b(peer(6), x, c), ypart))
    everything = slice(0, 4)
    c3 = [same(w3col(x, yy, c, everything), cpart)]
    xo = [same(w3col(x, yy, c, out_w), xpart)]
    x3 = [same(w3col(x, yy, c), xpart)]
    in_cot.wait()
    half = at(x * 32, 32)
    cots = wire.send_all(
        [(cota.at[r, half], cota.at[r, half], (peer(k), j)) for k in (3, 2, 1)], cota.at[0:3, 0:32]
    )
    def up_part(k):
        return up.at[:, at(peer(k) % 4 * 256, 256)], upb.at[i, :, at(c * 256, 256)], (peer(k), j)

    def down_part(k):
        return down.at[at(peer(k) % 4 * 256, 256), :], dnb.at[c, :, at(i * 128, 128)], (peer(k), j)

    near, crossing = (4, 6, 2), (5, 7, 3, 1)
    ups = [wire.send_all([up_part(k) for k in near[:2]], upb.at[0:2, :, 0:256])]
    dns = [wire.send_all([down_part(k) for k in near[:2]], dnb.at[0, :, 0:256])]
    media_norm(10, 20)
    for copy in y3:
        copy.wait_recv()
    c3.append(same(w3col(x, 1 - yy, c, everything), cpart))
    xo.append(same(w3col(x, 1 - yy, c, out_w), xpart))
    ups.append(wire.send_all([up_part(k) for k in (5, 7, 2, 3, 1)], upb.at[0:5, :, 0:256]))
    dns.append(wire.send_all([down_part(k) for k in (5, 7, 2, 3, 1)], dnb.at[0, :, 0:640]))
    for copy in c3:
        copy.wait_recv()

    count = counts[c]
    head_of_lane = lax.broadcasted_iota(jnp.int32, (256, 256), 1) // HEAD
    head_of_row = lax.broadcasted_iota(jnp.int32, (256, 256), 0) // HEAD
    own_head = head_of_lane == head_of_row
    lane64 = lax.broadcasted_iota(jnp.int32, (64, 256), 1) // HEAD

    def spread(v):
        v = v.astype(F32)
        return jnp.where(own_head, jnp.concatenate([v, v, v, v], axis=0), 0.0).astype(BF16)

    def gather_heads(v):
        out = jnp.zeros((64, 256), F32)
        for h in range(4):
            out = jnp.where(lane64 == h, v[h * 64 : (h + 1) * 64, :], out)
        return out

    def weight(g, m):
        return w4[g, :, :, m].reshape(1024, 256)

    def attention(g, mixing=True):
        a = kin[...]
        kb[g] = dot(a, weight(g, 0), NN).astype(BF16)
        vb[g] = dot(a, weight(g, 1), NN).astype(BF16)
        qb[g] = dot(kin[1280:1344, :], weight(g, 2), NN).astype(BF16)
        s = dot(kb[g], spread(qb[g]), NT) * 0.125
        key = lax.broadcasted_iota(jnp.int32, (1344, 256), 0)
        s = jnp.where(jnp.logical_or(key < count * PATCH, key >= 1280), s, -1e30)
        att[g] = s
        top = jnp.max(s, axis=0, keepdims=True)
        e = jnp.exp(att[g] - top)
        att[g] = e
        scale = 1.0 / jnp.sum(e, axis=0, keepdims=True)
        p = att[g] * scale
        att[g] = p
        attl[g] = p.astype(BF16)
        if mixing:
            mixed = dot(attl[g], vb[g], TN)
            mix[g] = gather_heads(mixed).astype(BF16)

    attention(x)
    mx = same(mix.at[x], xpart)
    cots.wait_recv()
    halves = [cota.at[peer(k) % 4, half] for k in (3, 2, 1)]
    cots_x = wire.send_all([(v, v, xpart) for v in halves], cota.at[0:3, 0:32])
    x3.append(same(w3col(x, 1 - yy, c), xpart))
    cob = []
    for copy, y_ in zip(xo, (yy, 1 - yy)):
        copy.wait_recv()
        cob.append(same(w3col(ox, y_, c, out_w), cpart))
    mx.wait_recv()
    for copy in cob:
        copy.wait_recv()

    middle = lat[...].astype(F32) + (dot(mix[0], weight(0, 3), NT) + dot(mix[1], weight(1, 3), NT))
    mid[...] = middle
    fmean = jnp.mean(middle, axis=-1, keepdims=True)
    fcen = middle - fmean
    frs = lax.rsqrt(jnp.mean(fcen * fcen, axis=-1, keepdims=True) + EPS)
    hid[r] = (fcen * frs * vec[4:5, :] + vec[5:6, :]).astype(BF16)
    hids = wire.send_all([(hid.at[r], hid.at[r], (peer(k), j)) for k in (3, 2, 1)], hid.at[0:3])

    in_up.wait()
    in_dn.wait()
    for copy in ups:
        copy.wait_recv()
    cup = same(upb.at[:, :, at(c * 256, 256)], cpart)
    for copy in dns:
        copy.wait_recv()
    cdn = same(dnb.at[c], cpart)
    hids.wait_recv()
    cots_x.wait_recv()
    cup.wait_recv()
    cdn.wait_recv()

    hid_all = hid[...].reshape(256, 1024)
    cot_all = cota[...].reshape(256, 1024)
    up_all = upb[...].reshape(1024, 512)
    dn_all = dnb[...].reshape(512, 1024)
    inner = dot(hid_all, up_all, NN)
    phi = 0.5 * (1.0 + lax.erf(inner * (0.5**0.5)))
    act[...] = (inner * phi).astype(BF16)
    agrad = dot(cot_all, dn_all, NT)
    dens = jnp.exp(inner * inner * -0.5) * 0.3989422804014327
    ig[...] = (agrad * (phi + inner * dens)).astype(BF16)
    hgs[...] = dot(ig[...], up_all, NT).astype(BF16).reshape(4, 64, 1024)

    slot = x * 4 + r
    parts = []
    for k in (7, 6, 5, 3, 2, 1, 4):
        tx, tj = (ox, jx) if k >= 4 else (x, j)
        src = hgs.at[peer(k % 4) % 4, at(tx * 32, 32), :]
        parts.append((src, hgr.at[slot], (peer(k % 4), tj)))
    hg_in = wire.send_all(parts, hgr.at[0:7])
    hgr[slot] = hgs[r, at(x * 32, 32), :]

    gus[...] = dot(hid_all, ig[:, at(oc * 256, 256)], TN).astype(BF16).reshape(8, 128, 256)
    gu_in = wire.send(gus, gur, cpart)
    gds[...] = dot(act[:, at(oc * 256, 256)], cot_all, TN).astype(BF16)
    gd_in = wire.send(gds, gdr, cpart)
    guo[...] = dot(hid_all, ig[:, at(c * 256, 256)], TN).reshape(8, 128, 256)
    gdo[...] = dot(act[:, at(c * 256, 256)], cot_all, TN)

    def sum_of(ref, n):
        total = ref[0].astype(F32)
        for s in range(1, n):
            total = total + ref[s].astype(F32)
        return total

    fos[...] = dot(act[...], dn_all, NN).astype(BF16).reshape(4, 64, 1024)

    def up_back(ks):
        return wire.send_all([(gu.at[peer(k)], gua.at[i], (peer(k), j)) for k in ks], gua.at[0 : len(ks)])

    def down_back(ks):
        return wire.send_all(
            [(gd.at[:, at(peer(k) * 128, 128)], gda.at[i], (peer(k), j)) for k in ks],
            gda.at[0 : len(ks)],
        )

    gu_in.wait_recv()
    gu[...] = (guo[...] + gur[...].astype(F32)).astype(BF16)
    gua[i] = gu[i]
    gu_out = [up_back(near), up_back(crossing)]
    gd_in.wait_recv()
    gd[...] = (gdo[...] + gdr[...].astype(F32)).astype(BF16)
    gda[i] = gd[:, at(i * 128, 128)]
    gd_out = [down_back(near)]
    c3b = []
    for copy, y_ in zip(x3, (yy, 1 - yy)):
        copy.wait_recv()
        c3b.append(same(w3col(ox, y_, c), cpart))
    for copy in c3b:
        copy.wait_recv()
    attention(ox, False)

    hg_in.wait_recv()
    hgx[x] = sum_of(hgr, 8).astype(BF16)
    hgx_in = same(hgx.at[x], xpart)
    fx_in = wire.send(fos.at[:, at(ox * 32, 32), :], fxr, xpart)
    hgx_in.wait_recv()
    dy = hgx[...].reshape(64, 1024).astype(F32)
    middle = mid[...]
    fmean = jnp.mean(middle, axis=-1, keepdims=True)
    fcen = middle - fmean
    frs = lax.rsqrt(jnp.mean(fcen * fcen, axis=-1, keepdims=True) + EPS)
    dz, zhat = norm_back(middle, fmean, frs, vec[4:5, :], dy)

    def put_vec(k, v):
        for ii in range(8):
            vgs[ii, k : k + 1, :] = v[:, ii * 128 : (ii + 1) * 128]

    put_vec(4, jnp.sum(dy * zhat, axis=0, keepdims=True))
    put_vec(5, jnp.sum(dy, axis=0, keepdims=True))
    middle_grad = cota[r].astype(F32) + dz
    midg[...] = middle_grad
    low = middle_grad.astype(BF16)
    for g in (0, 1):
        mgr[g] = dot(low, weight(g, 3), NN).astype(BF16)
    lowb[...] = low

    def back_values(g):
        m4 = spread(mgr[g])

        vg[g] = dot(attl[g], m4, NN).astype(BF16)
        pa = att[g] * dot(vb[g], m4, NT)
        dxs[:, 0:256] = pa
        return jnp.sum(pa, axis=0, keepdims=True)

    def back_keys(g, delta):
        q4 = spread(qb[g])

        sg = (dxs[:, 0:256] - att[g] * delta).astype(BF16)
        attl[g] = sg
        kg[g] = (dot(sg, q4, NN) * 0.125).astype(BF16)
        total = dot(attl[g], kb[g], TN)
        qg[g] = (gather_heads(total) * 0.125).astype(BF16)

    def split(m, wide):
        wsc[...] = wide
        mine, other = wsc[at(c * 128, 128), :], wsc[at(oc * 128, 128), :]
        for ii in range(8):
            cols = slice(ii * 128, (ii + 1) * 128)
            gown[ii // 2, ii % 2, m] = mine[:, cols]
            cgs[ii // 2, ii % 2, m] = other[:, cols].astype(BF16)

    def one(ref, p):
        return ref.at[:, :, p]

    def chip_sum(p):
        one(g1, p)[...] = (one(gown, p)[...] + one(cgr, p)[...].astype(F32)).astype(BF16)
        return wire.send(g1.at[:, 1 - yy, p], yr.at[:, p], ypart)

    def to_core(p):
        return wire.send(one(cgs, p), one(cgr, p), cpart)

    delta = back_values(x)
    split(0, dot(vg[x], kin[...], TN))
    cg_in = [to_core(0)]
    split(1, dot(mix[x], lowb[...], TN))
    cg_in.append(to_core(1))
    back_keys(x, delta)
    y_in = []

    def to_y(p):
        cg_in[p].wait_recv()
        y_in.append(chip_sum(p))

    to_y(0)
    split(2, dot(kg[x], kin[...], TN))
    cg_in.append(to_core(2))
    to_y(1)
    split(3, dot(qg[x], kin[1280:1344, :], TN))
    cg_in.append(to_core(3))
    to_y(2)
    to_y(3)
    fx_in.wait_recv()
    fos2[...] = (fos[:, at(x * 32, 32), :].astype(F32) + fxr[...].astype(F32)).astype(BF16)
    fors[r] = fos2[r]
    fo_in = wire.send_all(
        [(fos2.at[peer(k) % 4], fors.at[r], (peer(k), j)) for k in (3, 2, 1)], fors.at[0:3]
    )
    gd_out.append(down_back(crossing))
    back_keys(ox, back_values(ox))

    def dx_tile(rows):
        return (
            dot(kg[0, rows, :], weight(0, 0), NT)
            + dot(kg[1, rows, :], weight(1, 0), NT)
            + dot(vg[0, rows, :], weight(0, 1), NT)
            + dot(vg[1, rows, :], weight(1, 1), NT)
        )

    accg[...] = jnp.zeros((8, 1024), F32)
    accb[...] = jnp.zeros((8, 1024), F32)
    out_base = wire.take(5)

    def out_copy(t, slot):
        rows = at(t * 256, 256)
        return wire.make(slot, media_out.at[c, rows, :], media_out.at[c, rows, :], cpart)

    def media_back(t, carry):
        dxs[0:256, :] = dx_tile(at(t * 256, 256))

        rows = at(t * 256, 256)
        v = xin[rows, :].astype(F32)
        dy = dxs[0:256, :]
        dz, zhat = norm_back(v, mu[rows, :], rs[rows, :], vec[0:1, :], dy)
        media_out[c, rows, :] = dz.astype(BF16)
        accg[...] += (dy * zhat).reshape(32, 8, 1024).sum(0)
        accb[...] += dy.reshape(32, 8, 1024).sum(0)
        out_copy(t, out_base + t).start()
        return carry

    zn, zf = peer(2) // 2, peer(4) // 2
    zd = peer(6) // 2

    def to_near(p):
        y_in[p].wait_recv()
        g2[:, p] = (g1[:, yy, p].astype(F32) + yr[:, p].astype(F32)).astype(BF16)
        parts = [(g2.at[zn, p], zr.at[0, p], (peer(2), j)), (g2.at[zd, p], zr.at[1, p], (peer(2), j))]
        return wire.send_all(parts, zr.at[0:2, 0])

    def to_far(p):
        n_in[p].wait_recv()
        zs[p] = (g2[zf, p].astype(F32) + zr[1, p].astype(F32)).astype(BF16)
        return wire.send(zs.at[p], zr.at[2, p], (peer(4), j))

    n_in, f_in = [], []
    lax.fori_loop(0, 2, media_back, 0)
    n_in.append(to_near(0))
    lax.fori_loop(2, 4, media_back, 0)
    n_in.append(to_near(1))
    lax.fori_loop(4, 5, media_back, 0)
    f_in.append(to_far(0))
    n_in.append(to_near(2))
    put_vec(0, jnp.sum(accg[...], axis=0, keepdims=True))
    put_vec(1, jnp.sum(accb[...], axis=0, keepdims=True))
    dxs[0:64, :] = dx_tile(pl.ds(1280, 64))
    lsum = dxs[0:64, :] + dot(qg[0], weight(0, 2), NT) + dot(qg[1], weight(1, 2), NT)
    lat32 = lat[...].astype(F32)
    dz, zhat = norm_back(lat32, mu[1280:1344, :], rs[1280:1344, :], vec[2:3, :], lsum)
    lgrad_out[c] = (midg[...] + dz).astype(BF16)
    lg_in = same(lgrad_out.at[c], cpart)
    put_vec(2, jnp.sum(lsum * zhat, axis=0, keepdims=True))
    put_vec(3, jnp.sum(lsum, axis=0, keepdims=True))
    for ii in range(8):
        vgs[ii, 6:8, :] = jnp.zeros((2, 128), F32)
    vg_in = wire.send(vgs, vgc, cpart)

    f_in.append(to_far(1))
    n_in.append(to_near(3))
    vg_in.wait_recv()
    vgt[...] = vgs[...] + vgc[...]
    vga[i] = vgt[i]
    v_in = wire.send_all([(vgt.at[peer(k)], vga.at[i], (peer(k), j)) for k in others], vga.at[0:7])
    f_in.append(to_far(2))
    fo_in.wait_recv()
    fox[x] = sum_of(fors, 4).astype(BF16)
    fox_in = same(fox.at[x], xpart)
    f_in.append(to_far(3))
    for copy in gu_out:
        copy.wait_recv()
    for q in range(4):
        gup[:, q * 256 : (q + 1) * 256] = gua[q].astype(F32) + gua[4 + q].astype(F32)
    for copy in gd_out:
        copy.wait_recv()
    for q in range(4):
        gdown[q * 256 : (q + 1) * 256, :] = gda[q].astype(F32) + gda[4 + q].astype(F32)

    fox_in.wait_recv()
    lat_out[c] = (mid[...] + fox[...].reshape(64, 1024).astype(F32)).astype(BF16)
    lo_in = same(lat_out.at[c], cpart)
    for copy in f_in:
        copy.wait_recv()
    last = g2[z].astype(F32) + zr[0].astype(F32) + zr[2].astype(F32)
    gmat[0] = last[3].T
    gmat[1] = last[2].T
    gmat[2] = last[0].T
    gmat[3] = last[1]
    v_in.wait_recv()
    vecs[...] = sum_of(vga, 8)

    for t in range(5):
        out = out_copy(t, out_base + t)
        out.wait_send()
        out.wait_recv()
    lg_in.wait_recv()
    lo_in.wait_recv()
    wire.drain()


SCRATCH = (
    ("prm_own", (8, 128), F32),
    ("prm", (8, 8, 128), F32),
    ("vec", (8, 1024), F32),
    ("xin", (1280, 1024), BF16),
    ("lat", (64, 1024), BF16),
    ("kin", (1344, 1024), BF16),
    ("mu", (1344, 1), F32),
    ("rs", (1344, 1), F32),
    ("w4", (2, 4, 2, 4, 128, 256), BF16),
    ("wo_own", (128, 128), BF16),
    ("upb", (8, 128, 512), BF16),
    ("dnb", (2, 256, 1024), BF16),
    ("kb", (2, 1344, 256), BF16),
    ("vb", (2, 1344, 256), BF16),
    ("qb", (2, 64, 256), BF16),
    ("att", (2, 1344, 256), F32),
    ("attl", (2, 1344, 256), BF16),
    ("mix", (2, 64, 256), BF16),
    ("mid", (64, 1024), F32),
    ("hid", (4, 64, 1024), BF16),
    ("cota", (4, 64, 1024), BF16),
    ("act", (256, 512), BF16),
    ("ig", (256, 512), BF16),
    ("hgs", (4, 64, 1024), BF16),
    ("hgr", (8, 32, 1024), BF16),
    ("hgx", (2, 32, 1024), BF16),
    ("fos", (4, 64, 1024), BF16),
    ("fxr", (4, 32, 1024), BF16),
    ("fos2", (4, 32, 1024), BF16),
    ("fors", (4, 32, 1024), BF16),
    ("fox", (2, 32, 1024), BF16),
    ("gus", (8, 128, 256), BF16),
    ("gur", (8, 128, 256), BF16),
    ("guo", (8, 128, 256), F32),
    ("gu", (8, 128, 256), BF16),
    ("gua", (8, 128, 256), BF16),
    ("gds", (256, 1024), BF16),
    ("gdr", (256, 1024), BF16),
    ("gdo", (256, 1024), F32),
    ("gd", (256, 1024), BF16),
    ("gda", (8, 256, 128), BF16),
    ("midg", (64, 1024), F32),
    ("lowb", (64, 1024), BF16),
    ("mgr", (2, 64, 256), BF16),
    ("kg", (2, 1344, 256), BF16),
    ("vg", (2, 1344, 256), BF16),
    ("qg", (2, 64, 256), BF16),
    ("cgs", (4, 2, 4, 128, 128), BF16),
    ("cgr", (4, 2, 4, 128, 128), BF16),
    ("gown", (4, 2, 4, 128, 128), F32),
    ("g1", (4, 2, 4, 128, 128), BF16),
    ("yr", (4, 4, 128, 128), BF16),
    ("g2", (4, 4, 128, 128), BF16),
    ("zr", (3, 4, 128, 128), BF16),
    ("zs", (4, 128, 128), BF16),
    ("dxs", (1344, 1024), F32),
    ("accg", (8, 1024), F32),
    ("accb", (8, 1024), F32),
    ("wsc", (256, 1024), F32),
    ("vgs", (8, 8, 128), F32),
    ("vgc", (8, 8, 128), F32),
    ("vgt", (8, 8, 128), F32),
    ("vga", (8, 8, 128), F32),
)


def hand_out(lat, med, lgr, gmat, gup, gdown, vecs, *rest):
    outs, sem = rest[:15], rest[15]
    moves = [(med, outs[1]), (gup, outs[7]), (gdown, outs[8]), (lat, outs[0]), (lgr, outs[2])]
    moves += [(gmat.at[k], outs[3 + k]) for k in range(4)]
    moves += [(vecs.at[k : k + 1], outs[9 + k]) for k in range(6)]
    copies = [pltpu.make_async_copy(a, b, sem.at[k]) for k, (a, b) in enumerate(moves)]
    for copy in copies:
        copy.start()
    for copy in copies:
        copy.wait()


def fused(media, latents, cotangent, image_counts, wq, wk, wv, wo, up, down, *gains):
    anyspace = pl.BlockSpec(memory_space=pl.ANY)
    vmem = pl.BlockSpec(memory_space=pltpu.VMEM)
    smem = pl.BlockSpec(memory_space=pltpu.SMEM)
    shape = jax.ShapeDtypeStruct
    outs = pl.pallas_call(
        layer_kernel,
        out_shape=[
            pltpu.VMEM(latents.shape, BF16),
            pltpu.VMEM(media.shape, BF16),
            pltpu.VMEM(latents.shape, BF16),
            pltpu.VMEM((4, 128, 128), F32),
            pltpu.VMEM(up.shape, F32),
            pltpu.VMEM(down.shape, F32),
            pltpu.VMEM((8, 128), F32),
        ],
        in_specs=[smem] + [anyspace] * 9 + [vmem] * 6,
        out_specs=[vmem] * 7,
        scratch_shapes=[
            pltpu.SemaphoreType.DMA((SEMS,)),
            pltpu.SemaphoreType.DMA((SEMS,)),
            pltpu.SemaphoreType.DMA((9,)),
        ]
        + [pltpu.VMEM(size, kind) for _, size, kind in SCRATCH],
        compiler_params=pltpu.CompilerParams(
            collective_id=0, has_side_effects=True, vmem_limit_bytes=LIMIT * 2**20
        ),
        cost_estimate=pl.CostEstimate(
            flops=14 * 10**9, bytes_accessed=20 * 10**6, transcendentals=10**6
        ),
    )(
        image_counts,
        media,
        latents,
        cotangent,
        wq,
        wk,
        wv,
        wo,
        up,
        down,
        *[v.reshape(1, 128) for v in gains],
    )
    outs = pl.pallas_call(
        hand_out,
        out_shape=[shape(v.shape, BF16) for v in (latents, media, latents)]
        + [shape(v.shape, F32) for v in (wq, wk, wv, wo, up, down)]
        + [shape((1, 128), F32)] * 6,
        in_specs=[vmem] * 7,
        out_specs=[anyspace] * 15,
        scratch_shapes=[pltpu.SemaphoreType.DMA((15,))],
        compiler_params=pltpu.CompilerParams(vmem_limit_bytes=4 * 2**20),
    )(*[pltpu.with_memory_space_constraint(v, pltpu.VMEM) for v in outs])
    return tuple(outs[:9]) + tuple(v.reshape(128) for v in outs[9:])


def fits(mesh):
    return mesh.shape["dp"] == 8 and mesh.shape["mp"] == 4


MB = 2
SB = 1


def layer_norm(inputs, gain, bias):
    center = inputs - jnp.mean(inputs, axis=-1, keepdims=True)
    spread = jnp.mean(center * center, axis=-1, keepdims=True)
    return center * lax.rsqrt(spread + 1e-05) * gain + bias


def gelu_exact(inputs):
    return jax.nn.gelu(inputs, approximate=False)


def add_tuples(left, right):
    return tuple((first + second for first, second in zip(left, right)))


def micro_step(gathered, media, latents, cotangent, counts):
    (
        query_matrix,
        k_weight,
        v_weight,
        output_projection_weight,
        up_projection_weight,
        down_projection_weight,
        media_gain,
        media_bias,
        latent_gain,
        latent_bias,
        ff_gain,
        ff_bias,
    ) = gathered
    samples = media.shape[0]
    media_len = media.shape[1]
    latent_len = latents.shape[1]
    keys_len = media_len + latent_len
    span = query_matrix.shape[1]
    local_heads = span // HEAD
    wide_rows = jnp.float32
    key_matrix = jnp.concatenate([k_weight, v_weight], axis=1)
    latent_full = latents.astype(wide_rows)
    latent_norm32, latent_pull = jax.vjp(
        layer_norm, latent_full, latent_gain.astype(wide_rows), latent_bias.astype(wide_rows)
    )
    latent_normed_rows = latent_norm32.astype(jnp.bfloat16)
    media_norm32, media_pull = jax.vjp(
        layer_norm,
        media.astype(wide_rows),
        media_gain.astype(wide_rows),
        media_bias.astype(wide_rows),
    )
    media_norm = media_norm32.astype(jnp.bfloat16)
    media_kv = jnp.einsum(
        "snd,dh->snh", media_norm, key_matrix, preferred_element_type=wide_rows
    ).astype(jnp.bfloat16)
    query_rows = jnp.einsum(
        "gjm,mu->gju", latent_normed_rows, query_matrix, preferred_element_type=wide_rows
    ).astype(jnp.bfloat16)
    latent_kv = jnp.einsum(
        "gjm,mu->gju", latent_normed_rows, key_matrix, preferred_element_type=wide_rows
    ).astype(jnp.bfloat16)
    both_kv = jnp.concatenate([media_kv, latent_kv], axis=1)
    head_queries = query_rows.reshape(samples, latent_len, local_heads, HEAD)
    head_keys = both_kv[:, :, :span].reshape(samples, keys_len, local_heads, HEAD)
    head_values = both_kv[:, :, span:].reshape(samples, keys_len, local_heads, HEAD)
    places = jnp.arange(keys_len)
    valid = jnp.logical_or(places[None, :] // PATCH < counts[:, None], places[None, :] >= media_len)

    def scores_of():
        raw = (
            jnp.einsum("slhe,snhe->shln", head_queries, head_keys, preferred_element_type=wide_rows)
            * 0.125
        )
        return jnp.where(valid[:, None, None, :], raw, -1e30)

    scores = scores_of()
    row_max = jnp.max(scores, axis=-1, keepdims=True)
    logsum = row_max + jnp.log(jnp.sum(jnp.exp(scores - row_max), axis=-1, keepdims=True))
    attend_low = jnp.exp(scores - logsum).astype(jnp.bfloat16)
    mixed_rows = jnp.einsum(
        "shln,snhe->slhe", attend_low, head_values, preferred_element_type=wide_rows
    )
    mixed_rows = mixed_rows.reshape(samples, latent_len, span).astype(jnp.bfloat16)
    attn_out = lax.psum(
        jnp.einsum(
            "rwa,ax->rwx", mixed_rows, output_projection_weight, preferred_element_type=wide_rows
        ),
        "mp",
    )
    middle = latent_full + attn_out
    hidden32, ff_pull = jax.vjp(
        layer_norm, middle, ff_gain.astype(wide_rows), ff_bias.astype(wide_rows)
    )
    hidden_rows = hidden32.astype(jnp.bfloat16)
    inner_rows = jnp.einsum(
        "qab,bo->qao", hidden_rows, up_projection_weight, preferred_element_type=wide_rows
    )
    active32, gelu_pull = jax.vjp(gelu_exact, inner_rows)
    active_units = active32.astype(jnp.bfloat16)
    ff_out = lax.psum(
        jnp.einsum(
            "pye,ej->pyj", active_units, down_projection_weight, preferred_element_type=wide_rows
        ).astype(jnp.bfloat16),
        "mp",
    ).astype(jnp.float32)
    result = (middle + ff_out).astype(jnp.bfloat16)
    down_projection_grad = jnp.einsum(
        "kje,kju->eu", active_units, cotangent, preferred_element_type=wide_rows
    )
    active_units_grad = jnp.einsum(
        "jvw,ow->jvo", cotangent, down_projection_weight, preferred_element_type=wide_rows
    )
    (inner_grad,) = gelu_pull(active_units_grad)
    inner_rows_reduced = inner_grad.astype(jnp.bfloat16)
    up_projection_grad = jnp.einsum(
        "imw,imk->wk", hidden_rows, inner_rows_reduced, preferred_element_type=wide_rows
    )
    hidden_grad = lax.psum(
        jnp.einsum(
            "xvm,nm->xvn",
            inner_rows_reduced,
            up_projection_weight,
            preferred_element_type=wide_rows,
        ).astype(jnp.bfloat16),
        "mp",
    ).astype(jnp.float32)
    middle_part, ff_gain_grad, ff_bias_grad = ff_pull(hidden_grad)
    middle_grad = cotangent.astype(wide_rows) + middle_part
    middle_rows_reduced = middle_grad.astype(jnp.bfloat16)
    output_projection_grad = jnp.einsum(
        "gfb,gfw->bw", mixed_rows, middle_rows_reduced, preferred_element_type=wide_rows
    )
    mixed_grad = jnp.einsum(
        "kzw,nw->kzn",
        middle_rows_reduced,
        output_projection_weight,
        preferred_element_type=wide_rows,
    ).astype(jnp.bfloat16)
    mixed_grad = mixed_grad.reshape(samples, latent_len, local_heads, HEAD)
    attend = jnp.exp(scores_of() - logsum)
    attend_grad = jnp.einsum(
        "slhe,snhe->shln", mixed_grad, head_values, preferred_element_type=wide_rows
    )
    score_grad = attend * (attend_grad - jnp.sum(attend * attend_grad, axis=-1, keepdims=True))
    score_grad = score_grad.astype(jnp.bfloat16)
    query_rows_grad = (
        jnp.einsum("shln,snhe->slhe", score_grad, head_keys, preferred_element_type=wide_rows)
        * 0.125
    )
    query_rows_grad = query_rows_grad.astype(jnp.bfloat16).reshape(samples, latent_len, span)
    key_grad = (
        jnp.einsum("shln,slhe->snhe", score_grad, head_queries, preferred_element_type=wide_rows)
        * 0.125
    )
    key_grad = key_grad.astype(jnp.bfloat16).reshape(samples, keys_len, span)
    value_grad = jnp.einsum(
        "shln,slhe->snhe", attend_low, mixed_grad, preferred_element_type=wide_rows
    )
    value_grad = value_grad.astype(jnp.bfloat16).reshape(samples, keys_len, span)
    kv_grad = jnp.concatenate([key_grad, value_grad], axis=2)
    media_kv_grad = kv_grad[:, :media_len]
    latent_key_value_grad = kv_grad[:, media_len:]
    query_weight_grad = jnp.einsum(
        "cbi,cbu->iu", latent_normed_rows, query_rows_grad, preferred_element_type=wide_rows
    )
    latent_wgrad = jnp.einsum(
        "cbi,cbu->iu", latent_normed_rows, latent_key_value_grad, preferred_element_type=wide_rows
    )
    latent_portion = jnp.einsum(
        "kwt,gt->kwg", query_rows_grad, query_matrix, preferred_element_type=wide_rows
    )
    latent_portion = latent_portion + jnp.einsum(
        "kwt,gt->kwg", latent_key_value_grad, key_matrix, preferred_element_type=wide_rows
    )
    media_part = jnp.einsum(
        "snh,dh->snd", media_kv_grad, key_matrix, preferred_element_type=wide_rows
    )
    media_wgrad = jnp.einsum(
        "snd,snh->dh", media_norm, media_kv_grad, preferred_element_type=wide_rows
    )
    kv_weight_grad = media_wgrad + latent_wgrad
    media_sum, latent_sum = (
        lax.psum(media_part.astype(jnp.bfloat16), "mp").astype(jnp.float32),
        lax.psum(latent_portion.astype(jnp.bfloat16), "mp").astype(jnp.float32),
    )
    media_back, media_gain_grad, media_bias_grad = media_pull(media_sum)
    media_out = media_back.astype(jnp.bfloat16)
    latent_back, latent_gain_grad, latent_bias_grad = latent_pull(latent_sum)
    latent_grad = middle_grad + latent_back
    grads = (
        query_weight_grad,
        kv_weight_grad[:, :span],
        kv_weight_grad[:, span:],
        output_projection_grad,
        up_projection_grad,
        down_projection_grad,
        media_gain_grad,
        media_bias_grad,
        latent_gain_grad,
        latent_bias_grad,
        ff_gain_grad,
        ff_bias_grad,
    )
    return (result, media_out, latent_grad.astype(jnp.bfloat16), grads)


def local(
    media,
    latents,
    cotangent,
    image_counts,
    query_matrix,
    k_weight,
    v_weight,
    output_projection_weight,
    up_projection_weight,
    down_projection_weight,
    media_gain,
    media_bias,
    latent_gain,
    latent_bias,
    ff_gain,
    ff_bias,
):
    results = []
    media_grads = []
    latent_grads = []
    totals = ()
    for micro_index in range(MB):
        gathered = (
            lax.all_gather(query_matrix, "dp", axis=0, tiled=True),
            lax.all_gather(k_weight, "dp", axis=0, tiled=True),
            lax.all_gather(v_weight, "dp", axis=0, tiled=True),
            lax.all_gather(output_projection_weight, "dp", axis=1, tiled=True),
            lax.all_gather(up_projection_weight, "dp", axis=0, tiled=True),
            lax.all_gather(down_projection_weight, "dp", axis=1, tiled=True),
            lax.all_gather(media_gain, "dp", axis=0, tiled=True),
            lax.all_gather(media_bias, "dp", axis=0, tiled=True),
            lax.all_gather(latent_gain, "dp", axis=0, tiled=True),
            lax.all_gather(latent_bias, "dp", axis=0, tiled=True),
            lax.all_gather(ff_gain, "dp", axis=0, tiled=True),
            lax.all_gather(ff_bias, "dp", axis=0, tiled=True),
        )
        lower = micro_index * SB
        upper = lower + SB
        result, media_back, latent_back, grads = micro_step(
            gathered,
            media[lower:upper],
            latents[lower:upper],
            cotangent[lower:upper],
            image_counts[lower:upper],
        )
        grads = (
            lax.psum_scatter(grads[0], "dp", scatter_dimension=0, tiled=True),
            lax.psum_scatter(grads[1], "dp", scatter_dimension=0, tiled=True),
            lax.psum_scatter(grads[2], "dp", scatter_dimension=0, tiled=True),
            lax.psum_scatter(grads[3], "dp", scatter_dimension=1, tiled=True),
            lax.psum_scatter(grads[4], "dp", scatter_dimension=0, tiled=True),
            lax.psum_scatter(grads[5], "dp", scatter_dimension=1, tiled=True),
            lax.psum_scatter(grads[6], "dp", scatter_dimension=0, tiled=True),
            lax.psum_scatter(grads[7], "dp", scatter_dimension=0, tiled=True),
            lax.psum_scatter(grads[8], "dp", scatter_dimension=0, tiled=True),
            lax.psum_scatter(grads[9], "dp", scatter_dimension=0, tiled=True),
            lax.psum_scatter(grads[10], "dp", scatter_dimension=0, tiled=True),
            lax.psum_scatter(grads[11], "dp", scatter_dimension=0, tiled=True),
        )
        totals = grads if micro_index == 0 else add_tuples(totals, grads)
        results.append(result)
        media_grads.append(media_back)
        latent_grads.append(latent_back)
    return (
        jnp.concatenate(results, axis=0),
        jnp.concatenate(media_grads, axis=0),
        jnp.concatenate(latent_grads, axis=0),
        totals[0],
        totals[1],
        totals[2],
        totals[3],
        totals[4],
        totals[5],
        totals[6],
        totals[7],
        totals[8],
        totals[9],
        totals[10],
        totals[11],
    )


def solution(mesh):
    placed = (
        P("dp", None, None),
        P("dp", None, None),
        P("dp", None, None),
        P("dp"),
        P("dp", "mp"),
        P("dp", "mp"),
        P("dp", "mp"),
        P("mp", "dp"),
        P("dp", "mp"),
        P("mp", "dp"),
        P("dp"),
        P("dp"),
        P("dp"),
        P("dp"),
        P("dp"),
        P("dp"),
    )
    return jax.shard_map(
        fused if fits(mesh) else local,
        mesh=mesh,
        in_specs=placed,
        out_specs=(
            P("dp", None, None),
            P("dp", None, None),
            P("dp", None, None),
            P("dp", "mp"),
            P("dp", "mp"),
            P("dp", "mp"),
            P("mp", "dp"),
            P("dp", "mp"),
            P("mp", "dp"),
            P("dp"),
            P("dp"),
            P("dp"),
            P("dp"),
            P("dp"),
            P("dp"),
        ),
        check_vma=False,
    )
```
